32 devices in a mesh: groups: 2 (over x), wide: 16 (over z, y, core).
Axes of the slice: x: 2, y: 2, z: 4, core: 2. Of those that a mesh axis runs over, the one named last changes fastest.
Arguments:
- token_adapter_index: int32 [4096, 1], P(('groups', 'wide')), parts along dimension 0, may hold values from 0 to 15; in each aligned block of 128 rows (0 to 127, 128 to 255, ...) at most 16 rows name the same one
- hidden: bfloat16 [4096, 8192], P(('groups', 'wide')), parts along dimension 0, may hold values from -6 to 6
- adapter_down_maps: bfloat16 [16, 8192, 64], P('wide'), may hold values from -0.0625 to 0.0625
- adapter_up_maps: bfloat16 [16, 64, 8192], P('wide'), may hold values from -0.75 to 0.75
Outputs:
- lora_delta: bfloat16 [4096, 8192], P(('groups', 'wide')), parts along dimension 0
The draws below stay inside these ranges and needn't reach their ends.
There are 2 independent parts, one for each index of `groups`. The reference program is written for one: setup_inputs(seed, part) draws one part's arguments, and reference() takes and returns one part's arrays. A program takes and returns all parts, laid end to end along the dimension named above; an argument that names none is the same for every part. Nothing has to cross between parts.
Inputs may be any that keep to these rules, and one draw needn't show every extreme that they name: `token_adapter_index`: within the rows of one device at most 16 tokens name the same adapter, and 16 is reached in some device's rows; every adapter is named by some token.
All inputs are finite; a program needn't handle non-finite values.
Results may differ from the reference program's by a relative error of at most 0.0049.
Values may be sent and summed in bfloat16 or wider, within the bound.
No kernel may reach another device: no remote copies, remote signals or barrier semaphores. Data moves between devices by JAX's collectives and lax.ppermute only.
A program may use at most 64 MiB of HBM per device.

```python
import math
import jax
import jax.numpy as jnp
import numpy as np
from jax import lax

MODEL_WIDTH = 8192
QUERY_OUT_WIDTH = 8192
ADAPTER_RANK = 64
TOK_DEV = 128
ADAPTER_COUNT = 16
CAP = 16
TOKENS = 2048
N_WIDE = 16


def level_of(rng, extent, cuts, smallest, top_value):
    def one(position, parts):
        draws = jax.random.uniform(jax.random.fold_in(jax.random.fold_in(rng, 6), position), (parts,), jnp.float32, smallest / len(cuts), top_value / len(cuts))
        return jnp.repeat(jnp.exp(draws), extent[position] // parts).reshape((-1,) + (1,) * (len(extent) - position - 1))

    level = one(*cuts[0])
    for cut in cuts[1:]:
        level = level * one(*cut)
    return level


def routed_block(stream_key, own, number, rows, count, top, limit, skew):
    sequence = jax.random.permutation(stream_key, count)
    crowded, common = shares(count, rows * top, limit, skew, True), shares(count, rows * top, limit, skew, False)
    places = jnp.arange(count)

    def named(sizes, turn):
        used = int((sizes > 0).sum())
        fixed = max(1, used // 4)
        passed = fixed + (places - fixed + turn * (used - fixed)) % max(1, count - fixed)
        return jnp.zeros((count,), jnp.int32).at[sequence[jnp.where(places < fixed, places, passed)]].set(jnp.asarray(sizes, jnp.int32))

    sizes = jnp.where(number % 4 == 0, named(crowded, number // 4), named(common, number - number // 4 - 1))
    mixed = jax.random.permutation(jax.random.fold_in(own, 3), count)
    source_of, taker = mixed[0:count // 2 * 2:2], mixed[1:count // 2 * 2:2]
    slack = jnp.minimum(sizes[source_of] - 1, limit - sizes[taker]) // 2
    slack = jnp.where((source_of == sequence[0]) | (taker == sequence[0]) | (sizes[taker] == 0), 0, jnp.maximum(slack, 0))
    passed = jax.random.randint(jax.random.fold_in(own, 4), (count // 2,), 0, 1 << 20) % (slack + 1)
    sizes = sizes.at[source_of].add(-passed).at[taker].add(passed)
    items = jnp.searchsorted(jnp.cumsum(sizes), jnp.arange(rows * top), side="right").astype(jnp.int32)
    table = items.reshape(top, rows).T
    table = table[jax.random.permutation(jax.random.fold_in(own, 1), rows)]
    turn = jax.random.randint(jax.random.fold_in(own, 2), (rows, 1), 0, top)
    return jnp.take_along_axis(table, (jnp.arange(top)[None, :] + turn) % top, axis=1)


def shares(amount, total, bound, slope, full):
    portions = [(1 << 20) // math.isqrt(standing ** slope) + 1 for standing in range(1, amount + 1)]
    largest = bound if full else min(bound, max(-(-total // amount), total * portions[0] // sum(portions)))
    least = 1 if total - largest >= amount - 1 else 0
    holding, rest = [largest] + [least] * (amount - 1), total - largest - least * (amount - 1)
    while rest > 0:
        candidates = [i for i in range(1, amount) if holding[i] < largest] or [i for i in range(1, amount) if holding[i] < bound]
        pool, left = sum([portions[i] for i in candidates]), rest
        for i in candidates:
            extra = min(bound - holding[i], max(1, left * portions[i] // pool), rest)
            holding[i] = holding[i] + extra
            rest = rest - extra
    return np.array(holding)


def centred(stream_key, extent, spread, most, pieces=(), held_as=jnp.bfloat16):
    values = jax.random.normal(stream_key, extent, jnp.float32) * spread
    if len(pieces) > 0:
        values = level_of(stream_key, extent, pieces, -0.22, 0.18) * values
    return jnp.clip(values, min=-most, max=most).astype(held_as)


def setup_inputs(seed: int = 0, part: int = 0) -> dict:
    key_list = jax.random.split(jax.random.key(seed), 5)
    part_keys = jax.random.split(jax.random.fold_in(key_list[4], part), 5)
    token_adapter_index_keys = jax.random.split(jax.random.fold_in(part_keys[0], 1), TOKENS // TOK_DEV)
    token_adapter_index_turns = jax.random.permutation(jax.random.fold_in(part_keys[0], 3), TOKENS // TOK_DEV)
    token_adapter_index = jax.vmap(lambda own, number: routed_block(jax.random.fold_in(part_keys[0], 2), own, number, TOK_DEV, ADAPTER_COUNT, 1, CAP, 2))(token_adapter_index_keys, token_adapter_index_turns).reshape((TOKENS, 1))
    hidden = centred(part_keys[1], (TOKENS, MODEL_WIDTH), 1.0, 6.0, ((0, 16),))
    adapter_down_maps = centred(key_list[2], (ADAPTER_COUNT, MODEL_WIDTH, ADAPTER_RANK), MODEL_WIDTH ** -0.5, 0.0625, ((0, 16),))
    adapter_up_maps = centred(key_list[3], (ADAPTER_COUNT, ADAPTER_RANK, QUERY_OUT_WIDTH), ADAPTER_RANK ** -0.5, 0.75, ((0, 16),))
    return {"token_adapter_index": token_adapter_index, "hidden": hidden, "adapter_down_maps": adapter_down_maps, "adapter_up_maps": adapter_up_maps}


adapter_scale = 2.0


def reference(token_adapter_index, hidden, adapter_down_maps, adapter_up_maps):
    ids = token_adapter_index[:, 0].reshape(N_WIDE, TOK_DEV)
    order = jnp.arange(TOK_DEV, dtype=jnp.int32)

    def block_rank(row):
        same = (row[None, :] == row[:, None]) & (order[None, :] < order[:, None])
        return jnp.sum(same.astype(jnp.int32), axis=1).astype(jnp.int32)

    ranks = lax.map(block_rank, ids)
    blocks = jnp.arange(N_WIDE, dtype=jnp.int32)[:, None]
    flat = ((ids * N_WIDE + blocks) * CAP + ranks).reshape(-1).astype(jnp.int32)
    slots = ADAPTER_COUNT * N_WIDE * CAP
    adapter_table = jnp.full((slots,), TOKENS, jnp.int32).at[flat].set(jnp.arange(TOKENS, dtype=jnp.int32))
    adapter_table = adapter_table.reshape(ADAPTER_COUNT, N_WIDE * CAP)
    padded = jnp.concatenate([hidden, jnp.zeros((1, MODEL_WIDTH), hidden.dtype)], axis=0)

    def single_adapter(packed):
        picks, down_map, up_weight = packed
        token_rows = padded[picks]
        reduced_rows = jnp.dot(token_rows, down_map, preferred_element_type=jnp.float32).astype(jnp.bfloat16)
        return (adapter_scale * jnp.dot(reduced_rows, up_weight, preferred_element_type=jnp.float32)).astype(jnp.bfloat16)

    delta_outputs = lax.map(single_adapter, (adapter_table, adapter_down_maps, adapter_up_maps))
    return delta_outputs.reshape(slots, QUERY_OUT_WIDTH)[flat]
```

```python
import jax
import jax.numpy as jnp
from jax import lax
from jax.sharding import Mesh
from jax.sharding import PartitionSpec as P

adapter_scale = 2.0
PLANE = ("groups", "inner")


def own_width_slices(adapter, parts):
    rank, width = adapter.shape
    share = width // lax.axis_size("groups")
    half = lax.dynamic_slice_in_dim(adapter, lax.axis_index("groups") * share, share, axis=1)
    return half.reshape(rank, parts, share // parts).transpose(1, 0, 2)


def gathered(adapter):
    inner = lax.axis_size("inner")
    in_plane = lax.all_to_all(
        own_width_slices(adapter, inner), "inner", split_axis=0, concat_axis=0, tiled=True
    )
    return lax.all_gather(in_plane, "outer", axis=0, tiled=True)


def per_device(token_adapter_index, hidden, adapter_down_maps, adapter_up_maps):
    tok_count = hidden.shape[0]
    adapters = lax.axis_size("outer") * lax.axis_size("inner")
    down = gathered(adapter_down_maps[0].T)
    up = gathered(adapter_up_maps[0])
    rank, share = down.shape[1], down.shape[2]
    ids = lax.all_gather(token_adapter_index[:, 0], PLANE, axis=0, tiled=True)
    rows = lax.all_to_all(hidden, PLANE, split_axis=1, concat_axis=0, tiled=True)
    named = ids[None, None, :] == jnp.arange(adapters, dtype=jnp.int32)[:, None, None]

    partial = lax.dot_general(
        down.reshape(adapters * rank, share), rows, (((1,), (1,)), ((), ())), preferred_element_type=jnp.float32
    ).reshape(adapters, rank, rows.shape[0])
    partial = jnp.sum(jnp.where(named, partial, 0.0), axis=0)
    shrunk = lax.psum(partial, PLANE).astype(jnp.bfloat16)

    spread = jnp.where(named, shrunk[None], jnp.zeros((), jnp.bfloat16)).reshape(adapters * rank, rows.shape[0])
    delta = adapter_scale * lax.dot_general(
        spread, up.reshape(adapters * rank, share), (((0,), (0,)), ((), ())), preferred_element_type=jnp.float32
    )
    return lax.all_to_all(delta.astype(jnp.bfloat16), PLANE, split_axis=0, concat_axis=1, tiled=True)


def solution(mesh):
    groups, wide = mesh.shape["groups"], mesh.shape["wide"]
    outer = 1 << ((wide.bit_length() - 1) // 2)
    fine = Mesh(mesh.devices.reshape(groups, outer, wide // outer), ("groups", "outer", "inner"))
    owner = ("outer", "inner")
    rows = P(("groups",) + owner, None)
    return jax.shard_map(
        per_device,
        mesh=fine,
        in_specs=(rows, rows, P(owner, None, None), P(owner, None, None)),
        out_specs=rows,
        check_vma=False,
    )
```

```python
import jax
import jax.numpy as jnp
from jax import lax
from jax.sharding import Mesh
from jax.sharding import PartitionSpec as P

adapter_scale = 2.0
PLANE = ("groups", "inner")


def own_width_slices(adapter, parts):
    rank, width = adapter.shape
    share = width // lax.axis_size("groups")
    half = lax.dynamic_slice_in_dim(adapter, lax.axis_index("groups") * share, share, axis=1)
    return half.reshape(rank, parts, share // parts).transpose(1, 0, 2)


def gathered(adapter):
    inner, outer = lax.axis_size("inner"), lax.axis_size("outer")
    block = lax.all_to_all(
        own_width_slices(adapter, inner), "inner", split_axis=0, concat_axis=0, tiled=True
    )
    blocks = [block]
    for _ in range(outer - 1):
        block = lax.ppermute(block, "outer", [(i, (i + 1) % outer) for i in range(outer)])
        blocks.append(block)
    return jnp.concatenate(blocks, axis=0)


def per_device(token_adapter_index, hidden, adapter_down_maps, adapter_up_maps):
    tok_count, width = hidden.shape
    inner, outer = lax.axis_size("inner"), lax.axis_size("outer")
    members = lax.axis_size("groups") * inner
    share = width // members
    adapters = outer * inner
    down = gathered(adapter_down_maps[0].T)
    up = gathered(adapter_up_maps[0])
    rank = down.shape[1]

    ids = token_adapter_index[:, 0].astype(jnp.bfloat16)
    ids = jnp.pad(ids, (0, 8 * share - tok_count)).reshape(1, 8, share)
    outgoing = hidden.reshape(tok_count, members, share).transpose(1, 0, 2)
    outgoing = jnp.concatenate([outgoing, jnp.broadcast_to(ids, (members, 8, share))], axis=1)
    arrived = lax.all_to_all(outgoing, PLANE, split_axis=0, concat_axis=0, tiled=True)
    rows = arrived[:, :tok_count].reshape(members * tok_count, share)
    ids = arrived[:, tok_count:].reshape(members, 8 * share)[:, :tok_count].reshape(-1).astype(jnp.int32)

    steps_back = jnp.arange(outer, dtype=jnp.int32)
    owners = (lax.axis_index("outer") - steps_back + outer) % outer
    labels = (owners[:, None] * inner + jnp.arange(inner, dtype=jnp.int32)[None, :]).reshape(-1)
    named = ids[None, None, :] == labels[:, None, None]

    partial = lax.dot_general(
        down.reshape(adapters * rank, share), rows, (((1,), (1,)), ((), ())), preferred_element_type=jnp.float32
    ).reshape(adapters, rank, rows.shape[0])
    partial = jnp.sum(jnp.where(named, partial, 0.0), axis=0)
    partial = partial.reshape(rank, members, tok_count).transpose(1, 0, 2)
    terms = lax.all_to_all(partial, PLANE, split_axis=0, concat_axis=0, tiled=True)
    own = jnp.sum(terms, axis=0).astype(jnp.bfloat16)
    shrunk = lax.all_gather(own, PLANE, axis=0)
    shrunk = shrunk.transpose(1, 0, 2).reshape(rank, members * tok_count)

    spread = jnp.where(named, shrunk[None], jnp.zeros((), jnp.bfloat16)).reshape(adapters * rank, rows.shape[0])
    delta = adapter_scale * lax.dot_general(
        spread, up.reshape(adapters * rank, share), (((0,), (0,)), ((), ())), preferred_element_type=jnp.float32
    )
    delta = delta.astype(jnp.bfloat16).reshape(members, tok_count, share)
    returned = lax.all_to_all(delta, PLANE, split_axis=0, concat_axis=0, tiled=True)
    return returned.transpose(1, 0, 2).reshape(tok_count, width)


def solution(mesh):
    groups, wide = mesh.shape["groups"], mesh.shape["wide"]
    outer = 1 << ((wide.bit_length() - 1) // 2)
    fine = Mesh(mesh.devices.reshape(groups, outer, wide // outer), ("groups", "outer", "inner"))
    owner = ("outer", "inner")
    rows = P(("groups",) + owner, None)
    return jax.shard_map(
        per_device,
        mesh=fine,
        in_specs=(rows, rows, P(owner, None, None), P(owner, None, None)),
        out_specs=rows,
        check_vma=False,
    )
```

```python
import functools

import jax
import jax.numpy as jnp
from jax import lax
from jax.experimental import pallas as pl
from jax.experimental.pallas import tpu as pltpu
from jax.sharding import Mesh
from jax.sharding import PartitionSpec as P

adapter_scale = 2.0
PLANE = ("groups", "inner")
VMEM_BYTES = 32 << 20


def to_partner(value, axes, size, offset):
    return lax.ppermute(value, axes, [(i, i ^ offset) for i in range(size)])


def ring(block, outer):
    blocks = [block]
    for _ in range(outer - 1):
        block = lax.ppermute(block, "outer", [(i, (i + 1) % outer) for i in range(outer)])
        blocks.append(block)
    return blocks


def load_all(sources, target, sems):
    copies, at = [], 0
    for n, source in enumerate(sources):
        rows = source.shape[0]
        copies.append(pltpu.make_async_copy(source, target.at[pl.ds(at, rows)], sems.at[n]))
        at += rows
    for copy in copies:
        copy.start()
    return copies


def down_kernel(counts, tok, rank, labels_ref, ids_ref, *refs):
    map_count, members = counts
    maps, rows = refs[:map_count], refs[map_count : map_count + members]
    outs = refs[map_count + members : map_count + 2 * members]
    map_buf, row_buf, sums, sems = refs[map_count + 2 * members :]
    copies = load_all(list(maps), map_buf, sems)
    copies += load_all(list(rows), row_buf, sems.at[pl.ds(map_count, members)])
    for copy in copies:
        copy.wait()
    adapters = map_buf.shape[0] // rank
    batch = min(4, adapters)

    def one(member, _):
        tokens = row_buf[pl.ds(pl.multiple_of(member * tok, tok), tok), :]
        ids = ids_ref[pl.ds(member, 1), :]
        total = jnp.zeros((rank, tok), jnp.float32)
        for first in range(0, adapters, batch):
            product = lax.dot_general(
                map_buf[first * rank : (first + batch) * rank, :],
                tokens,
                (((1,), (1,)), ((), ())),
                preferred_element_type=jnp.float32,
            )
            for n in range(batch):
                named = ids == labels_ref[first + n]
                total += jnp.where(named, product[n * rank : (n + 1) * rank, :], 0.0)
        sums[member] = total
        return 0

    lax.fori_loop(0, members, one, 0)
    for member in range(members):
        outs[member][...] = sums[member]


def down_product(labels, ids, maps, rows, rank):
    tok, share = rows[0].shape
    map_rows = sum(m.shape[0] for m in maps)
    anywhere = pl.BlockSpec(memory_space=pl.ANY)
    in_vmem = pl.BlockSpec(memory_space=pltpu.VMEM)
    return pl.pallas_call(
        functools.partial(down_kernel, (len(maps), len(rows)), tok, rank),
        out_shape=[jax.ShapeDtypeStruct((rank, tok), jnp.float32)] * len(rows),
        in_specs=[pl.BlockSpec(memory_space=pltpu.SMEM), in_vmem] + [anywhere] * (len(maps) + len(rows)),
        out_specs=[in_vmem] * len(rows),
        scratch_shapes=[
            pltpu.VMEM((map_rows, share), jnp.bfloat16),
            pltpu.VMEM((len(rows) * tok, share), jnp.bfloat16),
            pltpu.VMEM((len(rows), rank, tok), jnp.float32),
            pltpu.SemaphoreType.DMA((len(maps) + len(rows),)),
        ],
        compiler_params=pltpu.CompilerParams(vmem_limit_bytes=VMEM_BYTES),
        cost_estimate=pl.CostEstimate(
            flops=2 * map_rows * len(rows) * tok * share,
            bytes_accessed=2 * share * (map_rows + len(rows) * tok),
            transcendentals=0,
        ),
        name="down_product",
    )(labels, ids, *maps, *rows)


def up_kernel(counts, tok, rank, labels_ref, ids_ref, *refs):
    map_count, members = counts
    maps, rows = refs[:map_count], refs[map_count : map_count + members]
    outs = refs[map_count + members : map_count + 2 * members]
    map_buf, row_buf, results, sems = refs[map_count + 2 * members :]
    copies = load_all(list(maps), map_buf, sems)
    for member in range(members):
        row_buf[member] = rows[member][...]
    for copy in copies:
        copy.wait()
    adapters = map_buf.shape[0] // rank
    per_tile = max(1, 128 // rank)
    lane = lax.broadcasted_iota(jnp.int32, (tok, per_tile * rank), 1)

    def one(member, _):
        shrunk = row_buf[member].astype(jnp.float32).T
        shrunk = jnp.concatenate([shrunk] * per_tile, axis=1)
        ids = jnp.broadcast_to(ids_ref[pl.ds(member, 1), :], (per_tile * rank, tok)).T
        pieces = []
        for first in range(0, adapters, per_tile):
            label = jnp.full(lane.shape, labels_ref[first], jnp.int32)
            for n in range(1, per_tile):
                label = jnp.where(lane >= n * rank, labels_ref[first + n], label)
            pieces.append(jnp.where(ids == label, shrunk, 0.0).astype(jnp.bfloat16))
        spread = jnp.concatenate(pieces, axis=1)
        product = jnp.dot(spread, map_buf[...], preferred_element_type=jnp.float32)
        results[member] = (adapter_scale * product).astype(jnp.bfloat16)
        return 0

    lax.fori_loop(0, members, one, 0)
    for member in range(members):
        outs[member][...] = results[member]


def up_product(labels, ids, maps, rows):
    rank, tok = rows[0].shape
    map_rows, piece = sum(m.shape[0] for m in maps), maps[0].shape[1]
    anywhere = pl.BlockSpec(memory_space=pl.ANY)
    in_vmem = pl.BlockSpec(memory_space=pltpu.VMEM)
    return pl.pallas_call(
        functools.partial(up_kernel, (len(maps), len(rows)), tok, rank),
        out_shape=[jax.ShapeDtypeStruct((tok, piece), jnp.bfloat16)] * len(rows),
        in_specs=[pl.BlockSpec(memory_space=pltpu.SMEM), in_vmem] + [anywhere] * len(maps) + [in_vmem] * len(rows),
        out_specs=[in_vmem] * len(rows),
        scratch_shapes=[
            pltpu.VMEM((map_rows, piece), jnp.bfloat16),
            pltpu.VMEM((len(rows), rank, tok), jnp.bfloat16),
            pltpu.VMEM((len(rows), tok, piece), jnp.bfloat16),
            pltpu.SemaphoreType.DMA((len(maps),)),
        ],
        compiler_params=pltpu.CompilerParams(vmem_limit_bytes=VMEM_BYTES),
        cost_estimate=pl.CostEstimate(
            flops=2 * map_rows * len(rows) * tok * piece,
            bytes_accessed=2 * piece * (map_rows + len(rows) * tok),
            transcendentals=0,
        ),
        name="up_product",
    )(labels, ids, *maps, *rows)


def place_kernel(members, pieces, me_ref, *refs):
    blocks, out_ref, sems = refs[: members * pieces], refs[-2], refs[-1]
    piece = blocks[0].shape[1]
    copies = []
    for n in range(members * pieces):
        offset, part = n % members, n // members
        at = (me_ref[0] ^ offset) * (pieces * piece) + part * piece
        target = out_ref.at[:, pl.ds(pl.multiple_of(at, 128), piece)]
        copies.append(pltpu.make_async_copy(blocks[n], target, sems.at[n]))
    for copy in copies:
        copy.start()
    for copy in copies:
        copy.wait()


def place(me, results):
    members, pieces = len(results[0]), len(results)
    tok, piece = results[0][0].shape
    anywhere = pl.BlockSpec(memory_space=pl.ANY)
    return pl.pallas_call(
        functools.partial(place_kernel, members, pieces),
        out_shape=jax.ShapeDtypeStruct((tok, members * pieces * piece), jnp.bfloat16),
        in_specs=[pl.BlockSpec(memory_space=pltpu.SMEM)] + [anywhere] * (members * pieces),
        out_specs=anywhere,
        scratch_shapes=[pltpu.SemaphoreType.DMA((members * pieces,))],
        compiler_params=pltpu.CompilerParams(vmem_limit_bytes=VMEM_BYTES),
        name="place_results",
    )(me, *[block for part in results for block in part])


def per_device(token_adapter_index, hidden, adapter_down_maps, adapter_up_maps):
    tok, width = hidden.shape
    groups, inner, outer = lax.axis_size("groups"), lax.axis_size("inner"), lax.axis_size("outer")
    members = groups * inner
    share = width // members
    rank = adapter_up_maps.shape[1]
    pieces = max(1, min(4, share // 256))
    piece = share // pieces
    per_ring = max(1, inner // 4)
    group, place_in_group, level = lax.axis_index("groups"), lax.axis_index("inner"), lax.axis_index("outer")
    me = group * inner + place_in_group

    def columns(array, offset):
        return lax.dynamic_slice_in_dim(array, (me ^ offset) * share, share, axis=1)

    def exchanged(array):
        blocks = [columns(array, 0)]
        for offset in range(1, inner):
            blocks.append(to_partner(columns(array, offset), "inner", inner, offset))
        return blocks

    blocks = exchanged(adapter_down_maps[0].T)
    rings = []
    for first in range(0, inner, per_ring):
        some = blocks[first : first + per_ring]
        rings.append(ring(some[0] if per_ring == 1 else jnp.concatenate(some, axis=0), outer))
    down_maps = [r[k] for k in range(outer) for r in rings]

    rows = [columns(hidden, 0)]
    for offset in range(1, members):
        rows.append(to_partner(columns(hidden, offset), PLANE, members, offset))
    ids = token_adapter_index[:, 0].reshape(1, tok)
    bit = 1
    while bit < members:
        ids = jnp.concatenate([ids, to_partner(ids, PLANE, members, bit)], axis=0)
        bit *= 2

    steps_back = jnp.arange(outer, dtype=jnp.int32)[:, None]
    labels = ((level - steps_back + outer) % outer) * inner + (
        place_in_group ^ jnp.arange(inner, dtype=jnp.int32)[None, :]
    )
    labels = labels.reshape(-1)

    partial = down_product(labels, ids, down_maps, rows, rank)
    total = partial[0]
    for offset in range(1, members):
        total = total + to_partner(partial[offset], PLANE, members, offset)
    own = total.astype(jnp.bfloat16)
    shrunk = [own] + [to_partner(own, PLANE, members, offset) for offset in range(1, members)]

    up_blocks = exchanged(adapter_up_maps[0])
    results = []
    for part in range(pieces):
        block = jnp.concatenate([b[:, part * piece : (part + 1) * piece] for b in up_blocks], axis=0)
        delta = up_product(labels, ids, ring(block, outer), shrunk)
        results.append(
            [delta[0]] + [to_partner(delta[offset], PLANE, members, offset) for offset in range(1, members)]
        )
    return place(me.reshape(1), results)


def solution(mesh):
    groups, wide = mesh.shape["groups"], mesh.shape["wide"]
    outer = 1 << ((wide.bit_length() - 1) // 2)
    fine = Mesh(mesh.devices.reshape(groups, outer, wide // outer), ("groups", "outer", "inner"))
    owner = ("outer", "inner")
    rows = P(("groups",) + owner, None)
    return jax.shard_map(
        per_device,
        mesh=fine,
        in_specs=(rows, rows, P(owner, None, None), P(owner, None, None)),
        out_specs=rows,
        check_vma=False,
    )
```

```python
import functools

import jax
import jax.numpy as jnp
from jax import lax
from jax.experimental import pallas as pl
from jax.experimental.pallas import tpu as pltpu
from jax.sharding import Mesh
from jax.sharding import PartitionSpec as P

adapter_scale = 2.0
PLANE = ("groups", "mid")
LANES = 128
CORES = 2
VMEM_BYTES = 40 << 20


def to_partner(value, axes, size, offset):
    return lax.ppermute(value, axes, [(i, i ^ offset) for i in range(size)])


def ring(block, outer):
    blocks = [block]
    for _ in range(outer - 1):
        block = lax.ppermute(block, "outer", [(i, (i + 1) % outer) for i in range(outer)])
        blocks.append(block)
    return blocks


def load_maps(sources, target, sems, rank):
    copies = []
    for first in range(0, len(sources), CORES):
        for at in range(0, sources[first].shape[0], rank):
            for source in sources[first : first + CORES]:
                n = len(copies)
                target_rows = target.at[pl.ds(n * rank, rank)]
                copies.append(pltpu.make_async_copy(source.at[pl.ds(at, rank)], target_rows, sems.at[n]))
    for copy in copies:
        copy.start()
    return copies


def pair_labels(labels_ref, pair, rank, shape):
    per_tile = LANES // rank
    lane = lax.broadcasted_iota(jnp.int32, shape, 1)
    label = jnp.full(shape, labels_ref[pair * per_tile], jnp.int32)
    for n in range(1, per_tile):
        label = jnp.where(lane >= n * rank, labels_ref[pair * per_tile + n], label)
    return label


def outgoing_kernel(members, share, hidden_ref, ids_ref, out_ref):
    for member in range(members):
        out_ref[member, :, :share] = hidden_ref[:, member * share : (member + 1) * share]
        out_ref[member, :, share:] = ids_ref[...]


def outgoing_rows(hidden, ids, members):
    tok, width = hidden.shape
    share = width // members
    in_vmem = pl.BlockSpec(memory_space=pltpu.VMEM)
    return pl.pallas_call(
        functools.partial(outgoing_kernel, members, share),
        out_shape=jax.ShapeDtypeStruct((members, tok, share + LANES), jnp.bfloat16),
        in_specs=[in_vmem, in_vmem],
        out_specs=in_vmem,
        compiler_params=pltpu.CompilerParams(vmem_limit_bytes=VMEM_BYTES),
        name="outgoing_rows",
    )(hidden, ids)


def down_kernel(map_count, rank, labels_ref, rows_ref, *refs):
    maps, (sums_ref, map_buf, sems) = refs[:map_count], refs[map_count:]
    for copy in load_maps(maps, map_buf, sems, rank):
        copy.wait()
    members, tok, _ = rows_ref.shape
    share = map_buf.shape[1]
    tiles = map_buf.shape[0] // LANES
    batch = 2 if tiles % 2 == 0 else 1

    def one(member, _):
        ids = rows_ref[member, :, share:].astype(jnp.float32).astype(jnp.int32)
        tokens = rows_ref[member, :, :share]
        total = jnp.zeros((tok, LANES), jnp.float32)
        for first in range(0, tiles, batch):
            product = lax.dot_general(
                tokens,
                map_buf[first * LANES : (first + batch) * LANES, :],
                (((1,), (1,)), ((), ())),
                preferred_element_type=jnp.float32,
            )
            for n in range(batch):
                named = ids == pair_labels(labels_ref, first + n, rank, ids.shape)
                total += jnp.where(named, product[:, n * LANES : (n + 1) * LANES], 0.0)
        sums_ref[member] = total
        return 0

    lax.fori_loop(0, members, one, 0)


def down_product(labels, rows, maps, rank):
    members, tok, wide_share = rows.shape
    share = wide_share - LANES
    map_rows = sum(m.shape[0] for m in maps)
    in_vmem = pl.BlockSpec(memory_space=pltpu.VMEM)
    return pl.pallas_call(
        functools.partial(down_kernel, len(maps), rank),
        out_shape=jax.ShapeDtypeStruct((members, tok, LANES), jnp.float32),
        in_specs=[pl.BlockSpec(memory_space=pltpu.SMEM), in_vmem]
        + [pl.BlockSpec(memory_space=pl.ANY)] * len(maps),
        out_specs=in_vmem,
        scratch_shapes=[
            pltpu.VMEM((map_rows, share), jnp.bfloat16),
            pltpu.SemaphoreType.DMA((map_rows // rank,)),
        ],
        compiler_params=pltpu.CompilerParams(vmem_limit_bytes=VMEM_BYTES),
        cost_estimate=pl.CostEstimate(
            flops=2 * map_rows * members * tok * share,
            bytes_accessed=2 * share * (map_rows + members * tok),
            transcendentals=0,
        ),
        name="down_product",
    )(labels, rows, *maps)


def up_kernel(map_count, rank, labels_ref, rows_ref, shrunk_ref, *refs):
    maps, (out_ref, map_buf, sems) = refs[:map_count], refs[map_count:]
    for copy in load_maps(maps, map_buf, sems, rank):
        copy.wait()
    members, tok, _ = shrunk_ref.shape
    tiles = map_buf.shape[0] // LANES

    def one(member, _):
        ids = rows_ref[member, :, :].astype(jnp.float32).astype(jnp.int32)
        shrunk = shrunk_ref[member].astype(jnp.float32)
        spread = [
            jnp.where(ids == pair_labels(labels_ref, tile, rank, ids.shape), shrunk, 0.0).astype(jnp.bfloat16)
            for tile in range(tiles)
        ]
        product = jnp.dot(
            jnp.concatenate(spread, axis=1), map_buf[...], preferred_element_type=jnp.float32
        )
        out_ref[member] = (adapter_scale * product).astype(jnp.bfloat16)
        return 0

    lax.fori_loop(0, members, one, 0)


def up_product(labels, rows, shrunk, maps, rank):
    members, tok, _ = shrunk.shape
    share = rows.shape[2] - LANES
    map_rows, piece = sum(m.shape[0] for m in maps), maps[0].shape[1]
    in_vmem = pl.BlockSpec(memory_space=pltpu.VMEM)
    return pl.pallas_call(
        functools.partial(up_kernel, len(maps), rank),
        grid=(1,),
        out_shape=jax.ShapeDtypeStruct((members, tok, piece), jnp.bfloat16),
        in_specs=[
            pl.BlockSpec(memory_space=pltpu.SMEM),
            pl.BlockSpec((members, tok, LANES), lambda _: (0, 0, share // LANES)),
            in_vmem,
        ]
        + [pl.BlockSpec(memory_space=pl.ANY)] * len(maps),
        out_specs=in_vmem,
        scratch_shapes=[
            pltpu.VMEM((map_rows, piece), jnp.bfloat16),
            pltpu.SemaphoreType.DMA((map_rows // rank,)),
        ],
        compiler_params=pltpu.CompilerParams(vmem_limit_bytes=VMEM_BYTES),
        cost_estimate=pl.CostEstimate(
            flops=2 * map_rows * members * tok * piece,
            bytes_accessed=2 * piece * (map_rows + members * tok),
            transcendentals=0,
        ),
        name="up_product",
    )(labels, rows, shrunk, *maps)


def place_kernel(pieces, *refs):
    parts, out_ref, sems = refs[:pieces], refs[-2], refs[-1]
    members, _, piece = parts[0].shape
    copies = []
    for n in range(members * pieces):
        member, part = n // pieces, n % pieces
        target = out_ref.at[:, pl.ds(n * piece, piece)]
        copies.append(pltpu.make_async_copy(parts[part].at[member], target, sems.at[n]))
    for copy in copies:
        copy.start()
    for copy in copies:
        copy.wait()


def place(parts):
    members, tok, piece = parts[0].shape
    anywhere = pl.BlockSpec(memory_space=pl.ANY)
    return pl.pallas_call(
        functools.partial(place_kernel, len(parts)),
        out_shape=jax.ShapeDtypeStruct((tok, members * len(parts) * piece), jnp.bfloat16),
        in_specs=[anywhere] * len(parts),
        out_specs=anywhere,
        scratch_shapes=[pltpu.SemaphoreType.DMA((members * len(parts),))],
        compiler_params=pltpu.CompilerParams(vmem_limit_bytes=VMEM_BYTES),
        name="place_results",
    )(*parts)


def after(value, earlier):
    return lax.optimization_barrier((value, earlier))[0]


def per_device(token_adapter_index, hidden, adapter_down_maps, adapter_up_maps):
    tok, width = hidden.shape
    groups, outer, mid, cores = (lax.axis_size(a) for a in ("groups", "outer", "mid", "cores"))
    members = groups * mid
    share = width // members
    rank = adapter_up_maps.shape[1]
    pieces = 2
    piece = share // pieces
    group, row, level, core = (lax.axis_index(a) for a in ("groups", "mid", "outer", "cores"))
    me = group * mid + row

    def columns(array, offset):
        return lax.dynamic_slice_in_dim(array, (me ^ offset) * share, share, axis=1)

    def exchanged(array):
        return [columns(array, 0)] + [
            to_partner(columns(array, offset), "mid", mid, offset) for offset in range(1, mid)
        ]

    def with_other_core(block):
        return [block] + [to_partner(block, "cores", cores, offset) for offset in range(1, cores)]

    rows_per_ring = max(1, mid // 2)

    def labels_of(first_row, row_count):
        back = jnp.arange(outer, dtype=jnp.int32)[:, None, None]
        rows_ = first_row + jnp.arange(row_count, dtype=jnp.int32)[None, :, None]
        cores_ = jnp.arange(cores, dtype=jnp.int32)[None, None, :]
        owner = ((level - back + outer) % outer) * mid + (row ^ rows_)
        return (owner * cores + (core ^ cores_)).reshape(-1)

    down_blocks = exchanged(adapter_down_maps[0].T)
    down_maps, down_labels, last = [], [], None
    for first in range(0, mid, rows_per_ring):
        some = down_blocks[first : first + rows_per_ring]
        blocks = ring(some[0] if len(some) == 1 else jnp.concatenate(some, axis=0), outer)
        last = blocks[-2]
        down_maps += [b for block in blocks for b in with_other_core(block)]
        down_labels.append(labels_of(first, rows_per_ring))
    down_labels = jnp.concatenate(down_labels)

    ids = jnp.broadcast_to(token_adapter_index.astype(jnp.bfloat16), (tok, LANES))
    rows = lax.all_to_all(outgoing_rows(hidden, ids, members), PLANE, split_axis=0, concat_axis=0, tiled=True)

    partial = down_product(down_labels, rows, down_maps, rank)
    terms = lax.all_to_all(partial, PLANE, split_axis=0, concat_axis=0, tiled=True)
    own = jnp.sum(terms, axis=0).astype(jnp.bfloat16)
    shrunk = lax.all_to_all(
        jnp.broadcast_to(own[None], (members,) + own.shape), PLANE, split_axis=0, concat_axis=0, tiled=True
    )

    up_blocks = exchanged(after(adapter_up_maps[0], last))
    up_labels = labels_of(0, mid)
    parts = []
    for part in range(pieces):
        block = jnp.concatenate([b[:, part * piece : (part + 1) * piece] for b in up_blocks], axis=0)
        maps = [b for held in ring(block, outer) for b in with_other_core(held)]
        delta = up_product(up_labels, rows, shrunk, maps, rank)
        parts.append(lax.all_to_all(delta, PLANE, split_axis=0, concat_axis=0, tiled=True))
    return place(parts)


def solution(mesh):
    groups, wide = mesh.shape["groups"], mesh.shape["wide"]
    outer = 1 << ((wide.bit_length() - 1) // 2)
    fine = Mesh(
        mesh.devices.reshape(groups, outer, wide // (outer * CORES), CORES), ("groups", "outer", "mid", "cores")
    )
    owner = ("outer", "mid", "cores")
    rows = P(("groups",) + owner, None)
    return jax.shard_map(
        per_device,
        mesh=fine,
        in_specs=(rows, rows, P(owner, None, None), P(owner, None, None)),
        out_specs=rows,
        check_vma=False,
    )
```

```python
import functools

import jax
import jax.numpy as jnp
from jax import lax
from jax.experimental import pallas as pl
from jax.experimental.pallas import tpu as pltpu
from jax.sharding import Mesh
from jax.sharding import PartitionSpec as P

adapter_scale = 2.0
PLANE = ("groups", "inner")
LANES = 128
ID_ROWS = 8
BLOCK = 8
VMEM_BYTES = 48 << 20
IN_VMEM = pl.BlockSpec(memory_space=pltpu.VMEM)
IN_SMEM = pl.BlockSpec(memory_space=pltpu.SMEM)
ANYWHERE = pl.BlockSpec(memory_space=pl.ANY)
PARAMS = pltpu.CompilerParams(vmem_limit_bytes=VMEM_BYTES)


def to_partner(value, axes, size, offset):
    return lax.ppermute(value, axes, [(i, i ^ offset) for i in range(size)])


def next_on_ring(block, outer):
    return lax.ppermute(block, "outer", [(i, (i + 1) % outer) for i in range(outer)])


def after(value, *earlier):
    return lax.optimization_barrier((value,) + earlier)[0]


def swap(value):
    return lax.all_to_all(value, PLANE, split_axis=0, concat_axis=0, tiled=True)


def tile_labels(labels_ref, tile, rank, shape):
    per_tile = LANES // rank
    lane = lax.broadcasted_iota(jnp.int32, shape, 1)
    label = jnp.full(shape, labels_ref[tile * per_tile], jnp.int32)
    for n in range(1, per_tile):
        label = jnp.where(lane >= n * rank, labels_ref[tile * per_tile + n], label)
    return label.astype(jnp.float32)


def outgoing_kernel(hidden_ref, ids_ref, out_ref):
    members, rows, share = out_ref.shape
    tok = rows - ID_ROWS
    for member in range(members):
        out_ref[member, :tok, :] = hidden_ref[:, member * share : (member + 1) * share]
        out_ref[member, tok:, :] = ids_ref[...]


def outgoing_rows(hidden, ids, members):
    tok, width = hidden.shape
    share = width // members
    ids = jnp.broadcast_to(jnp.pad(ids, ((0, 0), (0, share - tok))), (ID_ROWS, share))
    return pl.pallas_call(
        outgoing_kernel,
        out_shape=jax.ShapeDtypeStruct((members, tok + ID_ROWS, share), jnp.bfloat16),
        in_specs=[IN_VMEM, IN_VMEM],
        out_specs=IN_VMEM,
        compiler_params=PARAMS,
        name="outgoing_rows",
    )(hidden, ids)


def down_kernel(map_count, rank, labels_ref, rows_ref, *refs):
    maps, (packed_ref, ids_ref, total_ref) = refs[:map_count], refs[map_count:]
    members, rows, share = rows_ref.shape
    tok = rows - ID_ROWS
    block = min(BLOCK, members)
    half = tok // 2
    lane = lax.broadcasted_iota(jnp.int32, (half, LANES), 1)

    def one(step, _):
        first = step * block
        for n in range(block):
            row = rows_ref[first + n, tok : tok + 1, :LANES].astype(jnp.float32)
            ids_ref[first + n] = jnp.broadcast_to(row, (LANES, tok)).T
        tokens = rows_ref[pl.ds(first, block), :tok, :].reshape(block * tok, share)
        ids = ids_ref[pl.ds(first, block)].reshape(block * tok, LANES)
        tile = 0
        for at in range(0, map_count, 2):
            some = jnp.concatenate([m[...] for m in maps[at : at + 2]], axis=0)
            product = lax.dot_general(
                tokens, some, (((1,), (1,)), ((), ())), preferred_element_type=jnp.float32
            )
            total = jnp.zeros((block * tok, LANES), jnp.float32) if tile == 0 else total_ref[...]
            for n in range(some.shape[0] // LANES):
                named = ids == tile_labels(labels_ref, tile, rank, (1, LANES))
                total += jnp.where(named, product[:, n * LANES : (n + 1) * LANES], 0.0)
                tile += 1
            total_ref[...] = total
        for n in range(block):
            total = total_ref[n * tok : (n + 1) * tok, :]
            total += pltpu.roll(total, LANES // 2, 1)
            packed_ref[first + n] = jnp.where(lane < rank, total[:half], total[half:])
        return 0

    lax.fori_loop(0, members // block, one, 0)


def down_product(labels, rows, maps, rank):
    members, tok, share = rows.shape
    tok -= ID_ROWS
    map_rows = sum(m.shape[0] for m in maps)
    return pl.pallas_call(
        functools.partial(down_kernel, len(maps), rank),
        out_shape=[
            jax.ShapeDtypeStruct((members, tok // 2, LANES), jnp.float32),
            jax.ShapeDtypeStruct((members, tok, LANES), jnp.float32),
        ],
        in_specs=[IN_SMEM, IN_VMEM] + [IN_VMEM] * len(maps),
        out_specs=[IN_VMEM, IN_VMEM],
        scratch_shapes=[pltpu.VMEM((min(BLOCK, members) * tok, LANES), jnp.float32)],
        compiler_params=PARAMS,
        cost_estimate=pl.CostEstimate(
            flops=2 * map_rows * members * tok * share,
            bytes_accessed=2 * share * (map_rows + members * tok),
            transcendentals=0,
        ),
        name="down_product",
    )(labels, rows, *maps)


def copies_kernel(terms_ref, out_ref):
    own = jnp.sum(terms_ref[...], axis=0).astype(jnp.bfloat16)
    for member in range(out_ref.shape[0]):
        out_ref[member] = own


def summed_copies(terms):
    return pl.pallas_call(
        copies_kernel,
        out_shape=jax.ShapeDtypeStruct(terms.shape, jnp.bfloat16),
        in_specs=[IN_VMEM],
        out_specs=IN_VMEM,
        compiler_params=PARAMS,
        name="summed_copies",
    )(terms)


def up_kernel(map_count, rank, labels_ref, ids_ref, shrunk_ref, *refs):
    maps, (out_ref, spread_ref) = refs[:map_count], refs[map_count:]
    members, half, _ = shrunk_ref.shape
    tok = 2 * half
    block = min(BLOCK, members)
    tiles = spread_ref.shape[1] // LANES
    lane = lax.broadcasted_iota(jnp.int32, (half, LANES), 1)
    held = jnp.concatenate([m[...] for m in maps], axis=0)

    def one(step, _):
        first = step * block
        for n in range(block):
            packed = shrunk_ref[first + n].astype(jnp.float32)
            turned = pltpu.roll(packed, LANES // 2, 1)
            shrunk = jnp.concatenate(
                [jnp.where(lane < rank, packed, turned), jnp.where(lane < rank, turned, packed)], axis=0
            )
            ids = ids_ref[first + n]
            for tile in range(tiles):
                named = ids == tile_labels(labels_ref, tile, rank, (1, LANES))
                spread_ref[n * tok : (n + 1) * tok, tile * LANES : (tile + 1) * LANES] = jnp.where(
                    named, shrunk, 0.0
                ).astype(jnp.bfloat16)
        product = jnp.dot(spread_ref[...], held, preferred_element_type=jnp.float32)
        product = (adapter_scale * product).astype(jnp.bfloat16)
        out_ref[pl.ds(first, block)] = product.reshape(block, tok, product.shape[1])
        return 0

    lax.fori_loop(0, members // block, one, 0)


def up_product(labels, ids, shrunk, maps, rank):
    members, tok, _ = ids.shape
    map_rows, piece = sum(m.shape[0] for m in maps), maps[0].shape[1]
    return pl.pallas_call(
        functools.partial(up_kernel, len(maps), rank),
        out_shape=jax.ShapeDtypeStruct((members, tok, piece), jnp.bfloat16),
        in_specs=[IN_SMEM, IN_VMEM, IN_VMEM] + [IN_VMEM] * len(maps),
        out_specs=IN_VMEM,
        scratch_shapes=[pltpu.VMEM((min(BLOCK, members) * tok, map_rows), jnp.bfloat16)],
        compiler_params=PARAMS,
        cost_estimate=pl.CostEstimate(
            flops=2 * map_rows * members * tok * piece,
            bytes_accessed=2 * piece * (map_rows + members * tok),
            transcendentals=0,
        ),
        name="up_product",
    )(labels, ids, shrunk, *maps)


def place_kernel(pieces, *refs):
    parts, out_ref, sems = refs[:pieces], refs[-2], refs[-1]
    members, _, piece = parts[0].shape
    copies = []
    for n in range(members * pieces):
        member, part = n // pieces, n % pieces
        target = out_ref.at[:, pl.ds(n * piece, piece)]
        copies.append(pltpu.make_async_copy(parts[part].at[member], target, sems.at[n]))
    for copy in copies:
        copy.start()
    for copy in copies:
        copy.wait()


def place(parts):
    members, tok, piece = parts[0].shape
    return pl.pallas_call(
        functools.partial(place_kernel, len(parts)),
        out_shape=jax.ShapeDtypeStruct((tok, members * len(parts) * piece), jnp.bfloat16),
        in_specs=[ANYWHERE] * len(parts),
        out_specs=ANYWHERE,
        scratch_shapes=[pltpu.SemaphoreType.DMA((members * len(parts),))],
        compiler_params=PARAMS,
        name="place_results",
    )(*parts)


def per_device(token_adapter_index, hidden, adapter_down_maps, adapter_up_maps):
    tok, width = hidden.shape
    groups, outer, inner = (lax.axis_size(a) for a in ("groups", "outer", "inner"))
    group, level, place_in_group = (lax.axis_index(a) for a in ("groups", "outer", "inner"))
    members = groups * inner
    share = width // members
    rank = adapter_up_maps.shape[1]
    pieces = 2 if share % (2 * LANES) == 0 else 1
    piece = share // pieces
    me = group * inner + place_in_group

    def slices(array):
        return [
            lax.dynamic_slice_in_dim(array, (me ^ offset) * share, share, axis=1) for offset in range(inner)
        ]

    def exchanged(blocks):
        return blocks[:1] + [to_partner(blocks[n], "inner", inner, n) for n in range(1, inner)]

    steps_back = jnp.arange(outer, dtype=jnp.int32)[:, None]
    labels = ((level - steps_back + outer) % outer) * inner + (
        place_in_group ^ jnp.arange(inner, dtype=jnp.int32)[None, :]
    )
    labels = labels.reshape(-1)

    down = exchanged(slices(adapter_down_maps[0].T))
    near = [jnp.concatenate(down[: inner // 2], axis=0)]
    far = [jnp.concatenate(down[inner // 2 :], axis=0)]
    for _ in range(outer - 1):
        near.append(next_on_ring(near[-1], outer))
        far.append(next_on_ring(far[-1], outer))
    down_maps = [m for pair in zip(near, far) for m in pair]

    ids = token_adapter_index.astype(jnp.bfloat16).reshape(1, tok)
    rows = swap(after(outgoing_rows(hidden, ids, members), *down[inner // 2 :]))

    own_slices = slices(adapter_up_maps[0])
    up = exchanged([after(block, rows) for block in own_slices])
    held = [
        [jnp.concatenate([b[:, n * piece : (n + 1) * piece] for b in up], axis=0)] for n in range(pieces)
    ]
    held[0][0] = after(held[0][0], near[-1])
    held[-1][0] = after(held[-1][0], far[-1])
    for ring in held:
        for _ in range(outer - 1):
            ring.append(next_on_ring(ring[-1], outer))

    packed, id_columns = down_product(labels, rows, down_maps, rank)
    shrunk = swap(summed_copies(swap(packed)))
    return place([swap(up_product(labels, id_columns, shrunk, ring, rank)) for ring in held])


def solution(mesh):
    groups, wide = mesh.shape["groups"], mesh.shape["wide"]
    outer = 1 << ((wide.bit_length() - 1) // 2)
    fine = Mesh(mesh.devices.reshape(groups, outer, wide // outer), ("groups", "outer", "inner"))
    owner = ("outer", "inner")
    rows = P(("groups",) + owner, None)
    return jax.shard_map(
        per_device,
        mesh=fine,
        in_specs=(rows, rows, P(owner, None, None), P(owner, None, None)),
        out_specs=rows,
        check_vma=False,
    )
```

```python
import functools

import jax
import jax.numpy as jnp
from jax import lax
from jax.experimental import pallas as pl
from jax.experimental.pallas import tpu as pltpu
from jax.sharding import Mesh
from jax.sharding import PartitionSpec as P

adapter_scale = 2.0
PLANE = ("groups", "inner")
LANES = 128
ID_ROWS = 8
BLOCK = 8
VMEM_BYTES = 48 << 20
IN_VMEM = pl.BlockSpec(memory_space=pltpu.VMEM)
IN_SMEM = pl.BlockSpec(memory_space=pltpu.SMEM)
ANYWHERE = pl.BlockSpec(memory_space=pl.ANY)
PARAMS = pltpu.CompilerParams(vmem_limit_bytes=VMEM_BYTES)


def to_partner(value, axes, size, offset):
    return lax.ppermute(value, axes, [(i, i ^ offset) for i in range(size)])


def next_on_ring(block, outer):
    return lax.ppermute(block, "outer", [(i, (i + 1) % outer) for i in range(outer)])


def after(value, *earlier):
    return lax.optimization_barrier((value,) + earlier)[0]


def swap(value):
    return lax.all_to_all(value, PLANE, split_axis=0, concat_axis=0, tiled=True)


def tile_labels(labels_ref, tile, rank, shape):
    per_tile = LANES // rank
    lane = lax.broadcasted_iota(jnp.int32, shape, 1)
    label = jnp.full(shape, labels_ref[tile * per_tile], jnp.int32)
    for n in range(1, per_tile):
        label = jnp.where(lane >= n * rank, labels_ref[tile * per_tile + n], label)
    return label.astype(jnp.float32)


def outgoing_kernel(hidden_ref, ids_ref, out_ref):
    members, rows, share = out_ref.shape
    tok = rows - ID_ROWS
    for member in range(members):
        out_ref[member, :tok, :] = hidden_ref[:, member * share : (member + 1) * share]
        out_ref[member, tok:, :] = ids_ref[...]


def outgoing_rows(hidden, ids, members):
    tok, width = hidden.shape
    share = width // members
    ids = jnp.broadcast_to(jnp.pad(ids, ((0, 0), (0, share - tok))), (ID_ROWS, share))
    return pl.pallas_call(
        outgoing_kernel,
        out_shape=jax.ShapeDtypeStruct((members, tok + ID_ROWS, share), jnp.bfloat16),
        in_specs=[IN_VMEM, IN_VMEM],
        out_specs=IN_VMEM,
        compiler_params=PARAMS,
        name="outgoing_rows",
    )(hidden, ids)


def down_kernel(map_count, rank, labels_ref, rows_ref, *refs):
    maps, (packed_ref, ids_ref, total_ref) = refs[:map_count], refs[map_count:]
    members, rows, share = rows_ref.shape
    tok = rows - ID_ROWS
    block = min(BLOCK, members)
    half = tok // 2
    lane = lax.broadcasted_iota(jnp.int32, (half, LANES), 1)

    def one(step, _):
        first = step * block
        for n in range(block):
            row = rows_ref[first + n, tok : tok + 1, :LANES].astype(jnp.float32)
            ids_ref[first + n] = jnp.broadcast_to(row, (LANES, tok)).T
        tokens = rows_ref[pl.ds(first, block), :tok, :].reshape(block * tok, share)
        ids = ids_ref[pl.ds(first, block)].reshape(block * tok, LANES)
        tile = 0
        for at in range(0, map_count, 2):
            some = jnp.concatenate([m[...] for m in maps[at : at + 2]], axis=0)
            product = lax.dot_general(
                tokens, some, (((1,), (1,)), ((), ())), preferred_element_type=jnp.float32
            )
            total = jnp.zeros((block * tok, LANES), jnp.float32) if tile == 0 else total_ref[...]
            for n in range(some.shape[0] // LANES):
                named = ids == tile_labels(labels_ref, tile, rank, (1, LANES))
                total += jnp.where(named, product[:, n * LANES : (n + 1) * LANES], 0.0)
                tile += 1
            total_ref[...] = total
        for n in range(block):
            total = total_ref[n * tok : (n + 1) * tok, :]
            total += pltpu.roll(total, LANES // 2, 1)
            packed_ref[first + n] = jnp.where(lane < rank, total[:half], total[half:])
        return 0

    lax.fori_loop(0, members // block, one, 0)


def down_product(labels, rows, maps, rank):
    members, tok, share = rows.shape
    tok -= ID_ROWS
    map_rows = sum(m.shape[0] for m in maps)
    return pl.pallas_call(
        functools.partial(down_kernel, len(maps), rank),
        out_shape=[
            jax.ShapeDtypeStruct((members, tok // 2, LANES), jnp.float32),
            jax.ShapeDtypeStruct((members, tok, LANES), jnp.float32),
        ],
        in_specs=[IN_SMEM, IN_VMEM] + [IN_VMEM] * len(maps),
        out_specs=[IN_VMEM, IN_VMEM],
        scratch_shapes=[pltpu.VMEM((min(BLOCK, members) * tok, LANES), jnp.float32)],
        compiler_params=PARAMS,
        cost_estimate=pl.CostEstimate(
            flops=2 * map_rows * members * tok * share,
            bytes_accessed=2 * share * (map_rows + members * tok),
            transcendentals=0,
        ),
        name="down_product",
    )(labels, rows, *maps)


def copies_kernel(terms_ref, out_ref):
    own = jnp.sum(terms_ref[...], axis=0).astype(jnp.bfloat16)
    for member in range(out_ref.shape[0]):
        out_ref[member] = own


def summed_copies(terms):
    return pl.pallas_call(
        copies_kernel,
        out_shape=jax.ShapeDtypeStruct(terms.shape, jnp.bfloat16),
        in_specs=[IN_VMEM],
        out_specs=IN_VMEM,
        compiler_params=PARAMS,
        name="summed_copies",
    )(terms)


def up_kernel(map_count, rank, labels_ref, ids_ref, shrunk_ref, *refs):
    maps, (out_ref, spread_ref) = refs[:map_count], refs[map_count:]
    members, half, _ = shrunk_ref.shape
    tok = 2 * half
    block = min(BLOCK, members)
    tiles = spread_ref.shape[1] // LANES
    lane = lax.broadcasted_iota(jnp.int32, (half, LANES), 1)
    held = jnp.concatenate([m[...] for m in maps], axis=0)

    def one(step, _):
        first = step * block
        for n in range(block):
            packed = shrunk_ref[first + n].astype(jnp.float32)
            turned = pltpu.roll(packed, LANES // 2, 1)
            shrunk = jnp.concatenate(
                [jnp.where(lane < rank, packed, turned), jnp.where(lane < rank, turned, packed)], axis=0
            )
            ids = ids_ref[first + n]
            for tile in range(tiles):
                named = ids == tile_labels(labels_ref, tile, rank, (1, LANES))
                spread_ref[n * tok : (n + 1) * tok, tile * LANES : (tile + 1) * LANES] = jnp.where(
                    named, shrunk, 0.0
                ).astype(jnp.bfloat16)
        product = jnp.dot(spread_ref[...], held, preferred_element_type=jnp.float32)
        product = (adapter_scale * product).astype(jnp.bfloat16)
        out_ref[pl.ds(first, block)] = product.reshape(block, tok, product.shape[1])
        return 0

    lax.fori_loop(0, members // block, one, 0)


def up_product(labels, ids, shrunk, maps, rank):
    members, tok, _ = ids.shape
    map_rows, piece = sum(m.shape[0] for m in maps), maps[0].shape[1]
    return pl.pallas_call(
        functools.partial(up_kernel, len(maps), rank),
        out_shape=jax.ShapeDtypeStruct((members, tok, piece), jnp.bfloat16),
        in_specs=[IN_SMEM, IN_VMEM, IN_VMEM] + [IN_VMEM] * len(maps),
        out_specs=IN_VMEM,
        scratch_shapes=[pltpu.VMEM((min(BLOCK, members) * tok, map_rows), jnp.bfloat16)],
        compiler_params=PARAMS,
        cost_estimate=pl.CostEstimate(
            flops=2 * map_rows * members * tok * piece,
            bytes_accessed=2 * piece * (map_rows + members * tok),
            transcendentals=0,
        ),
        name="up_product",
    )(labels, ids, shrunk, *maps)


def place_kernel(pieces, *refs):
    parts, out_ref, sems = refs[:pieces], refs[-2], refs[-1]
    members, _, piece = parts[0].shape
    copies = []
    for n in range(members * pieces):
        member, part = n // pieces, n % pieces
        target = out_ref.at[:, pl.ds(n * piece, piece)]
        copies.append(pltpu.make_async_copy(parts[part].at[member], target, sems.at[n]))
    for copy in copies:
        copy.start()
    for copy in copies:
        copy.wait()


def place(parts):
    members, tok, piece = parts[0].shape
    return pl.pallas_call(
        functools.partial(place_kernel, len(parts)),
        out_shape=jax.ShapeDtypeStruct((tok, members * len(parts) * piece), jnp.bfloat16),
        in_specs=[ANYWHERE] * len(parts),
        out_specs=ANYWHERE,
        scratch_shapes=[pltpu.SemaphoreType.DMA((members * len(parts),))],
        compiler_params=PARAMS,
        name="place_results",
    )(*parts)


def per_device(token_adapter_index, hidden, adapter_down_maps, adapter_up_maps):
    tok, width = hidden.shape
    groups, outer, inner = (lax.axis_size(a) for a in ("groups", "outer", "inner"))
    group, level, place_in_group = (lax.axis_index(a) for a in ("groups", "outer", "inner"))
    members = groups * inner
    share = width // members
    rank = adapter_up_maps.shape[1]
    pieces = 2 if share % (2 * LANES) == 0 else 1
    piece = share // pieces
    me = group * inner + place_in_group

    def slices(offset):
        start = (me ^ offset) * share
        return jnp.concatenate(
            [
                lax.dynamic_slice_in_dim(adapter_down_maps[0].T, start, share, axis=1),
                lax.dynamic_slice_in_dim(adapter_up_maps[0], start, share, axis=1),
            ],
            axis=0,
        )

    got = [slices(0)] + [to_partner(slices(n), "inner", inner, n) for n in range(1, inner)]

    steps_back = jnp.arange(outer, dtype=jnp.int32)[:, None]
    labels = ((level - steps_back + outer) % outer) * inner + (
        place_in_group ^ jnp.arange(inner, dtype=jnp.int32)[None, :]
    )
    labels = labels.reshape(-1)

    near = [jnp.concatenate([g[:rank] for g in got[: inner // 2]], axis=0)]
    far = [jnp.concatenate([g[:rank] for g in got[inner // 2 :]], axis=0)]
    for _ in range(outer - 1):
        near.append(next_on_ring(near[-1], outer))
        far.append(next_on_ring(far[-1], outer))
    down_maps = [m for pair in zip(near, far) for m in pair]

    ids = token_adapter_index.astype(jnp.bfloat16).reshape(1, tok)
    rows = swap(after(outgoing_rows(hidden, ids, members), got[1]))

    held = [
        [jnp.concatenate([g[rank:, n * piece : (n + 1) * piece] for g in got], axis=0)] for n in range(pieces)
    ]
    held[0][0] = after(held[0][0], near[-1], rows)
    held[-1][0] = after(held[-1][0], far[-1])
    for step in range(1, outer):
        for n in range(pieces):
            block = held[n][-1]
            if n == 0 and step > 1:
                block = after(block, held[-1][step - 2])
            held[n].append(next_on_ring(block, outer))

    packed, id_columns = down_product(labels, rows, down_maps, rank)
    shrunk = after(swap(summed_copies(swap(packed))), held[-1][-2])
    return place([swap(up_product(labels, id_columns, shrunk, ring, rank)) for ring in held])


def solution(mesh):
    groups, wide = mesh.shape["groups"], mesh.shape["wide"]
    outer = 1 << ((wide.bit_length() - 1) // 2)
    fine = Mesh(mesh.devices.reshape(groups, outer, wide // outer), ("groups", "outer", "inner"))
    owner = ("outer", "inner")
    rows = P(("groups",) + owner, None)
    return jax.shard_map(
        per_device,
        mesh=fine,
        in_specs=(rows, rows, P(owner, None, None), P(owner, None, None)),
        out_specs=rows,
        check_vma=False,
    )
```

```python
import functools

import jax
import jax.numpy as jnp
from jax import lax
from jax.experimental import pallas as pl
from jax.experimental.pallas import tpu as pltpu
from jax.sharding import Mesh
from jax.sharding import PartitionSpec as P

adapter_scale = 2.0
PLANE = ("groups", "inner")
LANES = 128
ID_ROWS = 8
BLOCK = 8
IN_VMEM = pl.BlockSpec(memory_space=pltpu.VMEM)
IN_SMEM = pl.BlockSpec(memory_space=pltpu.SMEM)
ANYWHERE = pl.BlockSpec(memory_space=pl.ANY)


def params(scratch_bytes=0):
    return pltpu.CompilerParams(vmem_limit_bytes=(12 << 20) + 2 * scratch_bytes)


def to_partner(value, axes, size, offset):
    return lax.ppermute(value, axes, [(i, i ^ offset) for i in range(size)])


def next_on_ring(block, outer):
    return lax.ppermute(block, "outer", [(i, (i + 1) % outer) for i in range(outer)])


def after(value, *earlier):
    return lax.optimization_barrier((value,) + earlier)[0]


def swap(value):
    return lax.all_to_all(value, PLANE, split_axis=0, concat_axis=0, tiled=True)


def tile_labels(labels_ref, tile, rank, shape):
    per_tile = LANES // rank
    lane = lax.broadcasted_iota(jnp.int32, shape, 1)
    label = jnp.full(shape, labels_ref[tile * per_tile], jnp.int32)
    for n in range(1, per_tile):
        label = jnp.where(lane >= n * rank, labels_ref[tile * per_tile + n], label)
    return label.astype(jnp.float32)


def outgoing_kernel(hidden_ref, ids_ref, out_ref):
    members, rows, share = out_ref.shape
    tok = rows - ID_ROWS
    for member in range(members):
        out_ref[member, :tok, :] = hidden_ref[:, member * share : (member + 1) * share]
        out_ref[member, tok:, :] = ids_ref[...]


def outgoing_rows(hidden, ids, members):
    tok, width = hidden.shape
    share = width // members
    ids = jnp.broadcast_to(jnp.pad(ids, ((0, 0), (0, share - tok))), (ID_ROWS, share))
    return pl.pallas_call(
        outgoing_kernel,
        out_shape=jax.ShapeDtypeStruct((members, tok + ID_ROWS, share), jnp.bfloat16),
        in_specs=[IN_VMEM, IN_VMEM],
        out_specs=IN_VMEM,
        compiler_params=params(),
        name="outgoing_rows",
    )(hidden, ids)


def down_kernel(map_count, rank, labels_ref, rows_ref, *refs):
    maps, (packed_ref, ids_ref, total_ref) = refs[:map_count], refs[map_count:]
    members, rows, share = rows_ref.shape
    tok = rows - ID_ROWS
    block = min(BLOCK, members)
    half = tok // 2
    lane = lax.broadcasted_iota(jnp.int32, (half, LANES), 1)

    def one(step, _):
        first = step * block
        for n in range(block):
            row = rows_ref[first + n, tok : tok + 1, :LANES].astype(jnp.float32)
            ids_ref[first + n] = jnp.broadcast_to(row, (LANES, tok)).T
        tokens = rows_ref[pl.ds(first, block), :tok, :].reshape(block * tok, share)
        ids = ids_ref[pl.ds(first, block)].reshape(block * tok, LANES)
        tile = 0
        for at in range(0, map_count, 2):
            some = jnp.concatenate([m[...] for m in maps[at : at + 2]], axis=0)
            product = lax.dot_general(
                tokens, some, (((1,), (1,)), ((), ())), preferred_element_type=jnp.float32
            )
            total = jnp.zeros((block * tok, LANES), jnp.float32) if tile == 0 else total_ref[...]
            for n in range(some.shape[0] // LANES):
                named = ids == tile_labels(labels_ref, tile, rank, (1, LANES))
                total += jnp.where(named, product[:, n * LANES : (n + 1) * LANES], 0.0)
                tile += 1
            total_ref[...] = total
        for n in range(block):
            total = total_ref[n * tok : (n + 1) * tok, :]
            total += pltpu.roll(total, LANES // 2, 1)
            packed_ref[first + n] = jnp.where(lane < rank, total[:half], total[half:])
        return 0

    lax.fori_loop(0, members // block, one, 0)


def down_product(labels, rows, maps, rank):
    members, tok, share = rows.shape
    tok -= ID_ROWS
    map_rows = sum(m.shape[0] for m in maps)
    return pl.pallas_call(
        functools.partial(down_kernel, len(maps), rank),
        out_shape=[
            jax.ShapeDtypeStruct((members, tok // 2, LANES), jnp.float32),
            jax.ShapeDtypeStruct((members, tok, LANES), jnp.float32),
        ],
        in_specs=[IN_SMEM, IN_VMEM] + [IN_VMEM] * len(maps),
        out_specs=[IN_VMEM, IN_VMEM],
        scratch_shapes=[pltpu.VMEM((min(BLOCK, members) * tok, LANES), jnp.float32)],
        compiler_params=params(4 * min(BLOCK, members) * tok * LANES),
        cost_estimate=pl.CostEstimate(
            flops=2 * map_rows * members * tok * share,
            bytes_accessed=2 * share * (map_rows + members * tok),
            transcendentals=0,
        ),
        name="down_product",
    )(labels, rows, *maps)


def copies_kernel(terms_ref, out_ref):
    own = jnp.sum(terms_ref[...], axis=0).astype(jnp.bfloat16)
    for member in range(out_ref.shape[0]):
        out_ref[member] = own


def summed_copies(terms):
    return pl.pallas_call(
        copies_kernel,
        out_shape=jax.ShapeDtypeStruct(terms.shape, jnp.bfloat16),
        in_specs=[IN_VMEM],
        out_specs=IN_VMEM,
        compiler_params=params(),
        name="summed_copies",
    )(terms)


def up_kernel(map_count, rank, labels_ref, ids_ref, shrunk_ref, *refs):
    maps, (out_ref, spread_ref) = refs[:map_count], refs[map_count:]
    members, half, _ = shrunk_ref.shape
    tok = 2 * half
    block = min(BLOCK, members)
    tiles = spread_ref.shape[1] // LANES
    lane = lax.broadcasted_iota(jnp.int32, (half, LANES), 1)
    held = jnp.concatenate([m[...] for m in maps], axis=0)

    def one(step, _):
        first = step * block
        for n in range(block):
            packed = shrunk_ref[first + n].astype(jnp.float32)
            turned = pltpu.roll(packed, LANES // 2, 1)
            shrunk = jnp.concatenate(
                [jnp.where(lane < rank, packed, turned), jnp.where(lane < rank, turned, packed)], axis=0
            )
            ids = ids_ref[first + n]
            for tile in range(tiles):
                named = ids == tile_labels(labels_ref, tile, rank, (1, LANES))
                spread_ref[n * tok : (n + 1) * tok, tile * LANES : (tile + 1) * LANES] = jnp.where(
                    named, shrunk, 0.0
                ).astype(jnp.bfloat16)
        product = jnp.dot(spread_ref[...], held, preferred_element_type=jnp.float32)
        product = (adapter_scale * product).astype(jnp.bfloat16)
        out_ref[pl.ds(first, block)] = product.reshape(block, tok, product.shape[1])
        return 0

    lax.fori_loop(0, members // block, one, 0)


def up_product(labels, ids, shrunk, maps, rank):
    members, tok, _ = ids.shape
    map_rows, piece = sum(m.shape[0] for m in maps), maps[0].shape[1]
    return pl.pallas_call(
        functools.partial(up_kernel, len(maps), rank),
        out_shape=jax.ShapeDtypeStruct((members, tok, piece), jnp.bfloat16),
        in_specs=[IN_SMEM, IN_VMEM, IN_VMEM] + [IN_VMEM] * len(maps),
        out_specs=IN_VMEM,
        scratch_shapes=[pltpu.VMEM((min(BLOCK, members) * tok, map_rows), jnp.bfloat16)],
        compiler_params=params(2 * min(BLOCK, members) * tok * map_rows),
        cost_estimate=pl.CostEstimate(
            flops=2 * map_rows * members * tok * piece,
            bytes_accessed=2 * piece * (map_rows + members * tok),
            transcendentals=0,
        ),
        name="up_product",
    )(labels, ids, shrunk, *maps)


def place_kernel(pieces, *refs):
    parts, out_ref, sems = refs[:pieces], refs[-2], refs[-1]
    members, _, piece = parts[0].shape
    copies = []
    for n in range(members * pieces):
        member, part = n // pieces, n % pieces
        target = out_ref.at[:, pl.ds(n * piece, piece)]
        copies.append(pltpu.make_async_copy(parts[part].at[member], target, sems.at[n]))
    for copy in copies:
        copy.start()
    for copy in copies:
        copy.wait()


def place(parts):
    members, tok, piece = parts[0].shape
    return pl.pallas_call(
        functools.partial(place_kernel, len(parts)),
        out_shape=jax.ShapeDtypeStruct((tok, members * len(parts) * piece), jnp.bfloat16),
        in_specs=[ANYWHERE] * len(parts),
        out_specs=ANYWHERE,
        scratch_shapes=[pltpu.SemaphoreType.DMA((members * len(parts),))],
        compiler_params=params(),
        name="place_results",
    )(*parts)


def per_device(token_adapter_index, hidden, adapter_down_maps, adapter_up_maps):
    tok, width = hidden.shape
    groups, outer, inner = (lax.axis_size(a) for a in ("groups", "outer", "inner"))
    group, level, place_in_group = (lax.axis_index(a) for a in ("groups", "outer", "inner"))
    members = groups * inner
    share = width // members
    rank = adapter_up_maps.shape[1]
    me = group * inner + place_in_group

    def slices(array):
        return [
            lax.dynamic_slice_in_dim(array, (me ^ offset) * share, share, axis=1) for offset in range(inner)
        ]

    def exchanged(blocks):
        return blocks[:1] + [to_partner(blocks[n], "inner", inner, n) for n in range(1, inner)]

    def rings(blocks, near_after=(), far_after=(), second_after=()):
        near = [after(jnp.concatenate(blocks[: inner // 2], axis=0), *near_after)]
        far = [after(jnp.concatenate(blocks[inner // 2 :], axis=0), *far_after)]
        for step in range(1, outer):
            near.append(next_on_ring(after(near[-1], *second_after) if step == 2 else near[-1], outer))
            far.append(next_on_ring(far[-1], outer))
        return near, far

    steps_back = jnp.arange(outer, dtype=jnp.int32)[:, None]
    labels = ((level - steps_back + outer) % outer) * inner + (
        place_in_group ^ jnp.arange(inner, dtype=jnp.int32)[None, :]
    )
    labels = labels.reshape(-1)

    down = exchanged(slices(adapter_down_maps[0].T))
    up = exchanged([after(block, down[1]) for block in slices(adapter_up_maps[0])])
    ids = token_adapter_index.astype(jnp.bfloat16).reshape(1, tok)
    rows = swap(after(outgoing_rows(hidden, ids, members), *down[1:], *up[1:]))
    down_near, down_far = rings(down, second_after=up[1:])
    up_near, up_far = rings(up, near_after=[down_near[-1], rows], far_after=[down_far[-1]])

    down_maps = [m for pair in zip(down_near, down_far) for m in pair]
    up_maps = [m for pair in zip(up_near, up_far) for m in pair]
    packed, id_columns = down_product(labels, rows, down_maps, rank)
    shrunk = swap(summed_copies(swap(packed)))
    return place([swap(up_product(labels, id_columns, shrunk, up_maps, rank))])


def solution(mesh):
    groups, wide = mesh.shape["groups"], mesh.shape["wide"]
    outer = 1 << ((wide.bit_length() - 1) // 2)
    fine = Mesh(mesh.devices.reshape(groups, outer, wide // outer), ("groups", "outer", "inner"))
    owner = ("outer", "inner")
    rows = P(("groups",) + owner, None)
    return jax.shard_map(
        per_device,
        mesh=fine,
        in_specs=(rows, rows, P(owner, None, None), P(owner, None, None)),
        out_specs=rows,
        check_vma=False,
    )
```

```python
import functools

import jax
import jax.numpy as jnp
from jax import lax
from jax.experimental import pallas as pl
from jax.experimental.pallas import tpu as pltpu
from jax.sharding import Mesh
from jax.sharding import PartitionSpec as P

adapter_scale = 2.0
PLANE = ("groups", "inner")
LANES = 128
ID_ROWS = 8
BLOCK = 8
IN_VMEM = pl.BlockSpec(memory_space=pltpu.VMEM)
IN_SMEM = pl.BlockSpec(memory_space=pltpu.SMEM)
IN_HBM = pl.BlockSpec(memory_space=pltpu.HBM)
ANYWHERE = pl.BlockSpec(memory_space=pl.ANY)


def params(scratch_bytes=0):
    return pltpu.CompilerParams(vmem_limit_bytes=(12 << 20) + 2 * scratch_bytes)


def to_partner(value, axes, size, offset):
    return lax.ppermute(value, axes, [(i, i ^ offset) for i in range(size)])


def next_on_ring(block, outer):
    return lax.ppermute(block, "outer", [(i, (i + 1) % outer) for i in range(outer)])


def after(value, *earlier):
    return lax.optimization_barrier((value,) + earlier)[0]


def swap(value):
    return lax.all_to_all(value, PLANE, split_axis=0, concat_axis=0, tiled=True)


def tile_labels(labels_ref, tile, rank, shape):
    per_tile = LANES // rank
    lane = lax.broadcasted_iota(jnp.int32, shape, 1)
    label = jnp.full(shape, labels_ref[tile * per_tile], jnp.int32)
    for n in range(1, per_tile):
        label = jnp.where(lane >= n * rank, labels_ref[tile * per_tile + n], label)
    return label.astype(jnp.float32)


def outgoing_kernel(hidden_ref, ids_ref, out_ref):
    members, rows, share = out_ref.shape
    tok = rows - ID_ROWS
    for member in range(members):
        out_ref[member, :tok, :] = hidden_ref[:, member * share : (member + 1) * share]
        out_ref[member, tok:, :] = ids_ref[...]


def outgoing_rows(hidden, ids, members):
    tok, width = hidden.shape
    share = width // members
    ids = jnp.broadcast_to(jnp.pad(ids, ((0, 0), (0, share - tok))), (ID_ROWS, share))
    return pl.pallas_call(
        outgoing_kernel,
        out_shape=jax.ShapeDtypeStruct((members, tok + ID_ROWS, share), jnp.bfloat16),
        in_specs=[IN_VMEM, IN_VMEM],
        out_specs=IN_VMEM,
        compiler_params=params(),
        name="outgoing_rows",
    )(hidden, ids)


def down_kernel(map_count, rank, labels_ref, rows_ref, *refs):
    maps, (packed_ref, ids_out, total_ref, ids_ref, sem) = refs[:map_count], refs[map_count:]
    members, rows, share = rows_ref.shape
    tok = rows - ID_ROWS
    block = min(BLOCK, members)
    half = tok // 2
    lane = lax.broadcasted_iota(jnp.int32, (half, LANES), 1)

    def one(step, _):
        first = step * block
        for n in range(block):
            row = rows_ref[first + n, tok : tok + 1, :LANES].astype(jnp.float32)
            ids_ref[first + n] = jnp.broadcast_to(row, (LANES, tok)).T
        tokens = rows_ref[pl.ds(first, block), :tok, :].reshape(block * tok, share)
        here = pl.ds(first, block)
        kept = pltpu.make_async_copy(ids_ref.at[here], ids_out.at[here], sem)
        kept.start()
        ids = ids_ref[here].reshape(block * tok, LANES)
        tile = 0
        for at in range(0, map_count, 2):
            some = jnp.concatenate([m[...] for m in maps[at : at + 2]], axis=0)
            product = lax.dot_general(
                tokens, some, (((1,), (1,)), ((), ())), preferred_element_type=jnp.float32
            )
            total = jnp.zeros((block * tok, LANES), jnp.float32) if tile == 0 else total_ref[...]
            for n in range(some.shape[0] // LANES):
                named = ids == tile_labels(labels_ref, tile, rank, (1, LANES))
                total += jnp.where(named, product[:, n * LANES : (n + 1) * LANES], 0.0)
                tile += 1
            total_ref[...] = total
        for n in range(block):
            total = total_ref[n * tok : (n + 1) * tok, :]
            total += pltpu.roll(total, LANES // 2, 1)
            packed_ref[first + n] = jnp.where(lane < rank, total[:half], total[half:])
        kept.wait()
        return 0

    lax.fori_loop(0, members // block, one, 0)


def down_product(labels, rows, maps, rank):
    members, tok, share = rows.shape
    tok -= ID_ROWS
    map_rows = sum(m.shape[0] for m in maps)
    return pl.pallas_call(
        functools.partial(down_kernel, len(maps), rank),
        out_shape=[
            jax.ShapeDtypeStruct((members, tok // 2, LANES), jnp.float32),
            jax.ShapeDtypeStruct((members, tok, LANES), jnp.float32),
        ],
        in_specs=[IN_SMEM, IN_VMEM] + [IN_VMEM] * len(maps),
        out_specs=[IN_VMEM, IN_HBM],
        scratch_shapes=[
            pltpu.VMEM((min(BLOCK, members) * tok, LANES), jnp.float32),
            pltpu.VMEM((members, tok, LANES), jnp.float32),
            pltpu.SemaphoreType.DMA,
        ],
        compiler_params=params(8 * members * tok * LANES),
        cost_estimate=pl.CostEstimate(
            flops=2 * map_rows * members * tok * share,
            bytes_accessed=2 * share * (map_rows + members * tok),
            transcendentals=0,
        ),
        name="down_product",
    )(labels, rows, *maps)


def copies_kernel(terms_ref, out_ref):
    own = jnp.sum(terms_ref[...], axis=0).astype(jnp.bfloat16)
    for member in range(out_ref.shape[0]):
        out_ref[member] = own


def summed_copies(terms):
    return pl.pallas_call(
        copies_kernel,
        out_shape=jax.ShapeDtypeStruct(terms.shape, jnp.bfloat16),
        in_specs=[IN_VMEM],
        out_specs=IN_VMEM,
        compiler_params=params(),
        name="summed_copies",
    )(terms)


def up_kernel(map_count, rank, labels_ref, ids_ref, shrunk_ref, *refs):
    maps, (out_ref, spread_ref, ids_buf, sem) = refs[:map_count], refs[map_count:]
    kept = pltpu.make_async_copy(ids_ref, ids_buf, sem)
    kept.start()
    members, half, _ = shrunk_ref.shape
    tok = 2 * half
    block = min(BLOCK, members)
    tiles = spread_ref.shape[1] // LANES
    lane = lax.broadcasted_iota(jnp.int32, (half, LANES), 1)
    held = jnp.concatenate([m[...] for m in maps], axis=0)
    kept.wait()

    def one(step, _):
        first = step * block
        for n in range(block):
            packed = shrunk_ref[first + n].astype(jnp.float32)
            turned = pltpu.roll(packed, LANES // 2, 1)
            shrunk = jnp.concatenate(
                [jnp.where(lane < rank, packed, turned), jnp.where(lane < rank, turned, packed)], axis=0
            )
            ids = ids_buf[first + n]
            for tile in range(tiles):
                named = ids == tile_labels(labels_ref, tile, rank, (1, LANES))
                spread_ref[n * tok : (n + 1) * tok, tile * LANES : (tile + 1) * LANES] = jnp.where(
                    named, shrunk, 0.0
                ).astype(jnp.bfloat16)
        product = jnp.dot(spread_ref[...], held, preferred_element_type=jnp.float32)
        product = (adapter_scale * product).astype(jnp.bfloat16)
        out_ref[pl.ds(first, block)] = product.reshape(block, tok, product.shape[1])
        return 0

    lax.fori_loop(0, members // block, one, 0)


def up_product(labels, ids, shrunk, maps, rank):
    members, tok, _ = ids.shape
    map_rows, piece = sum(m.shape[0] for m in maps), maps[0].shape[1]
    return pl.pallas_call(
        functools.partial(up_kernel, len(maps), rank),
        out_shape=jax.ShapeDtypeStruct((members, tok, piece), jnp.bfloat16),
        in_specs=[IN_SMEM, IN_HBM, IN_VMEM] + [IN_VMEM] * len(maps),
        out_specs=IN_VMEM,
        scratch_shapes=[
            pltpu.VMEM((min(BLOCK, members) * tok, map_rows), jnp.bfloat16),
            pltpu.VMEM((members, tok, LANES), jnp.float32),
            pltpu.SemaphoreType.DMA,
        ],
        compiler_params=params(2 * min(BLOCK, members) * tok * map_rows + 4 * members * tok * LANES),
        cost_estimate=pl.CostEstimate(
            flops=2 * map_rows * members * tok * piece,
            bytes_accessed=2 * piece * (map_rows + members * tok),
            transcendentals=0,
        ),
        name="up_product",
    )(labels, ids, shrunk, *maps)


def place_kernel(pieces, *refs):
    parts, out_ref, sems = refs[:pieces], refs[-2], refs[-1]
    members, _, piece = parts[0].shape
    copies = []
    for n in range(members * pieces):
        member, part = n // pieces, n % pieces
        target = out_ref.at[:, pl.ds(n * piece, piece)]
        copies.append(pltpu.make_async_copy(parts[part].at[member], target, sems.at[n]))
    for copy in copies:
        copy.start()
    for copy in copies:
        copy.wait()


def place(parts):
    members, tok, piece = parts[0].shape
    return pl.pallas_call(
        functools.partial(place_kernel, len(parts)),
        out_shape=jax.ShapeDtypeStruct((tok, members * len(parts) * piece), jnp.bfloat16),
        in_specs=[ANYWHERE] * len(parts),
        out_specs=ANYWHERE,
        scratch_shapes=[pltpu.SemaphoreType.DMA((members * len(parts),))],
        compiler_params=params(),
        name="place_results",
    )(*parts)


def per_device(token_adapter_index, hidden, adapter_down_maps, adapter_up_maps):
    tok, width = hidden.shape
    groups, outer, inner = (lax.axis_size(a) for a in ("groups", "outer", "inner"))
    group, level, place_in_group = (lax.axis_index(a) for a in ("groups", "outer", "inner"))
    members = groups * inner
    share = width // members
    rank = adapter_up_maps.shape[1]
    me = group * inner + place_in_group

    def slices(array):
        return [
            lax.dynamic_slice_in_dim(array, (me ^ offset) * share, share, axis=1) for offset in range(inner)
        ]

    def exchanged(blocks):
        return blocks[:1] + [to_partner(blocks[n], "inner", inner, n) for n in range(1, inner)]

    def rings(blocks, near_after=(), far_after=(), second_after=()):
        near = [after(jnp.concatenate(blocks[: inner // 2], axis=0), *near_after)]
        far = [after(jnp.concatenate(blocks[inner // 2 :], axis=0), *far_after)]
        for step in range(1, outer):
            near.append(next_on_ring(after(near[-1], *second_after) if step == 2 else near[-1], outer))
            far.append(next_on_ring(far[-1], outer))
        return near, far

    steps_back = jnp.arange(outer, dtype=jnp.int32)[:, None]
    labels = ((level - steps_back + outer) % outer) * inner + (
        place_in_group ^ jnp.arange(inner, dtype=jnp.int32)[None, :]
    )
    labels = labels.reshape(-1)

    down = exchanged(slices(adapter_down_maps[0].T))
    up = exchanged([after(block, down[1]) for block in slices(adapter_up_maps[0])])
    down_near, down_far = rings(down, second_after=up[1:])
    ids = token_adapter_index.astype(jnp.bfloat16).reshape(1, tok)
    rows = swap(after(outgoing_rows(hidden, ids, members), *up[1:], down_near[1], down_far[1]))

    down_maps = [m for pair in zip(down_near, down_far) for m in pair]
    packed, id_columns = down_product(labels, rows, down_maps, rank)
    up_near, up_far = rings(up, [down_near[-1]], [down_far[-1]], second_after=[packed])
    up_maps = [m for pair in zip(up_near, up_far) for m in pair]
    shrunk = swap(summed_copies(swap(packed)))
    return place([swap(up_product(labels, id_columns, shrunk, up_maps, rank))])


def solution(mesh):
    groups, wide = mesh.shape["groups"], mesh.shape["wide"]
    outer = 1 << ((wide.bit_length() - 1) // 2)
    fine = Mesh(mesh.devices.reshape(groups, outer, wide // outer), ("groups", "outer", "inner"))
    owner = ("outer", "inner")
    rows = P(("groups",) + owner, None)
    return jax.shard_map(
        per_device,
        mesh=fine,
        in_specs=(rows, rows, P(owner, None, None), P(owner, None, None)),
        out_specs=rows,
        check_vma=False,
    )
```

```python
import functools

import jax
import jax.numpy as jnp
from jax import lax
from jax.experimental import pallas as pl
from jax.experimental.pallas import tpu as pltpu
from jax.sharding import Mesh
from jax.sharding import PartitionSpec as P

adapter_scale = 2.0
PLANE = ("groups", "inner")
LANES = 128
ID_ROWS = 8
BLOCK = 8
IN_VMEM = pl.BlockSpec(memory_space=pltpu.VMEM)
IN_SMEM = pl.BlockSpec(memory_space=pltpu.SMEM)
IN_HBM = pl.BlockSpec(memory_space=pltpu.HBM)
ANYWHERE = pl.BlockSpec(memory_space=pl.ANY)


def params(scratch_bytes=0):
    return pltpu.CompilerParams(vmem_limit_bytes=(12 << 20) + 2 * scratch_bytes)


def to_partner(value, axes, size, offset):
    return lax.ppermute(value, axes, [(i, i ^ offset) for i in range(size)])


def next_on_ring(block, outer):
    return lax.ppermute(block, "outer", [(i, (i + 1) % outer) for i in range(outer)])


def after(value, *earlier):
    return lax.optimization_barrier((value,) + earlier)[0]


def swap(value):
    return lax.all_to_all(value, PLANE, split_axis=0, concat_axis=0, tiled=True)


def load_maps(maps, map_buf, sems):
    rows = maps[0].shape[0]
    copies = [
        pltpu.make_async_copy(m, map_buf.at[pl.ds(n * rows, rows)], sems.at[n]) for n, m in enumerate(maps)
    ]
    for copy in copies:
        copy.start()
    return copies


def tile_labels(labels_ref, tile, rank, shape):
    per_tile = LANES // rank
    lane = lax.broadcasted_iota(jnp.int32, shape, 1)
    label = jnp.full(shape, labels_ref[tile * per_tile], jnp.int32)
    for n in range(1, per_tile):
        label = jnp.where(lane >= n * rank, labels_ref[tile * per_tile + n], label)
    return label.astype(jnp.float32)


def outgoing_kernel(hidden_ref, ids_ref, out_ref):
    members, rows, share = out_ref.shape
    tok = rows - ID_ROWS
    for member in range(members):
        out_ref[member, :tok, :] = hidden_ref[:, member * share : (member + 1) * share]
        out_ref[member, tok:, :] = ids_ref[...]


def outgoing_rows(hidden, ids, members):
    tok, width = hidden.shape
    share = width // members
    ids = jnp.broadcast_to(jnp.pad(ids, ((0, 0), (0, share - tok))), (ID_ROWS, share))
    return pl.pallas_call(
        outgoing_kernel,
        out_shape=jax.ShapeDtypeStruct((members, tok + ID_ROWS, share), jnp.bfloat16),
        in_specs=[IN_VMEM, IN_VMEM],
        out_specs=IN_VMEM,
        compiler_params=params(),
        name="outgoing_rows",
    )(hidden, ids)


def down_kernel(map_count, rank, labels_ref, rows_ref, *refs):
    maps, (packed_ref, ids_out, total_ref, ids_ref, map_buf, sem, map_sems) = refs[:map_count], refs[map_count:]
    copies = load_maps(maps, map_buf, map_sems)
    map_rows = maps[0].shape[0]
    members, rows, share = rows_ref.shape
    tok = rows - ID_ROWS
    block = min(BLOCK, members)
    half = tok // 2
    lane = lax.broadcasted_iota(jnp.int32, (half, LANES), 1)

    def one(step, _):
        first = step * block
        for n in range(block):
            row = rows_ref[first + n, tok : tok + 1, :LANES].astype(jnp.float32)
            ids_ref[first + n] = jnp.broadcast_to(row, (LANES, tok)).T
        tokens = rows_ref[pl.ds(first, block), :tok, :].reshape(block * tok, share)
        here = pl.ds(first, block)
        kept = pltpu.make_async_copy(ids_ref.at[here], ids_out.at[here], sem)
        kept.start()
        ids = ids_ref[here].reshape(block * tok, LANES)
        tile = 0
        for at in range(0, map_count, 2):

            @pl.when(step == 0)
            def _():
                for copy in copies[at : at + 2]:
                    copy.wait()

            some = map_buf[at * map_rows : (at + 2) * map_rows, :]
            product = lax.dot_general(
                tokens, some, (((1,), (1,)), ((), ())), preferred_element_type=jnp.float32
            )
            total = jnp.zeros((block * tok, LANES), jnp.float32) if tile == 0 else total_ref[...]
            for n in range(some.shape[0] // LANES):
                named = ids == tile_labels(labels_ref, tile, rank, (1, LANES))
                total += jnp.where(named, product[:, n * LANES : (n + 1) * LANES], 0.0)
                tile += 1
            total_ref[...] = total
        for n in range(block):
            total = total_ref[n * tok : (n + 1) * tok, :]
            total += pltpu.roll(total, LANES // 2, 1)
            packed_ref[first + n] = jnp.where(lane < rank, total[:half], total[half:])
        kept.wait()
        return 0

    lax.fori_loop(0, members // block, one, 0)


def down_product(labels, rows, maps, rank):
    members, tok, share = rows.shape
    tok -= ID_ROWS
    map_rows = sum(m.shape[0] for m in maps)
    return pl.pallas_call(
        functools.partial(down_kernel, len(maps), rank),
        out_shape=[
            jax.ShapeDtypeStruct((members, tok // 2, LANES), jnp.float32),
            jax.ShapeDtypeStruct((members, tok, LANES), jnp.float32),
        ],
        in_specs=[IN_SMEM, IN_VMEM] + [IN_HBM] * len(maps),
        out_specs=[IN_VMEM, IN_HBM],
        scratch_shapes=[
            pltpu.VMEM((min(BLOCK, members) * tok, LANES), jnp.float32),
            pltpu.VMEM((members, tok, LANES), jnp.float32),
            pltpu.VMEM((map_rows, maps[0].shape[1]), jnp.bfloat16),
            pltpu.SemaphoreType.DMA,
            pltpu.SemaphoreType.DMA((len(maps),)),
        ],
        compiler_params=params(8 * members * tok * LANES + 2 * map_rows * share),
        cost_estimate=pl.CostEstimate(
            flops=2 * map_rows * members * tok * share,
            bytes_accessed=2 * share * (map_rows + members * tok),
            transcendentals=0,
        ),
        name="down_product",
    )(labels, rows, *maps)


def copies_kernel(terms_ref, out_ref):
    own = jnp.sum(terms_ref[...], axis=0).astype(jnp.bfloat16)
    for member in range(out_ref.shape[0]):
        out_ref[member] = own


def summed_copies(terms):
    return pl.pallas_call(
        copies_kernel,
        out_shape=jax.ShapeDtypeStruct(terms.shape, jnp.bfloat16),
        in_specs=[IN_VMEM],
        out_specs=IN_VMEM,
        compiler_params=params(),
        name="summed_copies",
    )(terms)


def up_kernel(map_count, rank, labels_ref, ids_ref, shrunk_ref, *refs):
    maps, (out_ref, spread_ref, ids_buf, map_buf, sem, map_sems) = refs[:map_count], refs[map_count:]
    copies = load_maps(maps, map_buf, map_sems)
    kept = pltpu.make_async_copy(ids_ref, ids_buf, sem)
    kept.start()
    members, half, _ = shrunk_ref.shape
    tok = 2 * half
    block = min(BLOCK, members)
    tiles = spread_ref.shape[1] // LANES
    lane = lax.broadcasted_iota(jnp.int32, (half, LANES), 1)
    kept.wait()

    def one(step, _):
        first = step * block
        for n in range(block):
            packed = shrunk_ref[first + n].astype(jnp.float32)
            turned = pltpu.roll(packed, LANES // 2, 1)
            shrunk = jnp.concatenate(
                [jnp.where(lane < rank, packed, turned), jnp.where(lane < rank, turned, packed)], axis=0
            )
            ids = ids_buf[first + n]
            for tile in range(tiles):
                named = ids == tile_labels(labels_ref, tile, rank, (1, LANES))
                spread_ref[n * tok : (n + 1) * tok, tile * LANES : (tile + 1) * LANES] = jnp.where(
                    named, shrunk, 0.0
                ).astype(jnp.bfloat16)

        @pl.when(step == 0)
        def _():
            for copy in copies:
                copy.wait()

        product = jnp.dot(spread_ref[...], map_buf[...], preferred_element_type=jnp.float32)
        product = (adapter_scale * product).astype(jnp.bfloat16)
        out_ref[pl.ds(first, block)] = product.reshape(block, tok, product.shape[1])
        return 0

    lax.fori_loop(0, members // block, one, 0)


def up_product(labels, ids, shrunk, maps, rank):
    members, tok, _ = ids.shape
    map_rows, piece = sum(m.shape[0] for m in maps), maps[0].shape[1]
    return pl.pallas_call(
        functools.partial(up_kernel, len(maps), rank),
        out_shape=jax.ShapeDtypeStruct((members, tok, piece), jnp.bfloat16),
        in_specs=[IN_SMEM, IN_HBM, IN_VMEM] + [IN_HBM] * len(maps),
        out_specs=IN_VMEM,
        scratch_shapes=[
            pltpu.VMEM((min(BLOCK, members) * tok, map_rows), jnp.bfloat16),
            pltpu.VMEM((members, tok, LANES), jnp.float32),
            pltpu.VMEM((map_rows, maps[0].shape[1]), jnp.bfloat16),
            pltpu.SemaphoreType.DMA,
            pltpu.SemaphoreType.DMA((len(maps),)),
        ],
        compiler_params=params(2 * min(BLOCK, members) * tok * map_rows + 4 * members * tok * LANES + 2 * map_rows * piece),
        cost_estimate=pl.CostEstimate(
            flops=2 * map_rows * members * tok * piece,
            bytes_accessed=2 * piece * (map_rows + members * tok),
            transcendentals=0,
        ),
        name="up_product",
    )(labels, ids, shrunk, *maps)


def place_kernel(pieces, *refs):
    parts, out_ref, sems = refs[:pieces], refs[-2], refs[-1]
    members, _, piece = parts[0].shape
    copies = []
    for n in range(members * pieces):
        member, part = n // pieces, n % pieces
        target = out_ref.at[:, pl.ds(n * piece, piece)]
        copies.append(pltpu.make_async_copy(parts[part].at[member], target, sems.at[n]))
    for copy in copies:
        copy.start()
    for copy in copies:
        copy.wait()


def place(parts):
    members, tok, piece = parts[0].shape
    return pl.pallas_call(
        functools.partial(place_kernel, len(parts)),
        out_shape=jax.ShapeDtypeStruct((tok, members * len(parts) * piece), jnp.bfloat16),
        in_specs=[ANYWHERE] * len(parts),
        out_specs=ANYWHERE,
        scratch_shapes=[pltpu.SemaphoreType.DMA((members * len(parts),))],
        compiler_params=params(),
        name="place_results",
    )(*parts)


def per_device(token_adapter_index, hidden, adapter_down_maps, adapter_up_maps):
    tok, width = hidden.shape
    groups, outer, inner = (lax.axis_size(a) for a in ("groups", "outer", "inner"))
    group, level, place_in_group = (lax.axis_index(a) for a in ("groups", "outer", "inner"))
    members = groups * inner
    share = width // members
    rank = adapter_up_maps.shape[1]
    me = group * inner + place_in_group

    def slices(offset):
        start = (me ^ offset) * share
        return jnp.concatenate(
            [
                lax.dynamic_slice_in_dim(adapter_down_maps[0].T, start, share, axis=1),
                lax.dynamic_slice_in_dim(adapter_up_maps[0], start, share, axis=1),
            ],
            axis=0,
        )

    got = [slices(0)] + [to_partner(slices(n), "inner", inner, n) for n in range(1, inner)]

    def rings(blocks, near_after=(), far_after=(), second_after=()):
        near = [after(jnp.concatenate(blocks[: inner // 2], axis=0), *near_after)]
        far = [after(jnp.concatenate(blocks[inner // 2 :], axis=0), *far_after)]
        for step in range(1, outer):
            near.append(next_on_ring(after(near[-1], *second_after) if step == 2 else near[-1], outer))
            far.append(next_on_ring(far[-1], outer))
        return near, far

    steps_back = jnp.arange(outer, dtype=jnp.int32)[:, None]
    labels = ((level - steps_back + outer) % outer) * inner + (
        place_in_group ^ jnp.arange(inner, dtype=jnp.int32)[None, :]
    )
    labels = labels.reshape(-1)

    down_near, down_far = rings([g[:rank] for g in got])
    ids = token_adapter_index.astype(jnp.bfloat16).reshape(1, tok)
    rows = swap(after(outgoing_rows(hidden, ids, members), *got[1:], down_near[1]))

    down_maps = [m for pair in zip(down_near, down_far) for m in pair]
    packed, id_columns = down_product(labels, rows, down_maps, rank)
    up_near, up_far = rings([g[rank:] for g in got], [down_near[-1]], [down_far[-1]], second_after=[packed])
    up_maps = [m for pair in zip(up_near, up_far) for m in pair]
    shrunk = swap(summed_copies(swap(packed)))
    return place([swap(up_product(labels, id_columns, shrunk, up_maps, rank))])


def solution(mesh):
    groups, wide = mesh.shape["groups"], mesh.shape["wide"]
    outer = 1 << ((wide.bit_length() - 1) // 2)
    fine = Mesh(mesh.devices.reshape(groups, outer, wide // outer), ("groups", "outer", "inner"))
    owner = ("outer", "inner")
    rows = P(("groups",) + owner, None)
    return jax.shard_map(
        per_device,
        mesh=fine,
        in_specs=(rows, rows, P(owner, None, None), P(owner, None, None)),
        out_specs=rows,
        check_vma=False,
    )
```

```python
import functools

import jax
import jax.numpy as jnp
from jax import lax
from jax.experimental import pallas as pl
from jax.experimental.pallas import tpu as pltpu
from jax.sharding import Mesh
from jax.sharding import PartitionSpec as P

adapter_scale = 2.0
PLANE = ("groups", "inner")
LANES = 128
ID_ROWS = 8
BLOCK = 8
IN_VMEM = pl.BlockSpec(memory_space=pltpu.VMEM)
IN_SMEM = pl.BlockSpec(memory_space=pltpu.SMEM)
IN_HBM = pl.BlockSpec(memory_space=pltpu.HBM)
ANYWHERE = pl.BlockSpec(memory_space=pl.ANY)


def params(scratch_bytes=0):
    return pltpu.CompilerParams(vmem_limit_bytes=(12 << 20) + 2 * scratch_bytes)


def to_partner(value, axes, size, offset):
    return lax.ppermute(value, axes, [(i, i ^ offset) for i in range(size)])


def next_on_ring(block, outer):
    return lax.ppermute(block, "outer", [(i, (i + 1) % outer) for i in range(outer)])


def after(value, *earlier):
    return lax.optimization_barrier((value,) + earlier)[0]


def swap(value):
    return lax.all_to_all(value, PLANE, split_axis=0, concat_axis=0, tiled=True)


def tile_labels(labels_ref, tile, rank, shape):
    per_tile = LANES // rank
    lane = lax.broadcasted_iota(jnp.int32, shape, 1)
    label = jnp.full(shape, labels_ref[tile * per_tile], jnp.int32)
    for n in range(1, per_tile):
        label = jnp.where(lane >= n * rank, labels_ref[tile * per_tile + n], label)
    return label.astype(jnp.float32)


def outgoing_kernel(hidden_ref, ids_ref, out_ref):
    members, rows, share = out_ref.shape
    tok = rows - ID_ROWS
    for member in range(members):
        out_ref[member, :tok, :] = hidden_ref[:, member * share : (member + 1) * share]
        out_ref[member, tok:, :] = ids_ref[...]


def outgoing_rows(hidden, ids, members):
    tok, width = hidden.shape
    share = width // members
    ids = jnp.broadcast_to(jnp.pad(ids, ((0, 0), (0, share - tok))), (ID_ROWS, share))
    return pl.pallas_call(
        outgoing_kernel,
        out_shape=jax.ShapeDtypeStruct((members, tok + ID_ROWS, share), jnp.bfloat16),
        in_specs=[IN_VMEM, IN_VMEM],
        out_specs=IN_VMEM,
        compiler_params=params(),
        name="outgoing_rows",
    )(hidden, ids)


def down_kernel(map_count, rank, labels_ref, rows_ref, *refs):
    maps, (packed_ref, ids_out, total_ref, ids_ref, sem) = refs[:map_count], refs[map_count:]
    members, rows, share = rows_ref.shape
    tok = rows - ID_ROWS
    block = min(BLOCK, members)
    half = tok // 2
    lane = lax.broadcasted_iota(jnp.int32, (half, LANES), 1)

    def one(step, _):
        first = step * block
        for n in range(block):
            row = rows_ref[first + n, tok : tok + 1, :LANES].astype(jnp.float32)
            ids_ref[first + n] = jnp.broadcast_to(row, (LANES, tok)).T
        tokens = rows_ref[pl.ds(first, block), :tok, :].reshape(block * tok, share)
        here = pl.ds(first, block)
        kept = pltpu.make_async_copy(ids_ref.at[here], ids_out.at[here], sem)
        kept.start()
        ids = ids_ref[here].reshape(block * tok, LANES)
        tile = 0
        for at in range(0, map_count, 2):
            some = jnp.concatenate([m[...] for m in maps[at : at + 2]], axis=0)
            product = lax.dot_general(
                tokens, some, (((1,), (1,)), ((), ())), preferred_element_type=jnp.float32
            )
            total = jnp.zeros((block * tok, LANES), jnp.float32) if tile == 0 else total_ref[...]
            for n in range(some.shape[0] // LANES):
                named = ids == tile_labels(labels_ref, tile, rank, (1, LANES))
                total += jnp.where(named, product[:, n * LANES : (n + 1) * LANES], 0.0)
                tile += 1
            total_ref[...] = total
        for n in range(block):
            total = total_ref[n * tok : (n + 1) * tok, :]
            total += pltpu.roll(total, LANES // 2, 1)
            packed_ref[first + n] = jnp.where(lane < rank, total[:half], total[half:])
        kept.wait()
        return 0

    lax.fori_loop(0, members // block, one, 0)


def down_product(labels, rows, maps, rank):
    members, tok, share = rows.shape
    tok -= ID_ROWS
    map_rows = sum(m.shape[0] for m in maps)
    return pl.pallas_call(
        functools.partial(down_kernel, len(maps), rank),
        out_shape=[
            jax.ShapeDtypeStruct((members, tok // 2, LANES), jnp.float32),
            jax.ShapeDtypeStruct((members, tok, LANES), jnp.float32),
        ],
        in_specs=[IN_SMEM, IN_VMEM] + [IN_VMEM] * len(maps),
        out_specs=[IN_VMEM, IN_HBM],
        scratch_shapes=[
            pltpu.VMEM((min(BLOCK, members) * tok, LANES), jnp.float32),
            pltpu.VMEM((members, tok, LANES), jnp.float32),
            pltpu.SemaphoreType.DMA,
        ],
        compiler_params=params(8 * members * tok * LANES),
        cost_estimate=pl.CostEstimate(
            flops=2 * map_rows * members * tok * share,
            bytes_accessed=2 * share * (map_rows + members * tok),
            transcendentals=0,
        ),
        name="down_product",
    )(labels, rows, *maps)


def copies_kernel(terms_ref, out_ref):
    own = jnp.sum(terms_ref[...], axis=0).astype(jnp.bfloat16)
    for member in range(out_ref.shape[0]):
        out_ref[member] = own


def summed_copies(terms):
    return pl.pallas_call(
        copies_kernel,
        out_shape=jax.ShapeDtypeStruct(terms.shape, jnp.bfloat16),
        in_specs=[IN_VMEM],
        out_specs=IN_VMEM,
        compiler_params=params(),
        name="summed_copies",
    )(terms)


def up_kernel(map_count, rank, labels_ref, ids_ref, shrunk_ref, *refs):
    maps, (out_ref, spread_ref, ids_buf, sem) = refs[:map_count], refs[map_count:]
    kept = pltpu.make_async_copy(ids_ref, ids_buf, sem)
    kept.start()
    members, half, _ = shrunk_ref.shape
    tok = 2 * half
    block = min(BLOCK, members)
    tiles = spread_ref.shape[1] // LANES
    lane = lax.broadcasted_iota(jnp.int32, (half, LANES), 1)
    held = jnp.concatenate([m[...] for m in maps], axis=0)
    kept.wait()

    def one(step, _):
        first = step * block
        for n in range(block):
            packed = shrunk_ref[first + n].astype(jnp.float32)
            turned = pltpu.roll(packed, LANES // 2, 1)
            shrunk = jnp.concatenate(
                [jnp.where(lane < rank, packed, turned), jnp.where(lane < rank, turned, packed)], axis=0
            )
            ids = ids_buf[first + n]
            for tile in range(tiles):
                named = ids == tile_labels(labels_ref, tile, rank, (1, LANES))
                spread_ref[n * tok : (n + 1) * tok, tile * LANES : (tile + 1) * LANES] = jnp.where(
                    named, shrunk, 0.0
                ).astype(jnp.bfloat16)
        product = jnp.dot(spread_ref[...], held, preferred_element_type=jnp.float32)
        product = (adapter_scale * product).astype(jnp.bfloat16)
        out_ref[pl.ds(first, block)] = product.reshape(block, tok, product.shape[1])
        return 0

    lax.fori_loop(0, members // block, one, 0)


def up_product(labels, ids, shrunk, maps, rank):
    members, tok, _ = ids.shape
    map_rows, piece = sum(m.shape[0] for m in maps), maps[0].shape[1]
    return pl.pallas_call(
        functools.partial(up_kernel, len(maps), rank),
        out_shape=jax.ShapeDtypeStruct((members, tok, piece), jnp.bfloat16),
        in_specs=[IN_SMEM, IN_HBM, IN_VMEM] + [IN_VMEM] * len(maps),
        out_specs=IN_VMEM,
        scratch_shapes=[
            pltpu.VMEM((min(BLOCK, members) * tok, map_rows), jnp.bfloat16),
            pltpu.VMEM((members, tok, LANES), jnp.float32),
            pltpu.SemaphoreType.DMA,
        ],
        compiler_params=params(2 * min(BLOCK, members) * tok * map_rows + 4 * members * tok * LANES),
        cost_estimate=pl.CostEstimate(
            flops=2 * map_rows * members * tok * piece,
            bytes_accessed=2 * piece * (map_rows + members * tok),
            transcendentals=0,
        ),
        name="up_product",
    )(labels, ids, shrunk, *maps)


def place_kernel(pieces, *refs):
    parts, out_ref, sems = refs[:pieces], refs[-2], refs[-1]
    members, _, piece = parts[0].shape
    copies = []
    for n in range(members * pieces):
        member, part = n // pieces, n % pieces
        target = out_ref.at[:, pl.ds(n * piece, piece)]
        copies.append(pltpu.make_async_copy(parts[part].at[member], target, sems.at[n]))
    for copy in copies:
        copy.start()
    for copy in copies:
        copy.wait()


def place(parts):
    members, tok, piece = parts[0].shape
    return pl.pallas_call(
        functools.partial(place_kernel, len(parts)),
        out_shape=jax.ShapeDtypeStruct((tok, members * len(parts) * piece), jnp.bfloat16),
        in_specs=[ANYWHERE] * len(parts),
        out_specs=ANYWHERE,
        scratch_shapes=[pltpu.SemaphoreType.DMA((members * len(parts),))],
        compiler_params=params(),
        name="place_results",
    )(*parts)


def per_device(token_adapter_index, hidden, adapter_down_maps, adapter_up_maps):
    tok, width = hidden.shape
    groups, outer, inner = (lax.axis_size(a) for a in ("groups", "outer", "inner"))
    group, level, place_in_group = (lax.axis_index(a) for a in ("groups", "outer", "inner"))
    members = groups * inner
    share = width // members
    rank = adapter_up_maps.shape[1]
    me = group * inner + place_in_group

    def slices(array):
        return [
            lax.dynamic_slice_in_dim(array, (me ^ offset) * share, share, axis=1) for offset in range(inner)
        ]

    def exchanged(blocks):
        return blocks[:1] + [to_partner(blocks[n], "inner", inner, n) for n in range(1, inner)]

    def rings(blocks, near_after=(), far_after=(), second_after=()):
        near = [after(jnp.concatenate(blocks[: inner // 2], axis=0), *near_after)]
        far = [after(jnp.concatenate(blocks[inner // 2 :], axis=0), *far_after)]
        for step in range(1, outer):
            near.append(next_on_ring(after(near[-1], *second_after) if step == 2 else near[-1], outer))
            far.append(next_on_ring(after(far[-1], near[-1]), outer))
        return near, far

    steps_back = jnp.arange(outer, dtype=jnp.int32)[:, None]
    labels = ((level - steps_back + outer) % outer) * inner + (
        place_in_group ^ jnp.arange(inner, dtype=jnp.int32)[None, :]
    )
    labels = labels.reshape(-1)

    down = exchanged(slices(adapter_down_maps[0].T))
    down_near, down_far = rings(down)
    ids = token_adapter_index.astype(jnp.bfloat16).reshape(1, tok)
    rows = swap(after(outgoing_rows(hidden, ids, members), *down[1:], down_near[1]))
    up = exchanged([after(block, down_near[1]) for block in slices(adapter_up_maps[0])])

    down_maps = [m for pair in zip(down_near, down_far) for m in pair]
    packed, id_columns = down_product(labels, rows, down_maps, rank)
    up_near, up_far = rings(up, [down_near[-1]], [down_far[-1]], second_after=[packed])
    up_maps = [m for pair in zip(up_near, up_far) for m in pair]
    shrunk = swap(summed_copies(swap(packed)))
    return place([swap(up_product(labels, id_columns, shrunk, up_maps, rank))])


def solution(mesh):
    groups, wide = mesh.shape["groups"], mesh.shape["wide"]
    outer = 1 << ((wide.bit_length() - 1) // 2)
    fine = Mesh(mesh.devices.reshape(groups, outer, wide // outer), ("groups", "outer", "inner"))
    owner = ("outer", "inner")
    rows = P(("groups",) + owner, None)
    return jax.shard_map(
        per_device,
        mesh=fine,
        in_specs=(rows, rows, P(owner, None, None), P(owner, None, None)),
        out_specs=rows,
        check_vma=False,
    )
```

```python
import functools

import jax
import jax.numpy as jnp
from jax import lax
from jax.experimental import pallas as pl
from jax.experimental.pallas import tpu as pltpu
from jax.sharding import Mesh
from jax.sharding import PartitionSpec as P

adapter_scale = 2.0
PLANE = ("groups", "inner")
LANES = 128
ID_ROWS = 8
BLOCK = 8
IN_VMEM = pl.BlockSpec(memory_space=pltpu.VMEM)
IN_SMEM = pl.BlockSpec(memory_space=pltpu.SMEM)
IN_HBM = pl.BlockSpec(memory_space=pltpu.HBM)
ANYWHERE = pl.BlockSpec(memory_space=pl.ANY)


def params(scratch_bytes=0):
    return pltpu.CompilerParams(vmem_limit_bytes=(12 << 20) + 2 * scratch_bytes)


def to_partner(value, axes, size, offset):
    return lax.ppermute(value, axes, [(i, i ^ offset) for i in range(size)])


def next_on_ring(block, outer):
    return lax.ppermute(block, "outer", [(i, (i + 1) % outer) for i in range(outer)])


def after(value, *earlier):
    return lax.optimization_barrier((value,) + earlier)[0]


def swap(value):
    return lax.all_to_all(value, PLANE, split_axis=0, concat_axis=0, tiled=True)


def tile_labels(labels_ref, tile, rank, shape):
    per_tile = LANES // rank
    lane = lax.broadcasted_iota(jnp.int32, shape, 1)
    label = jnp.full(shape, labels_ref[tile * per_tile], jnp.int32)
    for n in range(1, per_tile):
        label = jnp.where(lane >= n * rank, labels_ref[tile * per_tile + n], label)
    return label.astype(jnp.float32)


def outgoing_kernel(hidden_ref, ids_ref, out_ref, sems):
    members, rows, share = out_ref.shape
    tok = rows - ID_ROWS
    copies = [
        pltpu.make_async_copy(
            hidden_ref.at[:, pl.ds(member * share, share)], out_ref.at[member, pl.ds(0, tok)], sems.at[member]
        )
        for member in range(members)
    ]
    for copy in copies:
        copy.start()
    ids = jnp.broadcast_to(ids_ref[...].astype(jnp.float32).astype(jnp.bfloat16), (ID_ROWS, tok))
    for member in range(members):
        out_ref[member, tok:, :tok] = ids
        if share > tok:
            out_ref[member, tok:, tok:] = jnp.zeros((ID_ROWS, share - tok), jnp.bfloat16)
    for copy in copies:
        copy.wait()


def outgoing_rows(hidden, ids, members):
    tok, width = hidden.shape
    share = width // members
    return pl.pallas_call(
        outgoing_kernel,
        out_shape=jax.ShapeDtypeStruct((members, tok + ID_ROWS, share), jnp.bfloat16),
        in_specs=[IN_HBM, IN_VMEM],
        out_specs=IN_VMEM,
        scratch_shapes=[pltpu.SemaphoreType.DMA((members,))],
        compiler_params=params(),
        name="outgoing_rows",
    )(hidden, ids)


def down_kernel(map_count, rank, labels_ref, rows_ref, *refs):
    maps, (packed_ref, ids_out, total_ref, ids_ref, sem) = refs[:map_count], refs[map_count:]
    members, rows, share = rows_ref.shape
    tok = rows - ID_ROWS
    block = min(BLOCK, members)
    half = tok // 2
    lane = lax.broadcasted_iota(jnp.int32, (half, LANES), 1)

    def one(step, _):
        first = step * block
        for n in range(block):
            row = rows_ref[first + n, tok : tok + 1, :LANES].astype(jnp.float32)
            ids_ref[first + n] = jnp.broadcast_to(row, (LANES, tok)).T
        tokens = rows_ref[pl.ds(first, block), :tok, :].reshape(block * tok, share)
        here = pl.ds(first, block)
        kept = pltpu.make_async_copy(ids_ref.at[here], ids_out.at[here], sem)
        kept.start()
        ids = ids_ref[here].reshape(block * tok, LANES)
        tile = 0
        for at in range(0, map_count, 2):
            some = jnp.concatenate([m[...] for m in maps[at : at + 2]], axis=0)
            product = lax.dot_general(
                tokens, some, (((1,), (1,)), ((), ())), preferred_element_type=jnp.float32
            )
            total = jnp.zeros((block * tok, LANES), jnp.float32) if tile == 0 else total_ref[...]
            for n in range(some.shape[0] // LANES):
                named = ids == tile_labels(labels_ref, tile, rank, (1, LANES))
                total += jnp.where(named, product[:, n * LANES : (n + 1) * LANES], 0.0)
                tile += 1
            total_ref[...] = total
        for n in range(block):
            total = total_ref[n * tok : (n + 1) * tok, :]
            total += pltpu.roll(total, LANES // 2, 1)
            packed_ref[first + n] = jnp.where(lane < rank, total[:half], total[half:])
        kept.wait()
        return 0

    lax.fori_loop(0, members // block, one, 0)


def down_product(labels, rows, maps, rank):
    members, tok, share = rows.shape
    tok -= ID_ROWS
    map_rows = sum(m.shape[0] for m in maps)
    return pl.pallas_call(
        functools.partial(down_kernel, len(maps), rank),
        out_shape=[
            jax.ShapeDtypeStruct((members, tok // 2, LANES), jnp.float32),
            jax.ShapeDtypeStruct((members, tok, LANES), jnp.float32),
        ],
        in_specs=[IN_SMEM, IN_VMEM] + [IN_VMEM] * len(maps),
        out_specs=[IN_VMEM, IN_HBM],
        scratch_shapes=[
            pltpu.VMEM((min(BLOCK, members) * tok, LANES), jnp.float32),
            pltpu.VMEM((members, tok, LANES), jnp.float32),
            pltpu.SemaphoreType.DMA,
        ],
        compiler_params=params(8 * members * tok * LANES),
        cost_estimate=pl.CostEstimate(
            flops=2 * map_rows * members * tok * share,
            bytes_accessed=2 * share * (map_rows + members * tok),
            transcendentals=0,
        ),
        name="down_product",
    )(labels, rows, *maps)


def copies_kernel(terms_ref, out_ref):
    own = jnp.sum(terms_ref[...], axis=0).astype(jnp.bfloat16)
    for member in range(out_ref.shape[0]):
        out_ref[member] = own


def summed_copies(terms):
    return pl.pallas_call(
        copies_kernel,
        out_shape=jax.ShapeDtypeStruct(terms.shape, jnp.bfloat16),
        in_specs=[IN_VMEM],
        out_specs=IN_VMEM,
        compiler_params=params(),
        name="summed_copies",
    )(terms)


def up_kernel(map_count, rank, labels_ref, ids_ref, shrunk_ref, *refs):
    maps, (out_ref, spread_ref, ids_buf, sem) = refs[:map_count], refs[map_count:]
    kept = pltpu.make_async_copy(ids_ref, ids_buf, sem)
    kept.start()
    members, half, _ = shrunk_ref.shape
    tok = 2 * half
    block = min(BLOCK, members)
    tiles = spread_ref.shape[1] // LANES
    lane = lax.broadcasted_iota(jnp.int32, (half, LANES), 1)
    held = jnp.concatenate([m[...] for m in maps], axis=0)
    kept.wait()

    def one(step, _):
        first = step * block
        for n in range(block):
            packed = shrunk_ref[first + n].astype(jnp.float32)
            turned = pltpu.roll(packed, LANES // 2, 1)
            shrunk = jnp.concatenate(
                [jnp.where(lane < rank, packed, turned), jnp.where(lane < rank, turned, packed)], axis=0
            )
            ids = ids_buf[first + n]
            for tile in range(tiles):
                named = ids == tile_labels(labels_ref, tile, rank, (1, LANES))
                spread_ref[n * tok : (n + 1) * tok, tile * LANES : (tile + 1) * LANES] = jnp.where(
                    named, shrunk, 0.0
                ).astype(jnp.bfloat16)
        product = jnp.dot(spread_ref[...], held, preferred_element_type=jnp.float32)
        product = (adapter_scale * product).astype(jnp.bfloat16)
        out_ref[pl.ds(first, block)] = product.reshape(block, tok, product.shape[1])
        return 0

    lax.fori_loop(0, members // block, one, 0)


def up_product(labels, ids, shrunk, maps, rank):
    members, tok, _ = ids.shape
    map_rows, piece = sum(m.shape[0] for m in maps), maps[0].shape[1]
    return pl.pallas_call(
        functools.partial(up_kernel, len(maps), rank),
        out_shape=jax.ShapeDtypeStruct((members, tok, piece), jnp.bfloat16),
        in_specs=[IN_SMEM, IN_HBM, IN_VMEM] + [IN_VMEM] * len(maps),
        out_specs=IN_VMEM,
        scratch_shapes=[
            pltpu.VMEM((min(BLOCK, members) * tok, map_rows), jnp.bfloat16),
            pltpu.VMEM((members, tok, LANES), jnp.float32),
            pltpu.SemaphoreType.DMA,
        ],
        compiler_params=params(2 * min(BLOCK, members) * tok * map_rows + 4 * members * tok * LANES),
        cost_estimate=pl.CostEstimate(
            flops=2 * map_rows * members * tok * piece,
            bytes_accessed=2 * piece * (map_rows + members * tok),
            transcendentals=0,
        ),
        name="up_product",
    )(labels, ids, shrunk, *maps)


def place_kernel(pieces, *refs):
    parts, out_ref, sems = refs[:pieces], refs[-2], refs[-1]
    members, _, piece = parts[0].shape
    copies = []
    for n in range(members * pieces):
        member, part = n // pieces, n % pieces
        target = out_ref.at[:, pl.ds(n * piece, piece)]
        copies.append(pltpu.make_async_copy(parts[part].at[member], target, sems.at[n]))
    for copy in copies:
        copy.start()
    for copy in copies:
        copy.wait()


def place(parts):
    members, tok, piece = parts[0].shape
    return pl.pallas_call(
        functools.partial(place_kernel, len(parts)),
        out_shape=jax.ShapeDtypeStruct((tok, members * len(parts) * piece), jnp.bfloat16),
        in_specs=[ANYWHERE] * len(parts),
        out_specs=ANYWHERE,
        scratch_shapes=[pltpu.SemaphoreType.DMA((members * len(parts),))],
        compiler_params=params(),
        name="place_results",
    )(*parts)


def per_device(token_adapter_index, hidden, adapter_down_maps, adapter_up_maps):
    tok, width = hidden.shape
    groups, outer, inner = (lax.axis_size(a) for a in ("groups", "outer", "inner"))
    group, level, place_in_group = (lax.axis_index(a) for a in ("groups", "outer", "inner"))
    members = groups * inner
    share = width // members
    rank = adapter_up_maps.shape[1]
    me = group * inner + place_in_group

    def slices(array):
        return [
            lax.dynamic_slice_in_dim(array, (me ^ offset) * share, share, axis=1) for offset in range(inner)
        ]

    def exchanged(blocks):
        return blocks[:1] + [to_partner(blocks[n], "inner", inner, n) for n in range(1, inner)]

    def rings(blocks, near_after=(), far_after=(), second_after=()):
        near = [after(jnp.concatenate(blocks[: inner // 2], axis=0), *near_after)]
        far = [after(jnp.concatenate(blocks[inner // 2 :], axis=0), *far_after)]
        for step in range(1, outer):
            near.append(next_on_ring(after(near[-1], *second_after) if step == 2 else near[-1], outer))
            far.append(next_on_ring(far[-1], outer))
        return near, far

    steps_back = jnp.arange(outer, dtype=jnp.int32)[:, None]
    labels = ((level - steps_back + outer) % outer) * inner + (
        place_in_group ^ jnp.arange(inner, dtype=jnp.int32)[None, :]
    )
    labels = labels.reshape(-1)

    down = exchanged(slices(adapter_down_maps[0].T))
    down_near, down_far = rings(down)
    ids = token_adapter_index.reshape(1, tok)
    rows = swap(after(outgoing_rows(hidden, ids, members), down[1]))
    up = exchanged([after(block, down_near[1]) for block in slices(adapter_up_maps[0])])

    down_maps = [m for pair in zip(down_near, down_far) for m in pair]
    packed, id_columns = down_product(labels, rows, down_maps, rank)
    up_near, up_far = rings(up, [down_near[-1]], [down_far[-1]], second_after=[packed])
    up_maps = [m for pair in zip(up_near, up_far) for m in pair]
    shrunk = swap(summed_copies(swap(packed)))
    return place([swap(up_product(labels, id_columns, shrunk, up_maps, rank))])


def solution(mesh):
    groups, wide = mesh.shape["groups"], mesh.shape["wide"]
    outer = 1 << ((wide.bit_length() - 1) // 2)
    fine = Mesh(mesh.devices.reshape(groups, outer, wide // outer), ("groups", "outer", "inner"))
    owner = ("outer", "inner")
    rows = P(("groups",) + owner, None)
    return jax.shard_map(
        per_device,
        mesh=fine,
        in_specs=(rows, rows, P(owner, None, None), P(owner, None, None)),
        out_specs=rows,
        check_vma=False,
    )
```

```python
import functools

import jax
import jax.numpy as jnp
from jax import lax
from jax.experimental import pallas as pl
from jax.experimental.pallas import tpu as pltpu
from jax.sharding import Mesh
from jax.sharding import PartitionSpec as P

adapter_scale = 2.0
PLANE = ("groups", "inner")
LANES = 128
ID_ROWS = 8
RINGS = 3
BLOCK = 8
IN_VMEM = pl.BlockSpec(memory_space=pltpu.VMEM)
IN_SMEM = pl.BlockSpec(memory_space=pltpu.SMEM)
IN_HBM = pl.BlockSpec(memory_space=pltpu.HBM)
ANYWHERE = pl.BlockSpec(memory_space=pl.ANY)


def params(scratch_bytes=0):
    return pltpu.CompilerParams(vmem_limit_bytes=(12 << 20) + 2 * scratch_bytes)


def to_partner(value, axes, size, offset):
    return lax.ppermute(value, axes, [(i, i ^ offset) for i in range(size)])


def next_on_ring(block, outer):
    return lax.ppermute(block, "outer", [(i, (i + 1) % outer) for i in range(outer)])


def after(value, *earlier):
    return lax.optimization_barrier((value,) + earlier)[0]


def swap(value):
    return lax.all_to_all(value, PLANE, split_axis=0, concat_axis=0, tiled=True)


def tile_labels(labels_ref, tile, rank, shape):
    per_tile = LANES // rank
    lane = lax.broadcasted_iota(jnp.int32, shape, 1)
    label = jnp.full(shape, labels_ref[tile * per_tile], jnp.int32)
    for n in range(1, per_tile):
        label = jnp.where(lane >= n * rank, labels_ref[tile * per_tile + n], label)
    return label.astype(jnp.float32)


def outgoing_kernel(hidden_ref, ids_ref, out_ref, sems):
    members, rows, share = out_ref.shape
    tok = rows - ID_ROWS
    copies = [
        pltpu.make_async_copy(
            hidden_ref.at[:, pl.ds(member * share, share)], out_ref.at[member, pl.ds(0, tok)], sems.at[member]
        )
        for member in range(members)
    ]
    for copy in copies:
        copy.start()
    ids = jnp.broadcast_to(ids_ref[...].astype(jnp.float32).astype(jnp.bfloat16), (ID_ROWS, tok))
    for member in range(members):
        out_ref[member, tok:, :tok] = ids
        if share > tok:
            out_ref[member, tok:, tok:] = jnp.zeros((ID_ROWS, share - tok), jnp.bfloat16)
    for copy in copies:
        copy.wait()


def outgoing_rows(hidden, ids, members):
    tok, width = hidden.shape
    share = width // members
    return pl.pallas_call(
        outgoing_kernel,
        out_shape=jax.ShapeDtypeStruct((members, tok + ID_ROWS, share), jnp.bfloat16),
        in_specs=[ANYWHERE, IN_VMEM],
        out_specs=IN_VMEM,
        scratch_shapes=[pltpu.SemaphoreType.DMA((members,))],
        compiler_params=params(),
        name="outgoing_rows",
    )(hidden, ids)


def held_maps(maps, step, first, rank):
    own, *others = maps[step * RINGS : (step + 1) * RINGS]
    return [own[first : first + rank, :]] + [other[...] for other in others]


def down_kernel(map_count, rank, labels_ref, rows_ref, *refs):
    maps, (packed_ref, ids_out, total_ref, ids_ref, sem) = refs[:map_count], refs[map_count:]
    members, rows, share = rows_ref.shape
    tok = rows - ID_ROWS
    block = min(BLOCK, members)
    half = tok // 2
    lane = lax.broadcasted_iota(jnp.int32, (half, LANES), 1)

    def one(step, _):
        first = step * block
        for n in range(block):
            row = rows_ref[first + n, tok : tok + 1, :LANES].astype(jnp.float32)
            ids_ref[first + n] = jnp.broadcast_to(row, (LANES, tok)).T
        tokens = rows_ref[pl.ds(first, block), :tok, :].reshape(block * tok, share)
        here = pl.ds(first, block)
        kept = pltpu.make_async_copy(ids_ref.at[here], ids_out.at[here], sem)
        kept.start()
        ids = ids_ref[here].reshape(block * tok, LANES)
        tile = 0
        for back in range(map_count // RINGS):
            held = jnp.concatenate(held_maps(maps, back, 0, rank), axis=0)
            for at in range(0, held.shape[0], 2 * LANES):
                some = held[at : at + 2 * LANES]
                product = lax.dot_general(
                    tokens, some, (((1,), (1,)), ((), ())), preferred_element_type=jnp.float32
                )
                total = jnp.zeros((block * tok, LANES), jnp.float32) if tile == 0 else total_ref[...]
                for n in range(some.shape[0] // LANES):
                    named = ids == tile_labels(labels_ref, tile, rank, (1, LANES))
                    total += jnp.where(named, product[:, n * LANES : (n + 1) * LANES], 0.0)
                    tile += 1
                total_ref[...] = total
        for n in range(block):
            total = total_ref[n * tok : (n + 1) * tok, :]
            total += pltpu.roll(total, LANES // 2, 1)
            packed_ref[first + n] = jnp.where(lane < rank, total[:half], total[half:])
        kept.wait()
        return 0

    lax.fori_loop(0, members // block, one, 0)


def down_product(labels, rows, maps, rank):
    members, tok, share = rows.shape
    tok -= ID_ROWS
    map_rows = labels.shape[0] * rank
    return pl.pallas_call(
        functools.partial(down_kernel, len(maps), rank),
        out_shape=[
            jax.ShapeDtypeStruct((members, tok // 2, LANES), jnp.float32),
            jax.ShapeDtypeStruct((members, tok, LANES), jnp.float32),
        ],
        in_specs=[IN_SMEM, IN_VMEM] + [IN_VMEM] * len(maps),
        out_specs=[IN_VMEM, IN_HBM],
        scratch_shapes=[
            pltpu.VMEM((min(BLOCK, members) * tok, LANES), jnp.float32),
            pltpu.VMEM((members, tok, LANES), jnp.float32),
            pltpu.SemaphoreType.DMA,
        ],
        compiler_params=params(8 * members * tok * LANES),
        cost_estimate=pl.CostEstimate(
            flops=2 * map_rows * members * tok * share,
            bytes_accessed=2 * share * (map_rows + members * tok),
            transcendentals=0,
        ),
        name="down_product",
    )(labels, rows, *maps)


def copies_kernel(terms_ref, out_ref):
    own = jnp.sum(terms_ref[...], axis=0).astype(jnp.bfloat16)
    for member in range(out_ref.shape[0]):
        out_ref[member] = own


def summed_copies(terms):
    return pl.pallas_call(
        copies_kernel,
        out_shape=jax.ShapeDtypeStruct(terms.shape, jnp.bfloat16),
        in_specs=[IN_VMEM],
        out_specs=IN_VMEM,
        compiler_params=params(),
        name="summed_copies",
    )(terms)


def up_kernel(map_count, rank, labels_ref, ids_ref, shrunk_ref, *refs):
    maps, (out_ref, spread_ref, ids_buf, sem) = refs[:map_count], refs[map_count:]
    kept = pltpu.make_async_copy(ids_ref, ids_buf, sem)
    kept.start()
    members, half, _ = shrunk_ref.shape
    tok = 2 * half
    block = min(BLOCK, members)
    tiles = spread_ref.shape[1] // LANES
    lane = lax.broadcasted_iota(jnp.int32, (half, LANES), 1)
    held = jnp.concatenate(
        [m for back in range(map_count // RINGS) for m in held_maps(maps, back, rank, rank)], axis=0
    )
    kept.wait()

    def one(step, _):
        first = step * block
        for n in range(block):
            packed = shrunk_ref[first + n].astype(jnp.float32)
            turned = pltpu.roll(packed, LANES // 2, 1)
            shrunk = jnp.concatenate(
                [jnp.where(lane < rank, packed, turned), jnp.where(lane < rank, turned, packed)], axis=0
            )
            ids = ids_buf[first + n]
            for tile in range(tiles):
                named = ids == tile_labels(labels_ref, tile, rank, (1, LANES))
                spread_ref[n * tok : (n + 1) * tok, tile * LANES : (tile + 1) * LANES] = jnp.where(
                    named, shrunk, 0.0
                ).astype(jnp.bfloat16)
        product = jnp.dot(spread_ref[...], held, preferred_element_type=jnp.float32)
        product = (adapter_scale * product).astype(jnp.bfloat16)
        out_ref[pl.ds(first, block)] = product.reshape(block, tok, product.shape[1])
        return 0

    lax.fori_loop(0, members // block, one, 0)


def up_product(labels, ids, shrunk, maps, rank):
    members, tok, _ = ids.shape
    map_rows, piece = labels.shape[0] * rank, maps[0].shape[1]
    return pl.pallas_call(
        functools.partial(up_kernel, len(maps), rank),
        out_shape=jax.ShapeDtypeStruct((members, tok, piece), jnp.bfloat16),
        in_specs=[IN_SMEM, IN_HBM, IN_VMEM] + [IN_VMEM] * len(maps),
        out_specs=IN_VMEM,
        scratch_shapes=[
            pltpu.VMEM((min(BLOCK, members) * tok, map_rows), jnp.bfloat16),
            pltpu.VMEM((members, tok, LANES), jnp.float32),
            pltpu.SemaphoreType.DMA,
        ],
        compiler_params=params(2 * min(BLOCK, members) * tok * map_rows + 4 * members * tok * LANES),
        cost_estimate=pl.CostEstimate(
            flops=2 * map_rows * members * tok * piece,
            bytes_accessed=2 * piece * (map_rows + members * tok),
            transcendentals=0,
        ),
        name="up_product",
    )(labels, ids, shrunk, *maps)


def place_kernel(pieces, *refs):
    parts, out_ref, sems = refs[:pieces], refs[-2], refs[-1]
    members, _, piece = parts[0].shape
    copies = []
    for n in range(members * pieces):
        member, part = n // pieces, n % pieces
        target = out_ref.at[:, pl.ds(n * piece, piece)]
        copies.append(pltpu.make_async_copy(parts[part].at[member], target, sems.at[n]))
    for copy in copies:
        copy.start()
    for copy in copies:
        copy.wait()


def place(parts):
    members, tok, piece = parts[0].shape
    return pl.pallas_call(
        functools.partial(place_kernel, len(parts)),
        out_shape=jax.ShapeDtypeStruct((tok, members * len(parts) * piece), jnp.bfloat16),
        in_specs=[ANYWHERE] * len(parts),
        out_specs=ANYWHERE,
        scratch_shapes=[pltpu.SemaphoreType.DMA((members * len(parts),))],
        compiler_params=params(),
        name="place_results",
    )(*parts)


def per_device(token_adapter_index, hidden, adapter_down_maps, adapter_up_maps):
    tok, width = hidden.shape
    groups, outer, inner = (lax.axis_size(a) for a in ("groups", "outer", "inner"))
    group, level, place_in_group = (lax.axis_index(a) for a in ("groups", "outer", "inner"))
    members = groups * inner
    share = width // members
    rank = adapter_up_maps.shape[1]
    me = group * inner + place_in_group

    def slices(offset):
        start = (me ^ offset) * share
        return jnp.concatenate(
            [
                lax.dynamic_slice_in_dim(adapter_down_maps[0].T, start, share, axis=1),
                lax.dynamic_slice_in_dim(adapter_up_maps[0], start, share, axis=1),
            ],
            axis=0,
        )

    got = [slices(0)] + [to_partner(slices(n), "inner", inner, n) for n in range(1, inner)]

    def ring(block, second_after=()):
        blocks = [block]
        for step in range(1, outer):
            block = next_on_ring(after(block, *second_after) if step == 2 else block, outer)
            blocks.append(block)
        return blocks

    steps_back = jnp.arange(outer, dtype=jnp.int32)[:, None]
    labels = ((level - steps_back + outer) % outer) * inner + (
        place_in_group ^ jnp.arange(inner, dtype=jnp.int32)[None, :]
    )
    labels = labels.reshape(-1)

    own = ring(got[0])
    down = [g[:rank] for g in got]
    up = [g[rank:] for g in got]
    middle = inner // 2
    down_near = ring(jnp.concatenate(down[1:middle], axis=0))
    down_far = ring(jnp.concatenate(down[middle:], axis=0))
    ids = token_adapter_index.reshape(1, tok)
    rows = swap(after(outgoing_rows(hidden, ids, members), *got[1:], own[2]))

    packed, id_columns = down_product(
        labels, rows, [m for step in zip(own, down_near, down_far) for m in step], rank
    )
    up_near = ring(after(jnp.concatenate(up[1:middle], axis=0), down_near[-1]))
    up_far = ring(after(jnp.concatenate(up[middle:], axis=0), down_far[-1]), second_after=[packed])
    shrunk = swap(summed_copies(swap(packed)))
    delta = up_product(labels, id_columns, shrunk, [m for step in zip(own, up_near, up_far) for m in step], rank)
    return place([swap(delta)])


def solution(mesh):
    groups, wide = mesh.shape["groups"], mesh.shape["wide"]
    outer = 1 << ((wide.bit_length() - 1) // 2)
    fine = Mesh(mesh.devices.reshape(groups, outer, wide // outer), ("groups", "outer", "inner"))
    owner = ("outer", "inner")
    rows = P(("groups",) + owner, None)
    return jax.shard_map(
        per_device,
        mesh=fine,
        in_specs=(rows, rows, P(owner, None, None), P(owner, None, None)),
        out_specs=rows,
        check_vma=False,
    )
```

```python
import functools

import jax
import jax.numpy as jnp
from jax import lax
from jax.experimental import pallas as pl
from jax.experimental.pallas import tpu as pltpu
from jax.sharding import Mesh
from jax.sharding import PartitionSpec as P

adapter_scale = 2.0
PLANE = ("groups", "inner")
LANES = 128
ID_ROWS = 8
BLOCK = 8
IN_VMEM = pl.BlockSpec(memory_space=pltpu.VMEM)
IN_SMEM = pl.BlockSpec(memory_space=pltpu.SMEM)
IN_HBM = pl.BlockSpec(memory_space=pltpu.HBM)
ANYWHERE = pl.BlockSpec(memory_space=pl.ANY)


def params(scratch_bytes=0):
    return pltpu.CompilerParams(vmem_limit_bytes=(12 << 20) + 2 * scratch_bytes)


def to_partner(value, axes, size, offset):
    return lax.ppermute(value, axes, [(i, i ^ offset) for i in range(size)])


def next_on_ring(block, outer):
    return lax.ppermute(block, "outer", [(i, (i + 1) % outer) for i in range(outer)])


def after(value, *earlier):
    return lax.optimization_barrier((value,) + earlier)[0]


def swap(value):
    return lax.all_to_all(value, PLANE, split_axis=0, concat_axis=0, tiled=True)


def tile_labels(labels_ref, tile, rank, shape):
    per_tile = LANES // rank
    lane = lax.broadcasted_iota(jnp.int32, shape, 1)
    label = jnp.full(shape, labels_ref[tile * per_tile], jnp.int32)
    for n in range(1, per_tile):
        label = jnp.where(lane >= n * rank, labels_ref[tile * per_tile + n], label)
    return label.astype(jnp.float32)


def join_kernel(*refs):
    blocks, out_ref = refs[:-1], refs[-1]
    rows = blocks[0].shape[0]
    for n, block in enumerate(blocks):
        out_ref[n * rows : (n + 1) * rows, :] = block[...]


def joined(blocks):
    rows, share = blocks[0].shape
    return pl.pallas_call(
        join_kernel,
        out_shape=jax.ShapeDtypeStruct((len(blocks) * rows, share), jnp.bfloat16),
        in_specs=[IN_VMEM] * len(blocks),
        out_specs=IN_VMEM,
        compiler_params=params(),
        cost_estimate=pl.CostEstimate(flops=10**11, bytes_accessed=10**9, transcendentals=0),
        name="join_blocks",
    )(*blocks)


def outgoing_kernel(hidden_ref, ids_ref, out_ref, sems):
    members, rows, share = out_ref.shape
    tok = rows - ID_ROWS
    copies = [
        pltpu.make_async_copy(
            hidden_ref.at[:, pl.ds(member * share, share)], out_ref.at[member, pl.ds(0, tok)], sems.at[member]
        )
        for member in range(members)
    ]
    for copy in copies:
        copy.start()
    ids = jnp.broadcast_to(ids_ref[...].astype(jnp.float32).astype(jnp.bfloat16), (ID_ROWS, tok))
    for member in range(members):
        out_ref[member, tok:, :tok] = ids
        if share > tok:
            out_ref[member, tok:, tok:] = jnp.zeros((ID_ROWS, share - tok), jnp.bfloat16)
    for copy in copies:
        copy.wait()


def outgoing_rows(hidden, ids, members):
    tok, width = hidden.shape
    share = width // members
    return pl.pallas_call(
        outgoing_kernel,
        out_shape=jax.ShapeDtypeStruct((members, tok + ID_ROWS, share), jnp.bfloat16),
        in_specs=[ANYWHERE, IN_VMEM],
        out_specs=IN_VMEM,
        scratch_shapes=[pltpu.SemaphoreType.DMA((members,))],
        compiler_params=params(),
        name="outgoing_rows",
    )(hidden, ids)


def down_kernel(map_count, rank, labels_ref, rows_ref, *refs):
    maps, (packed_ref, ids_out, total_ref, ids_ref, sem) = refs[:map_count], refs[map_count:]
    members, rows, share = rows_ref.shape
    tok = rows - ID_ROWS
    block = min(BLOCK, members)
    half = tok // 2
    lane = lax.broadcasted_iota(jnp.int32, (half, LANES), 1)

    def one(step, _):
        first = step * block
        for n in range(block):
            row = rows_ref[first + n, tok : tok + 1, :LANES].astype(jnp.float32)
            ids_ref[first + n] = jnp.broadcast_to(row, (LANES, tok)).T
        tokens = rows_ref[pl.ds(first, block), :tok, :].reshape(block * tok, share)
        here = pl.ds(first, block)
        kept = pltpu.make_async_copy(ids_ref.at[here], ids_out.at[here], sem)
        kept.start()
        ids = ids_ref[here].reshape(block * tok, LANES)
        tile = 0
        for at in range(0, map_count, 2):
            some = jnp.concatenate([m[...] for m in maps[at : at + 2]], axis=0)
            product = lax.dot_general(
                tokens, some, (((1,), (1,)), ((), ())), preferred_element_type=jnp.float32
            )
            total = jnp.zeros((block * tok, LANES), jnp.float32) if tile == 0 else total_ref[...]
            for n in range(some.shape[0] // LANES):
                named = ids == tile_labels(labels_ref, tile, rank, (1, LANES))
                total += jnp.where(named, product[:, n * LANES : (n + 1) * LANES], 0.0)
                tile += 1
            total_ref[...] = total
        for n in range(block):
            total = total_ref[n * tok : (n + 1) * tok, :]
            total += pltpu.roll(total, LANES // 2, 1)
            packed_ref[first + n] = jnp.where(lane < rank, total[:half], total[half:])
        kept.wait()
        return 0

    lax.fori_loop(0, members // block, one, 0)


def down_product(labels, rows, maps, rank):
    members, tok, share = rows.shape
    tok -= ID_ROWS
    map_rows = sum(m.shape[0] for m in maps)
    return pl.pallas_call(
        functools.partial(down_kernel, len(maps), rank),
        out_shape=[
            jax.ShapeDtypeStruct((members, tok // 2, LANES), jnp.float32),
            jax.ShapeDtypeStruct((members, tok, LANES), jnp.float32),
        ],
        in_specs=[IN_SMEM, IN_VMEM] + [IN_VMEM] * len(maps),
        out_specs=[IN_VMEM, IN_HBM],
        scratch_shapes=[
            pltpu.VMEM((min(BLOCK, members) * tok, LANES), jnp.float32),
            pltpu.VMEM((members, tok, LANES), jnp.float32),
            pltpu.SemaphoreType.DMA,
        ],
        compiler_params=params(8 * members * tok * LANES),
        cost_estimate=pl.CostEstimate(
            flops=2 * map_rows * members * tok * share,
            bytes_accessed=2 * share * (map_rows + members * tok),
            transcendentals=0,
        ),
        name="down_product",
    )(labels, rows, *maps)


def copies_kernel(terms_ref, out_ref):
    own = jnp.sum(terms_ref[...], axis=0).astype(jnp.bfloat16)
    for member in range(out_ref.shape[0]):
        out_ref[member] = own


def summed_copies(terms):
    return pl.pallas_call(
        copies_kernel,
        out_shape=jax.ShapeDtypeStruct(terms.shape, jnp.bfloat16),
        in_specs=[IN_VMEM],
        out_specs=IN_VMEM,
        compiler_params=params(),
        name="summed_copies",
    )(terms)


def up_kernel(map_count, rank, labels_ref, ids_ref, shrunk_ref, *refs):
    maps, (out_ref, spread_ref, ids_buf, sem) = refs[:map_count], refs[map_count:]
    kept = pltpu.make_async_copy(ids_ref, ids_buf, sem)
    kept.start()
    members, half, _ = shrunk_ref.shape
    tok = 2 * half
    block = min(BLOCK, members)
    tiles = spread_ref.shape[1] // LANES
    lane = lax.broadcasted_iota(jnp.int32, (half, LANES), 1)
    held = jnp.concatenate([m[...] for m in maps], axis=0)
    kept.wait()

    def one(step, _):
        first = step * block
        for n in range(block):
            packed = shrunk_ref[first + n].astype(jnp.float32)
            turned = pltpu.roll(packed, LANES // 2, 1)
            shrunk = jnp.concatenate(
                [jnp.where(lane < rank, packed, turned), jnp.where(lane < rank, turned, packed)], axis=0
            )
            ids = ids_buf[first + n]
            for tile in range(tiles):
                named = ids == tile_labels(labels_ref, tile, rank, (1, LANES))
                spread_ref[n * tok : (n + 1) * tok, tile * LANES : (tile + 1) * LANES] = jnp.where(
                    named, shrunk, 0.0
                ).astype(jnp.bfloat16)
        product = jnp.dot(spread_ref[...], held, preferred_element_type=jnp.float32)
        product = (adapter_scale * product).astype(jnp.bfloat16)
        out_ref[pl.ds(first, block)] = product.reshape(block, tok, product.shape[1])
        return 0

    lax.fori_loop(0, members // block, one, 0)


def up_product(labels, ids, shrunk, maps, rank):
    members, tok, _ = ids.shape
    map_rows, piece = sum(m.shape[0] for m in maps), maps[0].shape[1]
    return pl.pallas_call(
        functools.partial(up_kernel, len(maps), rank),
        out_shape=jax.ShapeDtypeStruct((members, tok, piece), jnp.bfloat16),
        in_specs=[IN_SMEM, IN_HBM, IN_VMEM] + [IN_VMEM] * len(maps),
        out_specs=IN_VMEM,
        scratch_shapes=[
            pltpu.VMEM((min(BLOCK, members) * tok, map_rows), jnp.bfloat16),
            pltpu.VMEM((members, tok, LANES), jnp.float32),
            pltpu.SemaphoreType.DMA,
        ],
        compiler_params=params(2 * min(BLOCK, members) * tok * map_rows + 4 * members * tok * LANES),
        cost_estimate=pl.CostEstimate(
            flops=2 * map_rows * members * tok * piece,
            bytes_accessed=2 * piece * (map_rows + members * tok),
            transcendentals=0,
        ),
        name="up_product",
    )(labels, ids, shrunk, *maps)


def place_kernel(pieces, *refs):
    parts, out_ref, sems = refs[:pieces], refs[-2], refs[-1]
    members, _, piece = parts[0].shape
    copies = []
    for n in range(members * pieces):
        member, part = n // pieces, n % pieces
        target = out_ref.at[:, pl.ds(n * piece, piece)]
        copies.append(pltpu.make_async_copy(parts[part].at[member], target, sems.at[n]))
    for copy in copies:
        copy.start()
    for copy in copies:
        copy.wait()


def place(parts):
    members, tok, piece = parts[0].shape
    return pl.pallas_call(
        functools.partial(place_kernel, len(parts)),
        out_shape=jax.ShapeDtypeStruct((tok, members * len(parts) * piece), jnp.bfloat16),
        in_specs=[ANYWHERE] * len(parts),
        out_specs=ANYWHERE,
        scratch_shapes=[pltpu.SemaphoreType.DMA((members * len(parts),))],
        compiler_params=params(),
        name="place_results",
    )(*parts)


def per_device(token_adapter_index, hidden, adapter_down_maps, adapter_up_maps):
    tok, width = hidden.shape
    groups, outer, inner = (lax.axis_size(a) for a in ("groups", "outer", "inner"))
    group, level, place_in_group = (lax.axis_index(a) for a in ("groups", "outer", "inner"))
    members = groups * inner
    share = width // members
    rank = adapter_up_maps.shape[1]
    me = group * inner + place_in_group

    def slices(array):
        return [
            lax.dynamic_slice_in_dim(array, (me ^ offset) * share, share, axis=1) for offset in range(inner)
        ]

    def exchanged(blocks):
        return blocks[:1] + [to_partner(blocks[n], "inner", inner, n) for n in range(1, inner)]

    def rings(near, far, second_after=()):
        near, far = [near], [far]
        for step in range(1, outer):
            near.append(next_on_ring(after(near[-1], *second_after) if step == 2 else near[-1], outer))
            far.append(next_on_ring(far[-1], outer))
        return near, far

    steps_back = jnp.arange(outer, dtype=jnp.int32)[:, None]
    labels = ((level - steps_back + outer) % outer) * inner + (
        place_in_group ^ jnp.arange(inner, dtype=jnp.int32)[None, :]
    )
    labels = labels.reshape(-1)

    middle = inner // 2
    down = exchanged(slices(adapter_down_maps[0].T))
    down_near, down_far = rings(joined(down[:middle]), joined(down[middle:]))
    ids = token_adapter_index.reshape(1, tok)
    rows = swap(after(outgoing_rows(hidden, ids, members), down_near[0]))
    up = exchanged([after(block, down_near[1]) for block in slices(adapter_up_maps[0])])

    down_maps = [m for pair in zip(down_near, down_far) for m in pair]
    packed, id_columns = down_product(labels, rows, down_maps, rank)
    up_near, up_far = rings(
        after(jnp.concatenate(up[:middle], axis=0), down_near[-1]),
        after(jnp.concatenate(up[middle:], axis=0), down_far[-1]),
        second_after=[packed],
    )
    up_maps = [m for pair in zip(up_near, up_far) for m in pair]
    shrunk = swap(summed_copies(swap(packed)))
    return place([swap(up_product(labels, id_columns, shrunk, up_maps, rank))])


def solution(mesh):
    groups, wide = mesh.shape["groups"], mesh.shape["wide"]
    outer = 1 << ((wide.bit_length() - 1) // 2)
    fine = Mesh(mesh.devices.reshape(groups, outer, wide // outer), ("groups", "outer", "inner"))
    owner = ("outer", "inner")
    rows = P(("groups",) + owner, None)
    return jax.shard_map(
        per_device,
        mesh=fine,
        in_specs=(rows, rows, P(owner, None, None), P(owner, None, None)),
        out_specs=rows,
        check_vma=False,
    )
```

```python
import functools

import jax
import jax.numpy as jnp
from jax import lax
from jax.experimental import pallas as pl
from jax.experimental.pallas import tpu as pltpu
from jax.sharding import Mesh
from jax.sharding import PartitionSpec as P

adapter_scale = 2.0
PLANE = ("groups", "inner")
LANES = 128
ID_ROWS = 8
AHEAD, SLIGHTLY_AHEAD = 10**9, 15 * 10**6
BLOCK = 8
IN_VMEM = pl.BlockSpec(memory_space=pltpu.VMEM)
IN_SMEM = pl.BlockSpec(memory_space=pltpu.SMEM)
IN_HBM = pl.BlockSpec(memory_space=pltpu.HBM)
ANYWHERE = pl.BlockSpec(memory_space=pl.ANY)


def params(scratch_bytes=0):
    return pltpu.CompilerParams(vmem_limit_bytes=(12 << 20) + 2 * scratch_bytes)


def to_partner(value, axes, size, offset):
    return lax.ppermute(value, axes, [(i, i ^ offset) for i in range(size)])


def next_on_ring(block, outer):
    return lax.ppermute(block, "outer", [(i, (i + 1) % outer) for i in range(outer)])


def after(value, *earlier):
    return lax.optimization_barrier((value,) + earlier)[0]


def swap(value):
    return lax.all_to_all(value, PLANE, split_axis=0, concat_axis=0, tiled=True)


def tile_labels(labels_ref, tile, rank, shape):
    per_tile = LANES // rank
    lane = lax.broadcasted_iota(jnp.int32, shape, 1)
    label = jnp.full(shape, labels_ref[tile * per_tile], jnp.int32)
    for n in range(1, per_tile):
        label = jnp.where(lane >= n * rank, labels_ref[tile * per_tile + n], label)
    return label.astype(jnp.float32)


def join_kernel(*refs):
    blocks, out_ref = refs[:-1], refs[-1]
    rows = blocks[0].shape[0]
    for n, block in enumerate(blocks):
        out_ref[n * rows : (n + 1) * rows, :] = block[...]


def joined(blocks, cost_bytes):
    rows, share = blocks[0].shape
    return pl.pallas_call(
        join_kernel,
        out_shape=jax.ShapeDtypeStruct((len(blocks) * rows, share), jnp.bfloat16),
        in_specs=[IN_VMEM] * len(blocks),
        out_specs=IN_VMEM,
        compiler_params=params(),
        cost_estimate=pl.CostEstimate(flops=0, bytes_accessed=cost_bytes, transcendentals=0),
        name="join_blocks",
    )(*blocks)


def outgoing_kernel(hidden_ref, ids_ref, out_ref, sems):
    members, rows, share = out_ref.shape
    tok = rows - ID_ROWS
    copies = [
        pltpu.make_async_copy(
            hidden_ref.at[:, pl.ds(member * share, share)], out_ref.at[member, pl.ds(0, tok)], sems.at[member]
        )
        for member in range(members)
    ]
    for copy in copies:
        copy.start()
    ids = jnp.broadcast_to(ids_ref[...].astype(jnp.float32).astype(jnp.bfloat16), (ID_ROWS, tok))
    for member in range(members):
        out_ref[member, tok:, :tok] = ids
        if share > tok:
            out_ref[member, tok:, tok:] = jnp.zeros((ID_ROWS, share - tok), jnp.bfloat16)
    for copy in copies:
        copy.wait()


def outgoing_rows(hidden, ids, members):
    tok, width = hidden.shape
    share = width // members
    return pl.pallas_call(
        outgoing_kernel,
        out_shape=jax.ShapeDtypeStruct((members, tok + ID_ROWS, share), jnp.bfloat16),
        in_specs=[ANYWHERE, IN_VMEM],
        out_specs=IN_VMEM,
        scratch_shapes=[pltpu.SemaphoreType.DMA((members,))],
        compiler_params=params(),
        name="outgoing_rows",
    )(hidden, ids)


def down_kernel(map_count, rank, labels_ref, rows_ref, *refs):
    maps, (packed_ref, ids_out, total_ref, ids_ref, sem) = refs[:map_count], refs[map_count:]
    members, rows, share = rows_ref.shape
    tok = rows - ID_ROWS
    block = min(BLOCK, members)
    half = tok // 2
    lane = lax.broadcasted_iota(jnp.int32, (half, LANES), 1)

    def one(step, _):
        first = step * block
        for n in range(block):
            row = rows_ref[first + n, tok : tok + 1, :LANES].astype(jnp.float32)
            ids_ref[first + n] = jnp.broadcast_to(row, (LANES, tok)).T
        tokens = rows_ref[pl.ds(first, block), :tok, :].reshape(block * tok, share)
        here = pl.ds(first, block)
        kept = pltpu.make_async_copy(ids_ref.at[here], ids_out.at[here], sem)
        kept.start()
        ids = ids_ref[here].reshape(block * tok, LANES)
        tile = 0
        for at in range(0, map_count, 2):
            some = jnp.concatenate([m[...] for m in maps[at : at + 2]], axis=0)
            product = lax.dot_general(
                tokens, some, (((1,), (1,)), ((), ())), preferred_element_type=jnp.float32
            )
            total = jnp.zeros((block * tok, LANES), jnp.float32) if tile == 0 else total_ref[...]
            for n in range(some.shape[0] // LANES):
                named = ids == tile_labels(labels_ref, tile, rank, (1, LANES))
                total += jnp.where(named, product[:, n * LANES : (n + 1) * LANES], 0.0)
                tile += 1
            total_ref[...] = total
        for n in range(block):
            total = total_ref[n * tok : (n + 1) * tok, :]
            total += pltpu.roll(total, LANES // 2, 1)
            packed_ref[first + n] = jnp.where(lane < rank, total[:half], total[half:])
        kept.wait()
        return 0

    lax.fori_loop(0, members // block, one, 0)


def down_product(labels, rows, maps, rank):
    members, tok, share = rows.shape
    tok -= ID_ROWS
    map_rows = sum(m.shape[0] for m in maps)
    return pl.pallas_call(
        functools.partial(down_kernel, len(maps), rank),
        out_shape=[
            jax.ShapeDtypeStruct((members, tok // 2, LANES), jnp.float32),
            jax.ShapeDtypeStruct((members, tok, LANES), jnp.float32),
        ],
        in_specs=[IN_SMEM, IN_VMEM] + [IN_VMEM] * len(maps),
        out_specs=[IN_VMEM, IN_HBM],
        scratch_shapes=[
            pltpu.VMEM((min(BLOCK, members) * tok, LANES), jnp.float32),
            pltpu.VMEM((members, tok, LANES), jnp.float32),
            pltpu.SemaphoreType.DMA,
        ],
        compiler_params=params(8 * members * tok * LANES),
        cost_estimate=pl.CostEstimate(
            flops=2 * map_rows * members * tok * share,
            bytes_accessed=2 * share * (map_rows + members * tok),
            transcendentals=0,
        ),
        name="down_product",
    )(labels, rows, *maps)


def copies_kernel(terms_ref, out_ref):
    own = jnp.sum(terms_ref[...], axis=0).astype(jnp.bfloat16)
    for member in range(out_ref.shape[0]):
        out_ref[member] = own


def summed_copies(terms):
    return pl.pallas_call(
        copies_kernel,
        out_shape=jax.ShapeDtypeStruct(terms.shape, jnp.bfloat16),
        in_specs=[IN_VMEM],
        out_specs=IN_VMEM,
        compiler_params=params(),
        name="summed_copies",
    )(terms)


def up_kernel(map_count, rank, labels_ref, ids_ref, shrunk_ref, *refs):
    maps, (out_ref, spread_ref, ids_buf, sem) = refs[:map_count], refs[map_count:]
    kept = pltpu.make_async_copy(ids_ref, ids_buf, sem)
    kept.start()
    members, half, _ = shrunk_ref.shape
    tok = 2 * half
    block = min(BLOCK, members)
    tiles = spread_ref.shape[1] // LANES
    lane = lax.broadcasted_iota(jnp.int32, (half, LANES), 1)
    held = jnp.concatenate([m[...] for m in maps], axis=0)
    kept.wait()

    def one(step, _):
        first = step * block
        for n in range(block):
            packed = shrunk_ref[first + n].astype(jnp.float32)
            turned = pltpu.roll(packed, LANES // 2, 1)
            shrunk = jnp.concatenate(
                [jnp.where(lane < rank, packed, turned), jnp.where(lane < rank, turned, packed)], axis=0
            )
            ids = ids_buf[first + n]
            for tile in range(tiles):
                named = ids == tile_labels(labels_ref, tile, rank, (1, LANES))
                spread_ref[n * tok : (n + 1) * tok, tile * LANES : (tile + 1) * LANES] = jnp.where(
                    named, shrunk, 0.0
                ).astype(jnp.bfloat16)
        product = jnp.dot(spread_ref[...], held, preferred_element_type=jnp.float32)
        product = (adapter_scale * product).astype(jnp.bfloat16)
        out_ref[pl.ds(first, block)] = product.reshape(block, tok, product.shape[1])
        return 0

    lax.fori_loop(0, members // block, one, 0)


def up_product(labels, ids, shrunk, maps, rank):
    members, tok, _ = ids.shape
    map_rows, piece = sum(m.shape[0] for m in maps), maps[0].shape[1]
    return pl.pallas_call(
        functools.partial(up_kernel, len(maps), rank),
        out_shape=jax.ShapeDtypeStruct((members, tok, piece), jnp.bfloat16),
        in_specs=[IN_SMEM, IN_HBM, IN_VMEM] + [IN_VMEM] * len(maps),
        out_specs=IN_VMEM,
        scratch_shapes=[
            pltpu.VMEM((min(BLOCK, members) * tok, map_rows), jnp.bfloat16),
            pltpu.VMEM((members, tok, LANES), jnp.float32),
            pltpu.SemaphoreType.DMA,
        ],
        compiler_params=params(2 * min(BLOCK, members) * tok * map_rows + 4 * members * tok * LANES),
        cost_estimate=pl.CostEstimate(
            flops=2 * map_rows * members * tok * piece,
            bytes_accessed=2 * piece * (map_rows + members * tok),
            transcendentals=0,
        ),
        name="up_product",
    )(labels, ids, shrunk, *maps)


def place_kernel(pieces, *refs):
    parts, out_ref, sems = refs[:pieces], refs[-2], refs[-1]
    members, _, piece = parts[0].shape
    copies = []
    for n in range(members * pieces):
        member, part = n // pieces, n % pieces
        target = out_ref.at[:, pl.ds(n * piece, piece)]
        copies.append(pltpu.make_async_copy(parts[part].at[member], target, sems.at[n]))
    for copy in copies:
        copy.start()
    for copy in copies:
        copy.wait()


def place(parts):
    members, tok, piece = parts[0].shape
    return pl.pallas_call(
        functools.partial(place_kernel, len(parts)),
        out_shape=jax.ShapeDtypeStruct((tok, members * len(parts) * piece), jnp.bfloat16),
        in_specs=[ANYWHERE] * len(parts),
        out_specs=ANYWHERE,
        scratch_shapes=[pltpu.SemaphoreType.DMA((members * len(parts),))],
        compiler_params=params(),
        name="place_results",
    )(*parts)


def per_device(token_adapter_index, hidden, adapter_down_maps, adapter_up_maps):
    tok, width = hidden.shape
    groups, outer, inner = (lax.axis_size(a) for a in ("groups", "outer", "inner"))
    group, level, place_in_group = (lax.axis_index(a) for a in ("groups", "outer", "inner"))
    members = groups * inner
    share = width // members
    rank = adapter_up_maps.shape[1]
    me = group * inner + place_in_group

    def slices(array):
        return [
            lax.dynamic_slice_in_dim(array, (me ^ offset) * share, share, axis=1) for offset in range(inner)
        ]

    def exchanged(blocks):
        return blocks[:1] + [to_partner(blocks[n], "inner", inner, n) for n in range(1, inner)]

    def rings(near, far, first_cost=0, second_after=()):
        near, far = [near], [far]
        for step in range(1, outer):
            if step == 2:
                near_block, far_block = after(near[-1], *second_after), after(far[-1], *second_after)
                if first_cost:
                    near_block = joined([near_block], first_cost)
            else:
                near_block, far_block = near[-1], far[-1]
            near.append(next_on_ring(near_block, outer))
            far.append(next_on_ring(far_block, outer))
        return near, far

    steps_back = jnp.arange(outer, dtype=jnp.int32)[:, None]
    labels = ((level - steps_back + outer) % outer) * inner + (
        place_in_group ^ jnp.arange(inner, dtype=jnp.int32)[None, :]
    )
    labels = labels.reshape(-1)

    middle = inner // 2
    down = exchanged(slices(adapter_down_maps[0].T))
    down_near, down_far = rings(joined(down[:middle], AHEAD), joined(down[middle:], AHEAD), first_cost=SLIGHTLY_AHEAD)
    ids = token_adapter_index.reshape(1, tok)
    rows = swap(after(outgoing_rows(hidden, ids, members), down_near[0]))
    up = exchanged([after(block, down_near[1]) for block in slices(adapter_up_maps[0])])

    down_maps = [m for pair in zip(down_near, down_far) for m in pair]
    packed, id_columns = down_product(labels, rows, down_maps, rank)
    up_near, up_far = rings(
        after(jnp.concatenate(up[:middle], axis=0), down_near[-1]),
        after(jnp.concatenate(up[middle:], axis=0), down_far[-1]),
        second_after=[packed],
    )
    up_maps = [m for pair in zip(up_near, up_far) for m in pair]
    shrunk = swap(summed_copies(swap(packed)))
    return place([swap(up_product(labels, id_columns, shrunk, up_maps, rank))])


def solution(mesh):
    groups, wide = mesh.shape["groups"], mesh.shape["wide"]
    outer = 1 << ((wide.bit_length() - 1) // 2)
    fine = Mesh(mesh.devices.reshape(groups, outer, wide // outer), ("groups", "outer", "inner"))
    owner = ("outer", "inner")
    rows = P(("groups",) + owner, None)
    return jax.shard_map(
        per_device,
        mesh=fine,
        in_specs=(rows, rows, P(owner, None, None), P(owner, None, None)),
        out_specs=rows,
        check_vma=False,
    )
```

```python
import functools

import jax
import jax.numpy as jnp
from jax import lax
from jax.experimental import pallas as pl
from jax.experimental.pallas import tpu as pltpu
from jax.sharding import Mesh
from jax.sharding import PartitionSpec as P

adapter_scale = 2.0
PLANE = ("groups", "inner")
LANES = 128
ID_ROWS = 8
AHEAD, SLIGHTLY_AHEAD = 10**11, 5 * 10**9
BLOCK = 8
IN_VMEM = pl.BlockSpec(memory_space=pltpu.VMEM)
IN_SMEM = pl.BlockSpec(memory_space=pltpu.SMEM)
IN_HBM = pl.BlockSpec(memory_space=pltpu.HBM)
ANYWHERE = pl.BlockSpec(memory_space=pl.ANY)


def params(scratch_bytes=0):
    return pltpu.CompilerParams(vmem_limit_bytes=(12 << 20) + 2 * scratch_bytes)


def to_partner(value, axes, size, offset):
    return lax.ppermute(value, axes, [(i, i ^ offset) for i in range(size)])


def next_on_ring(block, outer):
    return lax.ppermute(block, "outer", [(i, (i + 1) % outer) for i in range(outer)])


def after(value, *earlier):
    return lax.optimization_barrier((value,) + earlier)[0]


def swap(value):
    return lax.all_to_all(value, PLANE, split_axis=0, concat_axis=0, tiled=True)


def tile_labels(labels_ref, tile, rank, shape):
    per_tile = LANES // rank
    lane = lax.broadcasted_iota(jnp.int32, shape, 1)
    label = jnp.full(shape, labels_ref[tile * per_tile], jnp.int32)
    for n in range(1, per_tile):
        label = jnp.where(lane >= n * rank, labels_ref[tile * per_tile + n], label)
    return label.astype(jnp.float32)


def join_kernel(*refs):
    blocks, out_ref = refs[:-1], refs[-1]
    rows = blocks[0].shape[0]
    for n, block in enumerate(blocks):
        out_ref[n * rows : (n + 1) * rows, :] = block[...]


def joined(blocks, cost):
    rows, share = blocks[0].shape
    return pl.pallas_call(
        join_kernel,
        out_shape=jax.ShapeDtypeStruct((len(blocks) * rows, share), jnp.bfloat16),
        in_specs=[IN_VMEM] * len(blocks),
        out_specs=IN_VMEM,
        compiler_params=params(),
        cost_estimate=pl.CostEstimate(flops=cost, bytes_accessed=10**6, transcendentals=0),
        name="join_blocks",
    )(*blocks)


def outgoing_kernel(hidden_ref, ids_ref, out_ref, sems):
    members, rows, share = out_ref.shape
    tok = rows - ID_ROWS
    copies = [
        pltpu.make_async_copy(
            hidden_ref.at[:, pl.ds(member * share, share)], out_ref.at[member, pl.ds(0, tok)], sems.at[member]
        )
        for member in range(members)
    ]
    for copy in copies:
        copy.start()
    ids = jnp.broadcast_to(ids_ref[...].astype(jnp.float32).astype(jnp.bfloat16), (ID_ROWS, tok))
    for member in range(members):
        out_ref[member, tok:, :tok] = ids
        if share > tok:
            out_ref[member, tok:, tok:] = jnp.zeros((ID_ROWS, share - tok), jnp.bfloat16)
    for copy in copies:
        copy.wait()


def outgoing_rows(hidden, ids, members):
    tok, width = hidden.shape
    share = width // members
    return pl.pallas_call(
        outgoing_kernel,
        out_shape=jax.ShapeDtypeStruct((members, tok + ID_ROWS, share), jnp.bfloat16),
        in_specs=[ANYWHERE, IN_VMEM],
        out_specs=IN_VMEM,
        scratch_shapes=[pltpu.SemaphoreType.DMA((members,))],
        compiler_params=params(),
        name="outgoing_rows",
    )(hidden, ids)


def down_kernel(map_count, rank, labels_ref, rows_ref, *refs):
    maps, (packed_ref, ids_out, total_ref, ids_ref, sem) = refs[:map_count], refs[map_count:]
    members, rows, share = rows_ref.shape
    tok = rows - ID_ROWS
    block = min(BLOCK, members)
    half = tok // 2
    lane = lax.broadcasted_iota(jnp.int32, (half, LANES), 1)

    def one(step, _):
        first = step * block
        for n in range(block):
            row = rows_ref[first + n, tok : tok + 1, :LANES].astype(jnp.float32)
            ids_ref[first + n] = jnp.broadcast_to(row, (LANES, tok)).T
        tokens = rows_ref[pl.ds(first, block), :tok, :].reshape(block * tok, share)
        here = pl.ds(first, block)
        kept = pltpu.make_async_copy(ids_ref.at[here], ids_out.at[here], sem)
        kept.start()
        ids = ids_ref[here].reshape(block * tok, LANES)
        tile = 0
        for at in range(0, map_count, 2):
            some = jnp.concatenate([m[...] for m in maps[at : at + 2]], axis=0)
            product = lax.dot_general(
                tokens, some, (((1,), (1,)), ((), ())), preferred_element_type=jnp.float32
            )
            total = jnp.zeros((block * tok, LANES), jnp.float32) if tile == 0 else total_ref[...]
            for n in range(some.shape[0] // LANES):
                named = ids == tile_labels(labels_ref, tile, rank, (1, LANES))
                total += jnp.where(named, product[:, n * LANES : (n + 1) * LANES], 0.0)
                tile += 1
            total_ref[...] = total
        for n in range(block):
            total = total_ref[n * tok : (n + 1) * tok, :]
            total += pltpu.roll(total, LANES // 2, 1)
            packed_ref[first + n] = jnp.where(lane < rank, total[:half], total[half:])
        kept.wait()
        return 0

    lax.fori_loop(0, members // block, one, 0)


def down_product(labels, rows, maps, rank):
    members, tok, share = rows.shape
    tok -= ID_ROWS
    map_rows = sum(m.shape[0] for m in maps)
    return pl.pallas_call(
        functools.partial(down_kernel, len(maps), rank),
        out_shape=[
            jax.ShapeDtypeStruct((members, tok // 2, LANES), jnp.float32),
            jax.ShapeDtypeStruct((members, tok, LANES), jnp.float32),
        ],
        in_specs=[IN_SMEM, IN_VMEM] + [IN_VMEM] * len(maps),
        out_specs=[IN_VMEM, IN_HBM],
        scratch_shapes=[
            pltpu.VMEM((min(BLOCK, members) * tok, LANES), jnp.float32),
            pltpu.VMEM((members, tok, LANES), jnp.float32),
            pltpu.SemaphoreType.DMA,
        ],
        compiler_params=params(8 * members * tok * LANES),
        cost_estimate=pl.CostEstimate(
            flops=2 * map_rows * members * tok * share,
            bytes_accessed=2 * share * (map_rows + members * tok),
            transcendentals=0,
        ),
        name="down_product",
    )(labels, rows, *maps)


def copies_kernel(terms_ref, out_ref):
    own = jnp.sum(terms_ref[...], axis=0).astype(jnp.bfloat16)
    for member in range(out_ref.shape[0]):
        out_ref[member] = own


def summed_copies(terms):
    return pl.pallas_call(
        copies_kernel,
        out_shape=jax.ShapeDtypeStruct(terms.shape, jnp.bfloat16),
        in_specs=[IN_VMEM],
        out_specs=IN_VMEM,
        compiler_params=params(),
        name="summed_copies",
    )(terms)


def up_kernel(map_count, rank, labels_ref, me_ref, ids_ref, shrunk_ref, *refs):
    members, half, _ = shrunk_ref.shape
    maps, outs = refs[:map_count], refs[map_count : map_count + members]
    spread_ref, ids_buf, sem = refs[map_count + members :]
    kept = pltpu.make_async_copy(ids_ref, ids_buf, sem)
    kept.start()
    tok = 2 * half
    block = min(BLOCK, members)
    tiles = spread_ref.shape[1] // LANES
    lane = lax.broadcasted_iota(jnp.int32, (half, LANES), 1)
    held = jnp.concatenate([m[...] for m in maps], axis=0)
    kept.wait()
    for first in range(0, members, block):
        for n in range(block):
            member = me_ref[0] ^ (first + n)
            packed = shrunk_ref[member].astype(jnp.float32)
            turned = pltpu.roll(packed, LANES // 2, 1)
            shrunk = jnp.concatenate(
                [jnp.where(lane < rank, packed, turned), jnp.where(lane < rank, turned, packed)], axis=0
            )
            ids = ids_buf[member]
            for tile in range(tiles):
                named = ids == tile_labels(labels_ref, tile, rank, (1, LANES))
                spread_ref[n * tok : (n + 1) * tok, tile * LANES : (tile + 1) * LANES] = jnp.where(
                    named, shrunk, 0.0
                ).astype(jnp.bfloat16)
        product = jnp.dot(spread_ref[...], held, preferred_element_type=jnp.float32)
        product = (adapter_scale * product).astype(jnp.bfloat16)
        for n in range(block):
            outs[first + n][...] = product[n * tok : (n + 1) * tok, :]


def up_product(labels, me, ids, shrunk, maps, rank):
    members, tok, _ = ids.shape
    map_rows, piece = sum(m.shape[0] for m in maps), maps[0].shape[1]
    return pl.pallas_call(
        functools.partial(up_kernel, len(maps), rank),
        out_shape=[jax.ShapeDtypeStruct((tok, piece), jnp.bfloat16)] * members,
        in_specs=[IN_SMEM, IN_SMEM, IN_HBM, IN_VMEM] + [IN_VMEM] * len(maps),
        out_specs=[IN_VMEM] * members,
        scratch_shapes=[
            pltpu.VMEM((min(BLOCK, members) * tok, map_rows), jnp.bfloat16),
            pltpu.VMEM((members, tok, LANES), jnp.float32),
            pltpu.SemaphoreType.DMA,
        ],
        compiler_params=params(2 * min(BLOCK, members) * tok * map_rows + 4 * members * tok * LANES),
        cost_estimate=pl.CostEstimate(
            flops=2 * map_rows * members * tok * piece,
            bytes_accessed=2 * piece * (map_rows + members * tok),
            transcendentals=0,
        ),
        name="up_product",
    )(labels, me, ids, shrunk, *maps)


def place_kernel(me_ref, *refs):
    blocks, out_ref, sems = refs[:-2], refs[-2], refs[-1]
    share = blocks[0].shape[1]
    copies = []
    for offset, block in enumerate(blocks):
        at = pl.multiple_of((me_ref[0] ^ offset) * share, LANES)
        copies.append(pltpu.make_async_copy(block, out_ref.at[:, pl.ds(at, share)], sems.at[offset]))
    for copy in copies:
        copy.start()
    for copy in copies:
        copy.wait()


def place(me, blocks):
    tok, share = blocks[0].shape
    return pl.pallas_call(
        place_kernel,
        out_shape=jax.ShapeDtypeStruct((tok, len(blocks) * share), jnp.bfloat16),
        in_specs=[IN_SMEM] + [ANYWHERE] * len(blocks),
        out_specs=ANYWHERE,
        scratch_shapes=[pltpu.SemaphoreType.DMA((len(blocks),))],
        compiler_params=params(),
        name="place_results",
    )(me, *blocks)


def per_device(token_adapter_index, hidden, adapter_down_maps, adapter_up_maps):
    tok, width = hidden.shape
    groups, outer, inner = (lax.axis_size(a) for a in ("groups", "outer", "inner"))
    group, level, place_in_group = (lax.axis_index(a) for a in ("groups", "outer", "inner"))
    members = groups * inner
    share = width // members
    rank = adapter_up_maps.shape[1]
    me = group * inner + place_in_group

    def slices(array):
        return [
            lax.dynamic_slice_in_dim(array, (me ^ offset) * share, share, axis=1) for offset in range(inner)
        ]

    def exchanged(blocks):
        return blocks[:1] + [to_partner(blocks[n], "inner", inner, n) for n in range(1, inner)]

    def rings(near, far, first_cost=0, second_after=()):
        near, far = [near], [far]
        for step in range(1, outer):
            block = near[-1]
            if step == 2:
                block = after(block, *second_after)
                if first_cost:
                    block = joined([block], first_cost)
            near.append(next_on_ring(block, outer))
            far.append(next_on_ring(far[-1], outer))
        return near, far

    steps_back = jnp.arange(outer, dtype=jnp.int32)[:, None]
    labels = ((level - steps_back + outer) % outer) * inner + (
        place_in_group ^ jnp.arange(inner, dtype=jnp.int32)[None, :]
    )
    labels = labels.reshape(-1)

    middle = inner // 2
    down = exchanged(slices(adapter_down_maps[0].T))
    down_near, down_far = rings(joined(down[:middle], AHEAD), joined(down[middle:], AHEAD), first_cost=SLIGHTLY_AHEAD)
    ids = token_adapter_index.reshape(1, tok)
    rows = swap(after(outgoing_rows(hidden, ids, members), down_near[0]))
    up = exchanged([after(block, down_near[1]) for block in slices(adapter_up_maps[0])])

    down_maps = [m for pair in zip(down_near, down_far) for m in pair]
    packed, id_columns = down_product(labels, rows, down_maps, rank)
    up_near, up_far = rings(
        after(jnp.concatenate(up[:middle], axis=0), down_near[-1]),
        after(jnp.concatenate(up[middle:], axis=0), down_far[-1]),
        second_after=[packed],
    )
    up_maps = [m for pair in zip(up_near, up_far) for m in pair]
    shrunk = swap(summed_copies(swap(packed)))
    results = list(up_product(labels, me.reshape(1), id_columns, shrunk, up_maps, rank))
    returned = results[:1] + [to_partner(results[n], PLANE, members, n) for n in range(1, members)]
    return place(me.reshape(1), returned)


def solution(mesh):
    groups, wide = mesh.shape["groups"], mesh.shape["wide"]
    outer = 1 << ((wide.bit_length() - 1) // 2)
    fine = Mesh(mesh.devices.reshape(groups, outer, wide // outer), ("groups", "outer", "inner"))
    owner = ("outer", "inner")
    rows = P(("groups",) + owner, None)
    return jax.shard_map(
        per_device,
        mesh=fine,
        in_specs=(rows, rows, P(owner, None, None), P(owner, None, None)),
        out_specs=rows,
        check_vma=False,
    )
```

```python
import functools

import jax
import jax.numpy as jnp
from jax import lax
from jax.experimental import pallas as pl
from jax.experimental.pallas import tpu as pltpu
from jax.sharding import Mesh
from jax.sharding import PartitionSpec as P

adapter_scale = 2.0
PLANE = ("groups", "inner")
LANES = 128
ID_ROWS = 8
AHEAD, SLIGHTLY_AHEAD, SUM_AHEAD = 10**11, 3 * 10**9, 4 * 10**9
BLOCK = 8
IN_VMEM = pl.BlockSpec(memory_space=pltpu.VMEM)
IN_SMEM = pl.BlockSpec(memory_space=pltpu.SMEM)
ANYWHERE = pl.BlockSpec(memory_space=pl.ANY)


def params(scratch_bytes=0):
    return pltpu.CompilerParams(vmem_limit_bytes=(12 << 20) + 2 * scratch_bytes)


def to_partner(value, axes, size, offset):
    return lax.ppermute(value, axes, [(i, i ^ offset) for i in range(size)])


def next_on_ring(block, outer):
    return lax.ppermute(block, "outer", [(i, (i + 1) % outer) for i in range(outer)])


def after(value, *earlier):
    return lax.optimization_barrier((value,) + earlier)[0]


def swap(value):
    return lax.all_to_all(value, PLANE, split_axis=0, concat_axis=0, tiled=True)


def tile_labels(labels_ref, tile, rank, shape):
    per_tile = LANES // rank
    lane = lax.broadcasted_iota(jnp.int32, shape, 1)
    label = jnp.full(shape, labels_ref[tile * per_tile], jnp.int32)
    for n in range(1, per_tile):
        label = jnp.where(lane >= n * rank, labels_ref[tile * per_tile + n], label)
    return label.astype(jnp.float32)


def join_kernel(*refs):
    blocks, out_ref = refs[:-1], refs[-1]
    rows = blocks[0].shape[0]
    for n, block in enumerate(blocks):
        out_ref[n * rows : (n + 1) * rows, :] = block[...]


def joined(blocks, cost):
    rows, share = blocks[0].shape
    return pl.pallas_call(
        join_kernel,
        out_shape=jax.ShapeDtypeStruct((len(blocks) * rows, share), jnp.bfloat16),
        in_specs=[IN_VMEM] * len(blocks),
        out_specs=IN_VMEM,
        compiler_params=params(),
        cost_estimate=pl.CostEstimate(flops=cost, bytes_accessed=10**6, transcendentals=0),
        name="join_blocks",
    )(*blocks)


def outgoing_kernel(hidden_ref, ids_ref, out_ref, sems):
    members, rows, share = out_ref.shape
    tok = rows - ID_ROWS
    copies = [
        pltpu.make_async_copy(
            hidden_ref.at[:, pl.ds(member * share, share)], out_ref.at[member, pl.ds(0, tok)], sems.at[member]
        )
        for member in range(members)
    ]
    for copy in copies:
        copy.start()
    ids = jnp.broadcast_to(ids_ref[...].astype(jnp.float32).astype(jnp.bfloat16), (ID_ROWS, tok))
    for member in range(members):
        out_ref[member, tok:, :tok] = ids
        if share > tok:
            out_ref[member, tok:, tok:] = jnp.zeros((ID_ROWS, share - tok), jnp.bfloat16)
    for copy in copies:
        copy.wait()


def outgoing_rows(hidden, ids, members):
    tok, width = hidden.shape
    share = width // members
    return pl.pallas_call(
        outgoing_kernel,
        out_shape=jax.ShapeDtypeStruct((members, tok + ID_ROWS, share), jnp.bfloat16),
        in_specs=[ANYWHERE, IN_VMEM],
        out_specs=IN_VMEM,
        scratch_shapes=[pltpu.SemaphoreType.DMA((members,))],
        compiler_params=params(),
        name="outgoing_rows",
    )(hidden, ids)


def down_kernel(map_count, rank, labels_ref, rows_ref, *refs):
    maps, (packed_ref, id_rows_ref, total_ref, ids_ref) = refs[:map_count], refs[map_count:]
    members, rows, share = rows_ref.shape
    tok = rows - ID_ROWS
    block = min(BLOCK, members)
    half = tok // 2
    lane = lax.broadcasted_iota(jnp.int32, (half, LANES), 1)

    def one(step, _):
        first = step * block
        for n in range(block):
            row = rows_ref[first + n, tok : tok + 1, :LANES].astype(jnp.float32)
            id_rows_ref[pl.ds(first + n, 1), :] = row
            ids_ref[n] = jnp.broadcast_to(row, (LANES, tok)).T
        tokens = rows_ref[pl.ds(first, block), :tok, :].reshape(block * tok, share)
        ids = ids_ref[...].reshape(block * tok, LANES)
        tile = 0
        for at in range(0, map_count, 2):
            some = jnp.concatenate([m[...] for m in maps[at : at + 2]], axis=0)
            product = lax.dot_general(
                tokens, some, (((1,), (1,)), ((), ())), preferred_element_type=jnp.float32
            )
            total = jnp.zeros((block * tok, LANES), jnp.float32) if tile == 0 else total_ref[...]
            for n in range(some.shape[0] // LANES):
                named = ids == tile_labels(labels_ref, tile, rank, (1, LANES))
                total += jnp.where(named, product[:, n * LANES : (n + 1) * LANES], 0.0)
                tile += 1
            total_ref[...] = total
        for n in range(block):
            total = total_ref[n * tok : (n + 1) * tok, :]
            total += pltpu.roll(total, LANES // 2, 1)
            packed_ref[first + n] = jnp.where(lane < rank, total[:half], total[half:])
        return 0

    lax.fori_loop(0, members // block, one, 0)


def down_product(labels, rows, maps, rank):
    members, tok, share = rows.shape
    tok -= ID_ROWS
    map_rows = sum(m.shape[0] for m in maps)
    return pl.pallas_call(
        functools.partial(down_kernel, len(maps), rank),
        out_shape=[
            jax.ShapeDtypeStruct((members, tok // 2, LANES), jnp.float32),
            jax.ShapeDtypeStruct((members, tok), jnp.float32),
        ],
        in_specs=[IN_SMEM, IN_VMEM] + [IN_VMEM] * len(maps),
        out_specs=[IN_VMEM, IN_VMEM],
        scratch_shapes=[
            pltpu.VMEM((min(BLOCK, members) * tok, LANES), jnp.float32),
            pltpu.VMEM((min(BLOCK, members), tok, LANES), jnp.float32),
        ],
        compiler_params=params(8 * min(BLOCK, members) * tok * LANES),
        cost_estimate=pl.CostEstimate(
            flops=2 * map_rows * members * tok * share,
            bytes_accessed=2 * share * (map_rows + members * tok),
            transcendentals=0,
        ),
        name="down_product",
    )(labels, rows, *maps)


def copies_kernel(terms_ref, out_ref):
    own = jnp.sum(terms_ref[...], axis=0).astype(jnp.bfloat16)
    for member in range(out_ref.shape[0]):
        out_ref[member] = own


def summed_copies(terms):
    return pl.pallas_call(
        copies_kernel,
        out_shape=jax.ShapeDtypeStruct(terms.shape, jnp.bfloat16),
        in_specs=[IN_VMEM],
        out_specs=IN_VMEM,
        compiler_params=params(),
        cost_estimate=pl.CostEstimate(flops=SUM_AHEAD, bytes_accessed=10**6, transcendentals=0),
        name="summed_copies",
    )(terms)


def up_kernel(map_count, rank, labels_ref, me_ref, ids_ref, shrunk_ref, *refs):
    members, half, _ = shrunk_ref.shape
    maps, outs = refs[:map_count], refs[map_count : map_count + members]
    spread_ref = refs[-1]
    tok = 2 * half
    block = min(BLOCK, members)
    tiles = spread_ref.shape[1] // LANES
    lane = lax.broadcasted_iota(jnp.int32, (half, LANES), 1)
    held = jnp.concatenate([m[...] for m in maps], axis=0)
    for first in range(0, members, block):
        for n in range(block):
            member = me_ref[0] ^ (first + n)
            packed = shrunk_ref[member].astype(jnp.float32)
            turned = pltpu.roll(packed, LANES // 2, 1)
            shrunk = jnp.concatenate(
                [jnp.where(lane < rank, packed, turned), jnp.where(lane < rank, turned, packed)], axis=0
            )
            ids = jnp.broadcast_to(ids_ref[pl.ds(member, 1), :], (LANES, tok)).T
            for tile in range(tiles):
                named = ids == tile_labels(labels_ref, tile, rank, (1, LANES))
                spread_ref[n * tok : (n + 1) * tok, tile * LANES : (tile + 1) * LANES] = jnp.where(
                    named, shrunk, 0.0
                ).astype(jnp.bfloat16)
        product = jnp.dot(spread_ref[...], held, preferred_element_type=jnp.float32)
        product = (adapter_scale * product).astype(jnp.bfloat16)
        for n in range(block):
            outs[first + n][...] = product[n * tok : (n + 1) * tok, :]


def up_product(labels, me, ids, shrunk, maps, rank):
    members, tok = ids.shape
    map_rows, piece = sum(m.shape[0] for m in maps), maps[0].shape[1]
    return pl.pallas_call(
        functools.partial(up_kernel, len(maps), rank),
        out_shape=[jax.ShapeDtypeStruct((tok, piece), jnp.bfloat16)] * members,
        in_specs=[IN_SMEM, IN_SMEM, IN_VMEM, IN_VMEM] + [IN_VMEM] * len(maps),
        out_specs=[IN_VMEM] * members,
        scratch_shapes=[pltpu.VMEM((min(BLOCK, members) * tok, map_rows), jnp.bfloat16)],
        compiler_params=params(2 * min(BLOCK, members) * tok * map_rows),
        cost_estimate=pl.CostEstimate(
            flops=2 * map_rows * members * tok * piece,
            bytes_accessed=2 * piece * (map_rows + members * tok),
            transcendentals=0,
        ),
        name="up_product",
    )(labels, me, ids, shrunk, *maps)


def place_kernel(me_ref, *refs):
    blocks, out_ref, sems = refs[:-2], refs[-2], refs[-1]
    share = blocks[0].shape[1]
    copies = []
    for offset, block in enumerate(blocks):
        at = pl.multiple_of((me_ref[0] ^ offset) * share, LANES)
        copies.append(pltpu.make_async_copy(block, out_ref.at[:, pl.ds(at, share)], sems.at[offset]))
    for copy in copies:
        copy.start()
    for copy in copies:
        copy.wait()


def place(me, blocks):
    tok, share = blocks[0].shape
    return pl.pallas_call(
        place_kernel,
        out_shape=jax.ShapeDtypeStruct((tok, len(blocks) * share), jnp.bfloat16),
        in_specs=[IN_SMEM] + [ANYWHERE] * len(blocks),
        out_specs=ANYWHERE,
        scratch_shapes=[pltpu.SemaphoreType.DMA((len(blocks),))],
        compiler_params=params(),
        name="place_results",
    )(me, *blocks)


def per_device(token_adapter_index, hidden, adapter_down_maps, adapter_up_maps):
    tok, width = hidden.shape
    groups, outer, inner = (lax.axis_size(a) for a in ("groups", "outer", "inner"))
    group, level, place_in_group = (lax.axis_index(a) for a in ("groups", "outer", "inner"))
    members = groups * inner
    share = width // members
    rank = adapter_up_maps.shape[1]
    me = group * inner + place_in_group

    def slices(array):
        return [
            lax.dynamic_slice_in_dim(array, (me ^ offset) * share, share, axis=1) for offset in range(inner)
        ]

    def exchanged(blocks):
        return blocks[:1] + [to_partner(blocks[n], "inner", inner, n) for n in range(1, inner)]

    def rings(near, far, first_cost=0, second_after=()):
        near, far = [near], [far]
        for step in range(1, outer):
            for blocks in near, far:
                block = blocks[-1]
                if step == 2:
                    block = after(block, *second_after)
                    if first_cost:
                        block = joined([block], first_cost)
                blocks.append(next_on_ring(block, outer))
        return near, far

    steps_back = jnp.arange(outer, dtype=jnp.int32)[:, None]
    labels = ((level - steps_back + outer) % outer) * inner + (
        place_in_group ^ jnp.arange(inner, dtype=jnp.int32)[None, :]
    )
    labels = labels.reshape(-1)

    middle = inner // 2
    down = exchanged(slices(adapter_down_maps[0].T))
    down_near, down_far = rings(joined(down[:middle], AHEAD), joined(down[middle:], AHEAD), first_cost=SLIGHTLY_AHEAD)
    ids = token_adapter_index.reshape(1, tok)
    rows = swap(after(outgoing_rows(hidden, ids, members), down_near[0]))
    up = exchanged([after(block, down_near[1]) for block in slices(adapter_up_maps[0])])

    down_maps = [m for pair in zip(down_near, down_far) for m in pair]
    packed, id_rows = down_product(labels, rows, down_maps, rank)
    up_near, up_far = rings(
        after(jnp.concatenate(up[:middle], axis=0), down_near[-1]),
        after(jnp.concatenate(up[middle:], axis=0), down_far[-1]),
        second_after=[packed],
    )
    up_maps = [m for pair in zip(up_near, up_far) for m in pair]
    shrunk = swap(summed_copies(swap(packed)))
    results = list(up_product(labels, me.reshape(1), id_rows, shrunk, up_maps, rank))
    order = sorted(range(1, members), key=lambda n: (-(n >= inner) - (n % inner >= 2), -(n >= inner), n))
    returned = {n: to_partner(results[n], PLANE, members, n) for n in order}
    return place(me.reshape(1), results[:1] + [returned[n] for n in range(1, members)])


def solution(mesh):
    groups, wide = mesh.shape["groups"], mesh.shape["wide"]
    outer = 1 << ((wide.bit_length() - 1) // 2)
    fine = Mesh(mesh.devices.reshape(groups, outer, wide // outer), ("groups", "outer", "inner"))
    owner = ("outer", "inner")
    rows = P(("groups",) + owner, None)
    return jax.shard_map(
        per_device,
        mesh=fine,
        in_specs=(rows, rows, P(owner, None, None), P(owner, None, None)),
        out_specs=rows,
        check_vma=False,
    )
```

```python
import functools

import jax
import jax.numpy as jnp
from jax import lax
from jax.experimental import pallas as pl
from jax.experimental.pallas import tpu as pltpu
from jax.sharding import Mesh
from jax.sharding import PartitionSpec as P

adapter_scale = 2.0
PLANE = ("groups", "inner")
LANES = 128
ID_ROWS = 8
AHEAD, SLIGHTLY_AHEAD, SUM_AHEAD = 10**11, 3 * 10**9, 8 * 10**9
BLOCK = 8
IN_VMEM = pl.BlockSpec(memory_space=pltpu.VMEM)
IN_SMEM = pl.BlockSpec(memory_space=pltpu.SMEM)
ANYWHERE = pl.BlockSpec(memory_space=pl.ANY)


def params(scratch_bytes=0):
    return pltpu.CompilerParams(vmem_limit_bytes=(12 << 20) + 2 * scratch_bytes)


def to_partner(value, axes, size, offset):
    return lax.ppermute(value, axes, [(i, i ^ offset) for i in range(size)])


def next_on_ring(block, outer):
    return lax.ppermute(block, "outer", [(i, (i + 1) % outer) for i in range(outer)])


def after(value, *earlier):
    return lax.optimization_barrier((value,) + earlier)[0]


def swap(value):
    return lax.all_to_all(value, PLANE, split_axis=0, concat_axis=0, tiled=True)


def tile_labels(labels_ref, tile, rank, shape):
    per_tile = LANES // rank
    lane = lax.broadcasted_iota(jnp.int32, shape, 1)
    label = jnp.full(shape, labels_ref[tile * per_tile], jnp.int32)
    for n in range(1, per_tile):
        label = jnp.where(lane >= n * rank, labels_ref[tile * per_tile + n], label)
    return label.astype(jnp.float32)


def join_kernel(first, *refs):
    blocks, out_ref = refs[:-1], refs[-1]
    rows = out_ref.shape[0] // len(blocks)
    for n, block in enumerate(blocks):
        out_ref[n * rows : (n + 1) * rows, :] = block[first : first + rows, :]


def joined(blocks, first, rows, cost):
    share = blocks[0].shape[1]
    return pl.pallas_call(
        functools.partial(join_kernel, first),
        out_shape=jax.ShapeDtypeStruct((len(blocks) * rows, share), jnp.bfloat16),
        in_specs=[IN_VMEM] * len(blocks),
        out_specs=IN_VMEM,
        compiler_params=params(),
        cost_estimate=pl.CostEstimate(flops=cost, bytes_accessed=10**6, transcendentals=0),
        name="join_blocks",
    )(*blocks)


def outgoing_kernel(hidden_ref, ids_ref, out_ref, sems):
    members, rows, share = out_ref.shape
    tok = rows - ID_ROWS
    copies = [
        pltpu.make_async_copy(
            hidden_ref.at[:, pl.ds(member * share, share)], out_ref.at[member, pl.ds(0, tok)], sems.at[member]
        )
        for member in range(members)
    ]
    for copy in copies:
        copy.start()
    ids = jnp.broadcast_to(ids_ref[...].astype(jnp.float32).astype(jnp.bfloat16), (ID_ROWS, tok))
    for member in range(members):
        out_ref[member, tok:, :tok] = ids
        if share > tok:
            out_ref[member, tok:, tok:] = jnp.zeros((ID_ROWS, share - tok), jnp.bfloat16)
    for copy in copies:
        copy.wait()


def outgoing_rows(hidden, ids, members):
    tok, width = hidden.shape
    share = width // members
    return pl.pallas_call(
        outgoing_kernel,
        out_shape=jax.ShapeDtypeStruct((members, tok + ID_ROWS, share), jnp.bfloat16),
        in_specs=[ANYWHERE, IN_VMEM],
        out_specs=IN_VMEM,
        scratch_shapes=[pltpu.SemaphoreType.DMA((members,))],
        compiler_params=params(),
        name="outgoing_rows",
    )(hidden, ids)


def down_kernel(map_count, rank, labels_ref, rows_ref, *refs):
    maps, (packed_ref, id_rows_ref, total_ref, ids_ref) = refs[:map_count], refs[map_count:]
    members, rows, share = rows_ref.shape
    tok = rows - ID_ROWS
    block = min(BLOCK, members)
    half = tok // 2
    lane = lax.broadcasted_iota(jnp.int32, (half, LANES), 1)

    def one(step, _):
        first = step * block
        for n in range(block):
            row = rows_ref[first + n, tok : tok + 1, :LANES].astype(jnp.float32)
            id_rows_ref[pl.ds(first + n, 1), :] = row
            ids_ref[n] = jnp.broadcast_to(row, (LANES, tok)).T
        tokens = rows_ref[pl.ds(first, block), :tok, :].reshape(block * tok, share)
        ids = ids_ref[...].reshape(block * tok, LANES)
        tile = 0
        for at in range(0, map_count, 2):
            some = jnp.concatenate([m[...] for m in maps[at : at + 2]], axis=0)
            product = lax.dot_general(
                tokens, some, (((1,), (1,)), ((), ())), preferred_element_type=jnp.float32
            )
            total = jnp.zeros((block * tok, LANES), jnp.float32) if tile == 0 else total_ref[...]
            for n in range(some.shape[0] // LANES):
                named = ids == tile_labels(labels_ref, tile, rank, (1, LANES))
                total += jnp.where(named, product[:, n * LANES : (n + 1) * LANES], 0.0)
                tile += 1
            total_ref[...] = total
        for n in range(block):
            total = total_ref[n * tok : (n + 1) * tok, :]
            total += pltpu.roll(total, LANES // 2, 1)
            packed_ref[first + n] = jnp.where(lane < rank, total[:half], total[half:])
        return 0

    lax.fori_loop(0, members // block, one, 0)


def down_product(labels, rows, maps, rank):
    members, tok, share = rows.shape
    tok -= ID_ROWS
    map_rows = sum(m.shape[0] for m in maps)
    return pl.pallas_call(
        functools.partial(down_kernel, len(maps), rank),
        out_shape=[
            jax.ShapeDtypeStruct((members, tok // 2, LANES), jnp.float32),
            jax.ShapeDtypeStruct((members, tok), jnp.float32),
        ],
        in_specs=[IN_SMEM, IN_VMEM] + [IN_VMEM] * len(maps),
        out_specs=[IN_VMEM, IN_VMEM],
        scratch_shapes=[
            pltpu.VMEM((min(BLOCK, members) * tok, LANES), jnp.float32),
            pltpu.VMEM((min(BLOCK, members), tok, LANES), jnp.float32),
        ],
        compiler_params=params(8 * min(BLOCK, members) * tok * LANES),
        cost_estimate=pl.CostEstimate(
            flops=2 * map_rows * members * tok * share,
            bytes_accessed=2 * share * (map_rows + members * tok),
            transcendentals=0,
        ),
        name="down_product",
    )(labels, rows, *maps)


def copies_kernel(terms_ref, out_ref):
    own = jnp.sum(terms_ref[...], axis=0).astype(jnp.bfloat16)
    for member in range(out_ref.shape[0]):
        out_ref[member] = own


def summed_copies(terms):
    return pl.pallas_call(
        copies_kernel,
        out_shape=jax.ShapeDtypeStruct(terms.shape, jnp.bfloat16),
        in_specs=[IN_VMEM],
        out_specs=IN_VMEM,
        compiler_params=params(),
        cost_estimate=pl.CostEstimate(flops=SUM_AHEAD, bytes_accessed=10**6, transcendentals=0),
        name="summed_copies",
    )(terms)


def up_kernel(map_count, rank, labels_ref, me_ref, ids_ref, shrunk_ref, *refs):
    members, half, _ = shrunk_ref.shape
    maps, outs = refs[:map_count], refs[map_count : map_count + members]
    spread_ref = refs[-1]
    tok = 2 * half
    block = min(BLOCK, members)
    tiles = spread_ref.shape[1] // LANES
    lane = lax.broadcasted_iota(jnp.int32, (half, LANES), 1)
    held = jnp.concatenate([m[...] for m in maps], axis=0)
    for first in range(0, members, block):
        for n in range(block):
            member = me_ref[0] ^ (first + n)
            packed = shrunk_ref[member].astype(jnp.float32)
            turned = pltpu.roll(packed, LANES // 2, 1)
            shrunk = jnp.concatenate(
                [jnp.where(lane < rank, packed, turned), jnp.where(lane < rank, turned, packed)], axis=0
            )
            ids = jnp.broadcast_to(ids_ref[pl.ds(member, 1), :], (LANES, tok)).T
            for tile in range(tiles):
                named = ids == tile_labels(labels_ref, tile, rank, (1, LANES))
                spread_ref[n * tok : (n + 1) * tok, tile * LANES : (tile + 1) * LANES] = jnp.where(
                    named, shrunk, 0.0
                ).astype(jnp.bfloat16)
        product = jnp.dot(spread_ref[...], held, preferred_element_type=jnp.float32)
        product = (adapter_scale * product).astype(jnp.bfloat16)
        for n in range(block):
            outs[first + n][...] = product[n * tok : (n + 1) * tok, :]


def up_product(labels, me, ids, shrunk, maps, rank):
    members, tok = ids.shape
    map_rows, piece = sum(m.shape[0] for m in maps), maps[0].shape[1]
    return pl.pallas_call(
        functools.partial(up_kernel, len(maps), rank),
        out_shape=[jax.ShapeDtypeStruct((tok, piece), jnp.bfloat16)] * members,
        in_specs=[IN_SMEM, IN_SMEM, IN_VMEM, IN_VMEM] + [IN_VMEM] * len(maps),
        out_specs=[IN_VMEM] * members,
        scratch_shapes=[pltpu.VMEM((min(BLOCK, members) * tok, map_rows), jnp.bfloat16)],
        compiler_params=params(2 * min(BLOCK, members) * tok * map_rows),
        cost_estimate=pl.CostEstimate(
            flops=2 * map_rows * members * tok * piece,
            bytes_accessed=2 * piece * (map_rows + members * tok),
            transcendentals=0,
        ),
        name="up_product",
    )(labels, me, ids, shrunk, *maps)


def place_kernel(offsets, me_ref, *refs):
    blocks, out_ref, sems = refs[:-2], refs[-2], refs[-1]
    share = blocks[0].shape[1]
    copies = []
    for n, block in enumerate(blocks):
        at = pl.multiple_of((me_ref[0] ^ offsets[n]) * share, LANES)
        copies.append(pltpu.make_async_copy(block, out_ref.at[:, pl.ds(at, share)], sems.at[n]))
    for copy in copies:
        copy.start()
    for copy in copies:
        copy.wait()


def place(me, offsets, blocks):
    tok, share = blocks[0].shape
    return pl.pallas_call(
        functools.partial(place_kernel, offsets),
        out_shape=jax.ShapeDtypeStruct((tok, len(blocks) * share), jnp.bfloat16),
        in_specs=[IN_SMEM] + [ANYWHERE] * len(blocks),
        out_specs=ANYWHERE,
        scratch_shapes=[pltpu.SemaphoreType.DMA((len(blocks),))],
        compiler_params=params(),
        name="place_results",
    )(me, *blocks)


def per_device(token_adapter_index, hidden, adapter_down_maps, adapter_up_maps):
    tok, width = hidden.shape
    groups, outer, inner = (lax.axis_size(a) for a in ("groups", "outer", "inner"))
    group, level, place_in_group = (lax.axis_index(a) for a in ("groups", "outer", "inner"))
    members = groups * inner
    share = width // members
    rank = adapter_up_maps.shape[1]
    me = group * inner + place_in_group

    def slices(offset):
        start = (me ^ offset) * share
        return jnp.concatenate(
            [
                lax.dynamic_slice_in_dim(adapter_down_maps[0].T, start, share, axis=1),
                lax.dynamic_slice_in_dim(adapter_up_maps[0], start, share, axis=1),
            ],
            axis=0,
        )

    got = [slices(0)] + [to_partner(slices(n), "inner", inner, n) for n in range(1, inner)]

    def rings(near, far, first_cost=0, second_after=()):
        near, far = [near], [far]
        for step in range(1, outer):
            for blocks in near, far:
                block = blocks[-1]
                if step == 2:
                    block = after(block, *second_after)
                    if first_cost:
                        block = joined([block], 0, block.shape[0], first_cost)
                blocks.append(next_on_ring(block, outer))
        return near, far

    steps_back = jnp.arange(outer, dtype=jnp.int32)[:, None]
    labels = ((level - steps_back + outer) % outer) * inner + (
        place_in_group ^ jnp.arange(inner, dtype=jnp.int32)[None, :]
    )
    labels = labels.reshape(-1)

    middle = inner // 2
    down_near, down_far = rings(
        joined(got[:middle], 0, rank, AHEAD), joined(got[middle:], 0, rank, AHEAD), first_cost=SLIGHTLY_AHEAD
    )
    ids = token_adapter_index.reshape(1, tok)
    rows = swap(after(outgoing_rows(hidden, ids, members), down_near[0]))

    down_maps = [m for pair in zip(down_near, down_far) for m in pair]
    packed, id_rows = down_product(labels, rows, down_maps, rank)
    up_near, up_far = rings(
        after(jnp.concatenate([g[rank:] for g in got[:middle]], axis=0), down_near[-1]),
        after(jnp.concatenate([g[rank:] for g in got[middle:]], axis=0), down_far[-1]),
        second_after=[packed],
    )
    up_maps = [m for pair in zip(up_near, up_far) for m in pair]
    shrunk = swap(summed_copies(swap(packed)))
    results = list(up_product(labels, me.reshape(1), id_rows, shrunk, up_maps, rank))
    offsets = sorted(range(1, members), key=lambda n: (-(n >= inner) - (n % inner >= 2), -(n >= inner), n))
    returned = [to_partner(results[n], PLANE, members, n) for n in offsets]
    return place(me.reshape(1), offsets + [0], returned + results[:1])


def solution(mesh):
    groups, wide = mesh.shape["groups"], mesh.shape["wide"]
    outer = 1 << ((wide.bit_length() - 1) // 2)
    fine = Mesh(mesh.devices.reshape(groups, outer, wide // outer), ("groups", "outer", "inner"))
    owner = ("outer", "inner")
    rows = P(("groups",) + owner, None)
    return jax.shard_map(
        per_device,
        mesh=fine,
        in_specs=(rows, rows, P(owner, None, None), P(owner, None, None)),
        out_specs=rows,
        check_vma=False,
    )
```

```python
import functools

import jax
import jax.numpy as jnp
from jax import lax
from jax.experimental import pallas as pl
from jax.experimental.pallas import tpu as pltpu
from jax.sharding import Mesh
from jax.sharding import PartitionSpec as P

adapter_scale = 2.0
PLANE = ("groups", "inner")
LANES = 128
ID_ROWS = 8
AHEAD, SLIGHTLY_AHEAD = 10**11, 6 * 10**9
BLOCK = 8
IN_VMEM = pl.BlockSpec(memory_space=pltpu.VMEM)
IN_SMEM = pl.BlockSpec(memory_space=pltpu.SMEM)
ANYWHERE = pl.BlockSpec(memory_space=pl.ANY)


def params(scratch_bytes=0):
    return pltpu.CompilerParams(vmem_limit_bytes=(12 << 20) + 2 * scratch_bytes)


def to_partner(value, axes, size, offset):
    return lax.ppermute(value, axes, [(i, i ^ offset) for i in range(size)])


def next_on_ring(block, outer):
    return lax.ppermute(block, "outer", [(i, (i + 1) % outer) for i in range(outer)])


def after(value, *earlier):
    return lax.optimization_barrier((value,) + earlier)[0]


def swap(value):
    return lax.all_to_all(value, PLANE, split_axis=0, concat_axis=0, tiled=True)


def tile_labels(labels_ref, tile, rank, shape):
    per_tile = LANES // rank
    lane = lax.broadcasted_iota(jnp.int32, shape, 1)
    label = jnp.full(shape, labels_ref[tile * per_tile], jnp.int32)
    for n in range(1, per_tile):
        label = jnp.where(lane >= n * rank, labels_ref[tile * per_tile + n], label)
    return label.astype(jnp.float32)


def join_kernel(*refs):
    blocks, out_ref = refs[:-1], refs[-1]
    rows = blocks[0].shape[0]
    for n, block in enumerate(blocks):
        out_ref[n * rows : (n + 1) * rows, :] = block[...]


def joined(blocks, cost):
    rows, share = blocks[0].shape
    return pl.pallas_call(
        join_kernel,
        out_shape=jax.ShapeDtypeStruct((len(blocks) * rows, share), jnp.bfloat16),
        in_specs=[IN_VMEM] * len(blocks),
        out_specs=IN_VMEM,
        compiler_params=params(),
        cost_estimate=pl.CostEstimate(flops=cost, bytes_accessed=10**6, transcendentals=0),
        name="join_blocks",
    )(*blocks)


def outgoing_kernel(hidden_ref, ids_ref, out_ref, sems):
    members, rows, share = out_ref.shape
    tok = rows - ID_ROWS
    copies = [
        pltpu.make_async_copy(
            hidden_ref.at[:, pl.ds(member * share, share)], out_ref.at[member, pl.ds(0, tok)], sems.at[member]
        )
        for member in range(members)
    ]
    for copy in copies:
        copy.start()
    ids = jnp.broadcast_to(ids_ref[...].astype(jnp.float32).astype(jnp.bfloat16), (ID_ROWS, tok))
    for member in range(members):
        out_ref[member, tok:, :tok] = ids
        if share > tok:
            out_ref[member, tok:, tok:] = jnp.zeros((ID_ROWS, share - tok), jnp.bfloat16)
    for copy in copies:
        copy.wait()


def outgoing_rows(hidden, ids, members):
    tok, width = hidden.shape
    share = width // members
    return pl.pallas_call(
        outgoing_kernel,
        out_shape=jax.ShapeDtypeStruct((members, tok + ID_ROWS, share), jnp.bfloat16),
        in_specs=[ANYWHERE, IN_VMEM],
        out_specs=IN_VMEM,
        scratch_shapes=[pltpu.SemaphoreType.DMA((members,))],
        compiler_params=params(),
        name="outgoing_rows",
    )(hidden, ids)


def down_kernel(map_count, rank, labels_ref, rows_ref, *refs):
    maps, (packed_ref, id_rows_ref, total_ref, ids_ref) = refs[:map_count], refs[map_count:]
    members, rows, share = rows_ref.shape
    tok = rows - ID_ROWS
    block = min(BLOCK, members)
    half = tok // 2
    lane = lax.broadcasted_iota(jnp.int32, (half, LANES), 1)

    def one(step, _):
        first = step * block
        for n in range(block):
            row = rows_ref[first + n, tok : tok + 1, :LANES].astype(jnp.float32)
            id_rows_ref[pl.ds(first + n, 1), :] = row
            ids_ref[n] = jnp.broadcast_to(row, (LANES, tok)).T
        tokens = rows_ref[pl.ds(first, block), :tok, :].reshape(block * tok, share)
        ids = ids_ref[...].reshape(block * tok, LANES)
        tile = 0
        for at in range(0, map_count, 2):
            some = jnp.concatenate([m[...] for m in maps[at : at + 2]], axis=0)
            product = lax.dot_general(
                tokens, some, (((1,), (1,)), ((), ())), preferred_element_type=jnp.float32
            )
            total = jnp.zeros((block * tok, LANES), jnp.float32) if tile == 0 else total_ref[...]
            for n in range(some.shape[0] // LANES):
                named = ids == tile_labels(labels_ref, tile, rank, (1, LANES))
                total += jnp.where(named, product[:, n * LANES : (n + 1) * LANES], 0.0)
                tile += 1
            total_ref[...] = total
        for n in range(block):
            total = total_ref[n * tok : (n + 1) * tok, :]
            total += pltpu.roll(total, LANES // 2, 1)
            packed_ref[first + n] = jnp.where(lane < rank, total[:half], total[half:])
        return 0

    lax.fori_loop(0, members // block, one, 0)


def down_product(labels, rows, maps, rank):
    members, tok, share = rows.shape
    tok -= ID_ROWS
    map_rows = sum(m.shape[0] for m in maps)
    return pl.pallas_call(
        functools.partial(down_kernel, len(maps), rank),
        out_shape=[
            jax.ShapeDtypeStruct((members, tok // 2, LANES), jnp.float32),
            jax.ShapeDtypeStruct((members, tok), jnp.float32),
        ],
        in_specs=[IN_SMEM, IN_VMEM] + [IN_VMEM] * len(maps),
        out_specs=[IN_VMEM, IN_VMEM],
        scratch_shapes=[
            pltpu.VMEM((min(BLOCK, members) * tok, LANES), jnp.float32),
            pltpu.VMEM((min(BLOCK, members), tok, LANES), jnp.float32),
        ],
        compiler_params=params(8 * min(BLOCK, members) * tok * LANES),
        cost_estimate=pl.CostEstimate(
            flops=2 * map_rows * members * tok * share,
            bytes_accessed=2 * share * (map_rows + members * tok),
            transcendentals=0,
        ),
        name="down_product",
    )(labels, rows, *maps)


def copies_kernel(terms_ref, out_ref):
    own = jnp.sum(terms_ref[...], axis=0).astype(jnp.bfloat16)
    for member in range(out_ref.shape[0]):
        out_ref[member] = own


def summed_copies(terms):
    return pl.pallas_call(
        copies_kernel,
        out_shape=jax.ShapeDtypeStruct(terms.shape, jnp.bfloat16),
        in_specs=[IN_VMEM],
        out_specs=IN_VMEM,
        compiler_params=params(),
        name="summed_copies",
    )(terms)


def up_kernel(map_count, rank, labels_ref, me_ref, ids_ref, shrunk_ref, *refs):
    members, half, _ = shrunk_ref.shape
    maps, outs = refs[:map_count], refs[map_count : map_count + members]
    spread_ref = refs[-1]
    tok = 2 * half
    block = min(BLOCK, members)
    tiles = spread_ref.shape[1] // LANES
    lane = lax.broadcasted_iota(jnp.int32, (half, LANES), 1)
    held = jnp.concatenate([m[...] for m in maps], axis=0)
    for first in range(0, members, block):
        for n in range(block):
            member = me_ref[0] ^ (first + n)
            packed = shrunk_ref[member].astype(jnp.float32)
            turned = pltpu.roll(packed, LANES // 2, 1)
            shrunk = jnp.concatenate(
                [jnp.where(lane < rank, packed, turned), jnp.where(lane < rank, turned, packed)], axis=0
            )
            ids = jnp.broadcast_to(ids_ref[pl.ds(member, 1), :], (LANES, tok)).T
            for tile in range(tiles):
                named = ids == tile_labels(labels_ref, tile, rank, (1, LANES))
                spread_ref[n * tok : (n + 1) * tok, tile * LANES : (tile + 1) * LANES] = jnp.where(
                    named, shrunk, 0.0
                ).astype(jnp.bfloat16)
        product = jnp.dot(spread_ref[...], held, preferred_element_type=jnp.float32)
        product = (adapter_scale * product).astype(jnp.bfloat16)
        for n in range(block):
            outs[first + n][...] = product[n * tok : (n + 1) * tok, :]


def up_product(labels, me, ids, shrunk, maps, rank):
    members, tok = ids.shape
    map_rows, piece = sum(m.shape[0] for m in maps), maps[0].shape[1]
    return pl.pallas_call(
        functools.partial(up_kernel, len(maps), rank),
        out_shape=[jax.ShapeDtypeStruct((tok, piece), jnp.bfloat16)] * members,
        in_specs=[IN_SMEM, IN_SMEM, IN_VMEM, IN_VMEM] + [IN_VMEM] * len(maps),
        out_specs=[IN_VMEM] * members,
        scratch_shapes=[pltpu.VMEM((min(BLOCK, members) * tok, map_rows), jnp.bfloat16)],
        compiler_params=params(2 * min(BLOCK, members) * tok * map_rows),
        cost_estimate=pl.CostEstimate(
            flops=2 * map_rows * members * tok * piece,
            bytes_accessed=2 * piece * (map_rows + members * tok),
            transcendentals=0,
        ),
        name="up_product",
    )(labels, me, ids, shrunk, *maps)


def place_kernel(offsets, me_ref, *refs):
    blocks, out_ref, sems = refs[:-2], refs[-2], refs[-1]
    share = blocks[0].shape[1]
    copies = []
    for n, block in enumerate(blocks):
        at = pl.multiple_of((me_ref[0] ^ offsets[n]) * share, LANES)
        copies.append(pltpu.make_async_copy(block, out_ref.at[:, pl.ds(at, share)], sems.at[n]))
    for copy in copies:
        copy.start()
    for copy in copies:
        copy.wait()


def place(me, offsets, blocks):
    tok, share = blocks[0].shape
    return pl.pallas_call(
        functools.partial(place_kernel, offsets),
        out_shape=jax.ShapeDtypeStruct((tok, len(blocks) * share), jnp.bfloat16),
        in_specs=[IN_SMEM] + [ANYWHERE] * len(blocks),
        out_specs=ANYWHERE,
        scratch_shapes=[pltpu.SemaphoreType.DMA((len(blocks),))],
        compiler_params=params(),
        name="place_results",
    )(me, *blocks)


def per_device(token_adapter_index, hidden, adapter_down_maps, adapter_up_maps):
    tok, width = hidden.shape
    groups, outer, inner = (lax.axis_size(a) for a in ("groups", "outer", "inner"))
    group, level, place_in_group = (lax.axis_index(a) for a in ("groups", "outer", "inner"))
    members = groups * inner
    share = width // members
    rank = adapter_up_maps.shape[1]
    me = group * inner + place_in_group

    def slices(array):
        return [
            lax.dynamic_slice_in_dim(array, (me ^ offset) * share, share, axis=1) for offset in range(inner)
        ]

    def exchanged(blocks):
        return blocks[:1] + [to_partner(blocks[n], "inner", inner, n) for n in range(1, inner)]

    def rings(near, far, first_cost=0):
        near, far = [near], [far]
        for step in range(1, outer):
            for blocks in near, far:
                block = blocks[-1]
                if step == 2 and first_cost:
                    block = joined([block], first_cost)
                blocks.append(next_on_ring(block, outer))
        return near, far

    steps_back = jnp.arange(outer, dtype=jnp.int32)[:, None]
    labels = ((level - steps_back + outer) % outer) * inner + (
        place_in_group ^ jnp.arange(inner, dtype=jnp.int32)[None, :]
    )
    labels = labels.reshape(-1)

    middle = inner // 2
    down = exchanged(slices(adapter_down_maps[0].T))
    down_near, down_far = rings(joined(down[:middle], AHEAD), joined(down[middle:], AHEAD), first_cost=SLIGHTLY_AHEAD)
    ids = token_adapter_index.reshape(1, tok)
    rows = swap(outgoing_rows(after(hidden, down_near[0]), ids, members))
    up = exchanged([after(block, down_near[1]) for block in slices(adapter_up_maps[0])])

    down_maps = [m for pair in zip(down_near, down_far) for m in pair]
    packed, id_rows = down_product(labels, rows, down_maps, rank)
    up_near, up_far = rings(
        after(jnp.concatenate(up[:middle], axis=0), down_near[-1]),
        after(jnp.concatenate(up[middle:], axis=0), down_far[-1], packed),
    )
    up_maps = [m for pair in zip(up_near, up_far) for m in pair]
    shrunk = swap(summed_copies(swap(packed)))
    results = list(up_product(labels, me.reshape(1), id_rows, shrunk, up_maps, rank))
    offsets = sorted(range(1, members), key=lambda n: (-(n >= inner) - (n % inner >= 2), -(n >= inner), n))
    returned = [to_partner(results[n], PLANE, members, n) for n in offsets]
    return place(me.reshape(1), offsets + [0], returned + results[:1])


def solution(mesh):
    groups, wide = mesh.shape["groups"], mesh.shape["wide"]
    outer = 1 << ((wide.bit_length() - 1) // 2)
    fine = Mesh(mesh.devices.reshape(groups, outer, wide // outer), ("groups", "outer", "inner"))
    owner = ("outer", "inner")
    rows = P(("groups",) + owner, None)
    return jax.shard_map(
        per_device,
        mesh=fine,
        in_specs=(rows, rows, P(owner, None, None), P(owner, None, None)),
        out_specs=rows,
        check_vma=False,
    )
```

```python
import functools

import jax
import jax.numpy as jnp
from jax import lax
from jax.experimental import pallas as pl
from jax.experimental.pallas import tpu as pltpu
from jax.sharding import Mesh
from jax.sharding import PartitionSpec as P

adapter_scale = 2.0
PLANE = ("groups", "inner")
LANES = 128
ID_ROWS = 8
AHEAD, SLIGHTLY_AHEAD = 10**11, 6 * 10**9
BLOCK = 8
IN_VMEM = pl.BlockSpec(memory_space=pltpu.VMEM)
IN_SMEM = pl.BlockSpec(memory_space=pltpu.SMEM)
ANYWHERE = pl.BlockSpec(memory_space=pl.ANY)


def params(scratch_bytes=0):
    return pltpu.CompilerParams(vmem_limit_bytes=(12 << 20) + 2 * scratch_bytes)


def to_partner(value, axes, size, offset):
    return lax.ppermute(value, axes, [(i, i ^ offset) for i in range(size)])


def next_on_ring(block, outer):
    return lax.ppermute(block, "outer", [(i, (i + 1) % outer) for i in range(outer)])


def after(value, *earlier):
    return lax.optimization_barrier((value,) + earlier)[0]


def swap(value):
    return lax.all_to_all(value, PLANE, split_axis=0, concat_axis=0, tiled=True)


def tile_labels(labels_ref, tile, rank, shape):
    per_tile = LANES // rank
    lane = lax.broadcasted_iota(jnp.int32, shape, 1)
    label = jnp.full(shape, labels_ref[tile * per_tile], jnp.int32)
    for n in range(1, per_tile):
        label = jnp.where(lane >= n * rank, labels_ref[tile * per_tile + n], label)
    return label.astype(jnp.float32)


def join_kernel(*refs):
    blocks, out_ref = refs[:-1], refs[-1]
    rows = blocks[0].shape[0]
    for n, block in enumerate(blocks):
        out_ref[n * rows : (n + 1) * rows, :] = block[...]


def joined(blocks, cost):
    rows, share = blocks[0].shape
    return pl.pallas_call(
        join_kernel,
        out_shape=jax.ShapeDtypeStruct((len(blocks) * rows, share), jnp.bfloat16),
        in_specs=[IN_VMEM] * len(blocks),
        out_specs=IN_VMEM,
        compiler_params=params(),
        cost_estimate=pl.CostEstimate(flops=cost, bytes_accessed=10**6, transcendentals=0),
        name="join_blocks",
    )(*blocks)


def outgoing_kernel(hidden_ref, ids_ref, out_ref, sems):
    members, rows, share = out_ref.shape
    tok = rows - ID_ROWS
    copies = [
        pltpu.make_async_copy(
            hidden_ref.at[:, pl.ds(member * share, share)], out_ref.at[member, pl.ds(0, tok)], sems.at[member]
        )
        for member in range(members)
    ]
    for copy in copies:
        copy.start()
    ids = jnp.broadcast_to(ids_ref[...].astype(jnp.float32).astype(jnp.bfloat16), (ID_ROWS, tok))
    for member in range(members):
        out_ref[member, tok:, :tok] = ids
        if share > tok:
            out_ref[member, tok:, tok:] = jnp.zeros((ID_ROWS, share - tok), jnp.bfloat16)
    for copy in copies:
        copy.wait()


def outgoing_rows(hidden, ids, members):
    tok, width = hidden.shape
    share = width // members
    return pl.pallas_call(
        outgoing_kernel,
        out_shape=jax.ShapeDtypeStruct((members, tok + ID_ROWS, share), jnp.bfloat16),
        in_specs=[ANYWHERE, IN_VMEM],
        out_specs=IN_VMEM,
        scratch_shapes=[pltpu.SemaphoreType.DMA((members,))],
        compiler_params=params(),
        name="outgoing_rows",
    )(hidden, ids)


def down_kernel(map_count, rank, labels_ref, rows_ref, *refs):
    maps, (packed_ref, id_rows_ref, total_ref, ids_ref) = refs[:map_count], refs[map_count:]
    members, rows, share = rows_ref.shape
    tok = rows - ID_ROWS
    block = min(BLOCK, members)
    half = tok // 2
    lane = lax.broadcasted_iota(jnp.int32, (half, LANES), 1)

    def one(step, _):
        first = step * block
        for n in range(block):
            row = rows_ref[first + n, tok : tok + 1, :LANES].astype(jnp.float32)
            id_rows_ref[pl.ds(first + n, 1), :] = row
            ids_ref[n] = jnp.broadcast_to(row, (LANES, tok)).T
        tokens = rows_ref[pl.ds(first, block), :tok, :].reshape(block * tok, share)
        ids = ids_ref[...].reshape(block * tok, LANES)
        tile = 0
        for at in range(0, map_count, 2):
            some = jnp.concatenate([m[...] for m in maps[at : at + 2]], axis=0)
            product = lax.dot_general(
                tokens, some, (((1,), (1,)), ((), ())), preferred_element_type=jnp.float32
            )
            total = jnp.zeros((block * tok, LANES), jnp.float32) if tile == 0 else total_ref[...]
            for n in range(some.shape[0] // LANES):
                named = ids == tile_labels(labels_ref, tile, rank, (1, LANES))
                total += jnp.where(named, product[:, n * LANES : (n + 1) * LANES], 0.0)
                tile += 1
            total_ref[...] = total
        for n in range(block):
            total = total_ref[n * tok : (n + 1) * tok, :]
            total += pltpu.roll(total, LANES // 2, 1)
            packed_ref[first + n] = jnp.where(lane < rank, total[:half], total[half:])
        return 0

    lax.fori_loop(0, members // block, one, 0)


def down_product(labels, rows, maps, rank):
    members, tok, share = rows.shape
    tok -= ID_ROWS
    map_rows = sum(m.shape[0] for m in maps)
    return pl.pallas_call(
        functools.partial(down_kernel, len(maps), rank),
        out_shape=[
            jax.ShapeDtypeStruct((members, tok // 2, LANES), jnp.float32),
            jax.ShapeDtypeStruct((members, tok), jnp.float32),
        ],
        in_specs=[IN_SMEM, IN_VMEM] + [IN_VMEM] * len(maps),
        out_specs=[IN_VMEM, IN_VMEM],
        scratch_shapes=[
            pltpu.VMEM((min(BLOCK, members) * tok, LANES), jnp.float32),
            pltpu.VMEM((min(BLOCK, members), tok, LANES), jnp.float32),
        ],
        compiler_params=params(8 * min(BLOCK, members) * tok * LANES),
        cost_estimate=pl.CostEstimate(
            flops=2 * map_rows * members * tok * share,
            bytes_accessed=2 * share * (map_rows + members * tok),
            transcendentals=0,
        ),
        name="down_product",
    )(labels, rows, *maps)


def copies_kernel(terms_ref, out_ref):
    own = jnp.sum(terms_ref[...], axis=0).astype(jnp.bfloat16)
    for member in range(out_ref.shape[0]):
        out_ref[member] = own


def summed_copies(terms):
    return pl.pallas_call(
        copies_kernel,
        out_shape=jax.ShapeDtypeStruct(terms.shape, jnp.bfloat16),
        in_specs=[IN_VMEM],
        out_specs=IN_VMEM,
        compiler_params=params(),
        name="summed_copies",
    )(terms)


def up_kernel(map_count, rank, offsets, labels_ref, me_ref, ids_ref, shrunk_ref, *refs):
    half, members = shrunk_ref.shape[1], len(offsets)
    maps, outs = refs[:map_count], refs[map_count : map_count + members]
    spread_ref = refs[-1]
    tok = 2 * half
    block = min(BLOCK, members)
    tiles = spread_ref.shape[1] // LANES
    lane = lax.broadcasted_iota(jnp.int32, (half, LANES), 1)
    held = jnp.concatenate([m[...] for m in maps], axis=0)
    for first in range(0, members, block):
        for n in range(block):
            member = me_ref[0] ^ offsets[first + n]
            packed = shrunk_ref[member].astype(jnp.float32)
            turned = pltpu.roll(packed, LANES // 2, 1)
            shrunk = jnp.concatenate(
                [jnp.where(lane < rank, packed, turned), jnp.where(lane < rank, turned, packed)], axis=0
            )
            ids = jnp.broadcast_to(ids_ref[pl.ds(member, 1), :], (LANES, tok)).T
            for tile in range(tiles):
                named = ids == tile_labels(labels_ref, tile, rank, (1, LANES))
                spread_ref[n * tok : (n + 1) * tok, tile * LANES : (tile + 1) * LANES] = jnp.where(
                    named, shrunk, 0.0
                ).astype(jnp.bfloat16)
        product = jnp.dot(spread_ref[...], held, preferred_element_type=jnp.float32)
        product = (adapter_scale * product).astype(jnp.bfloat16)
        for n in range(block):
            outs[first + n][...] = product[n * tok : (n + 1) * tok, :]


def up_product(labels, me, ids, shrunk, maps, rank, offsets):
    members, tok = len(offsets), ids.shape[1]
    map_rows, piece = sum(m.shape[0] for m in maps), maps[0].shape[1]
    return pl.pallas_call(
        functools.partial(up_kernel, len(maps), rank, offsets),
        out_shape=[jax.ShapeDtypeStruct((tok, piece), jnp.bfloat16)] * members,
        in_specs=[IN_SMEM, IN_SMEM, IN_VMEM, IN_VMEM] + [IN_VMEM] * len(maps),
        out_specs=[IN_VMEM] * members,
        scratch_shapes=[pltpu.VMEM((min(BLOCK, members) * tok, map_rows), jnp.bfloat16)],
        compiler_params=params(2 * min(BLOCK, members) * tok * map_rows),
        cost_estimate=pl.CostEstimate(
            flops=2 * map_rows * members * tok * piece,
            bytes_accessed=2 * piece * (map_rows + members * tok),
            transcendentals=0,
        ),
        name="up_product",
    )(labels, me, ids, shrunk, *maps)


def place_kernel(offsets, me_ref, *refs):
    blocks, out_ref, sems = refs[:-2], refs[-2], refs[-1]
    share = blocks[0].shape[1]
    copies = []
    for n, block in enumerate(blocks):
        at = pl.multiple_of((me_ref[0] ^ offsets[n]) * share, LANES)
        copies.append(pltpu.make_async_copy(block, out_ref.at[:, pl.ds(at, share)], sems.at[n]))
    for copy in copies:
        copy.start()
    for copy in copies:
        copy.wait()


def place(me, offsets, blocks):
    tok, share = blocks[0].shape
    return pl.pallas_call(
        functools.partial(place_kernel, offsets),
        out_shape=jax.ShapeDtypeStruct((tok, len(blocks) * share), jnp.bfloat16),
        in_specs=[IN_SMEM] + [ANYWHERE] * len(blocks),
        out_specs=ANYWHERE,
        scratch_shapes=[pltpu.SemaphoreType.DMA((len(blocks),))],
        compiler_params=params(),
        name="place_results",
    )(me, *blocks)


def per_device(token_adapter_index, hidden, adapter_down_maps, adapter_up_maps):
    tok, width = hidden.shape
    groups, outer, inner = (lax.axis_size(a) for a in ("groups", "outer", "inner"))
    group, level, place_in_group = (lax.axis_index(a) for a in ("groups", "outer", "inner"))
    members = groups * inner
    share = width // members
    rank = adapter_up_maps.shape[1]
    me = group * inner + place_in_group

    def slices(array):
        return [
            lax.dynamic_slice_in_dim(array, (me ^ offset) * share, share, axis=1) for offset in range(inner)
        ]

    def exchanged(blocks):
        return blocks[:1] + [to_partner(blocks[n], "inner", inner, n) for n in range(1, inner)]

    def rings(near, far, first_cost=0, third_after=()):
        near, far = [near], [far]
        for step in range(1, outer):
            for blocks in near, far:
                block = blocks[-1]
                if step == 2 and first_cost:
                    block = joined([block], first_cost)
                if step == 3:
                    block = after(block, *third_after)
                blocks.append(next_on_ring(block, outer))
        return near, far

    steps_back = jnp.arange(outer, dtype=jnp.int32)[:, None]
    labels = ((level - steps_back + outer) % outer) * inner + (
        place_in_group ^ jnp.arange(inner, dtype=jnp.int32)[None, :]
    )
    labels = labels.reshape(-1)

    middle = inner // 2
    down = exchanged(slices(adapter_down_maps[0].T))
    down_near, down_far = rings(joined(down[:middle], AHEAD), joined(down[middle:], AHEAD), first_cost=SLIGHTLY_AHEAD)
    ids = token_adapter_index.reshape(1, tok)
    rows = swap(outgoing_rows(after(hidden, down_near[0]), ids, members))
    up = exchanged([after(block, down_near[1]) for block in slices(adapter_up_maps[0])])

    down_maps = [m for pair in zip(down_near, down_far) for m in pair]
    packed, id_rows = down_product(labels, rows, down_maps, rank)
    terms = swap(packed)
    up_near, up_far = rings(
        after(jnp.concatenate(up[:middle], axis=0), down_near[-1]),
        jnp.concatenate([after(block, packed) for block in up[middle:]], axis=0),
        third_after=[terms],
    )
    up_maps = [m for pair in zip(up_near, up_far) for m in pair]
    shrunk = swap(summed_copies(terms))
    offsets = sorted(range(1, members), key=lambda n: (-(n >= inner) - (n % inner >= 2), -(n >= inner), n)) + [0]
    results = []
    for some in offsets[: members // 2], offsets[members // 2 :]:
        results += up_product(labels, me.reshape(1), id_rows, shrunk, up_maps, rank, some)
    returned = [to_partner(r, PLANE, members, n) for r, n in zip(results[:-1], offsets)]
    return place(me.reshape(1), offsets, returned + results[-1:])


def solution(mesh):
    groups, wide = mesh.shape["groups"], mesh.shape["wide"]
    outer = 1 << ((wide.bit_length() - 1) // 2)
    fine = Mesh(mesh.devices.reshape(groups, outer, wide // outer), ("groups", "outer", "inner"))
    owner = ("outer", "inner")
    rows = P(("groups",) + owner, None)
    return jax.shard_map(
        per_device,
        mesh=fine,
        in_specs=(rows, rows, P(owner, None, None), P(owner, None, None)),
        out_specs=rows,
        check_vma=False,
    )
```

```python
import functools

import jax
import jax.numpy as jnp
from jax import lax
from jax.experimental import pallas as pl
from jax.experimental.pallas import tpu as pltpu
from jax.sharding import Mesh
from jax.sharding import PartitionSpec as P

adapter_scale = 2.0
PLANE = ("groups", "inner")
LANES = 128
ID_ROWS = 8
AHEAD, SLIGHTLY_AHEAD = 10**11, 6 * 10**9
BLOCK = 8
IN_VMEM = pl.BlockSpec(memory_space=pltpu.VMEM)
IN_SMEM = pl.BlockSpec(memory_space=pltpu.SMEM)
ANYWHERE = pl.BlockSpec(memory_space=pl.ANY)


def params(scratch_bytes=0):
    return pltpu.CompilerParams(vmem_limit_bytes=(12 << 20) + 2 * scratch_bytes)


def to_partner(value, axes, size, offset):
    return lax.ppermute(value, axes, [(i, i ^ offset) for i in range(size)])


def next_on_ring(block, outer):
    return lax.ppermute(block, "outer", [(i, (i + 1) % outer) for i in range(outer)])


def after(value, *earlier):
    return lax.optimization_barrier((value,) + earlier)[0]


def swap(value):
    return lax.all_to_all(value, PLANE, split_axis=0, concat_axis=0, tiled=True)


def tile_labels(labels_ref, tile, rank, shape):
    per_tile = LANES // rank
    lane = lax.broadcasted_iota(jnp.int32, shape, 1)
    label = jnp.full(shape, labels_ref[tile * per_tile], jnp.int32)
    for n in range(1, per_tile):
        label = jnp.where(lane >= n * rank, labels_ref[tile * per_tile + n], label)
    return label.astype(jnp.float32)


def join_kernel(*refs):
    blocks, out_ref = refs[:-1], refs[-1]
    rows = blocks[0].shape[0]
    for n, block in enumerate(blocks):
        out_ref[n * rows : (n + 1) * rows, :] = block[...]


def joined(blocks, cost):
    rows, share = blocks[0].shape
    return pl.pallas_call(
        join_kernel,
        out_shape=jax.ShapeDtypeStruct((len(blocks) * rows, share), jnp.bfloat16),
        in_specs=[IN_VMEM] * len(blocks),
        out_specs=IN_VMEM,
        compiler_params=params(),
        cost_estimate=pl.CostEstimate(flops=cost, bytes_accessed=10**6, transcendentals=0),
        name="join_blocks",
    )(*blocks)


def outgoing_kernel(hidden_ref, ids_ref, out_ref, sems):
    members, rows, share = out_ref.shape
    tok = rows - ID_ROWS
    copies = [
        pltpu.make_async_copy(
            hidden_ref.at[:, pl.ds(member * share, share)], out_ref.at[member, pl.ds(0, tok)], sems.at[member]
        )
        for member in range(members)
    ]
    for copy in copies:
        copy.start()
    ids = jnp.broadcast_to(ids_ref[...].astype(jnp.float32).astype(jnp.bfloat16), (ID_ROWS, tok))
    for member in range(members):
        out_ref[member, tok:, :tok] = ids
        if share > tok:
            out_ref[member, tok:, tok:] = jnp.zeros((ID_ROWS, share - tok), jnp.bfloat16)
    for copy in copies:
        copy.wait()


def outgoing_rows(hidden, ids, members):
    tok, width = hidden.shape
    share = width // members
    return pl.pallas_call(
        outgoing_kernel,
        out_shape=jax.ShapeDtypeStruct((members, tok + ID_ROWS, share), jnp.bfloat16),
        in_specs=[ANYWHERE, IN_VMEM],
        out_specs=IN_VMEM,
        scratch_shapes=[pltpu.SemaphoreType.DMA((members,))],
        compiler_params=params(),
        name="outgoing_rows",
    )(hidden, ids)


def down_kernel(map_count, rank, labels_ref, rows_ref, *refs):
    maps, (packed_ref, id_rows_ref, total_ref, ids_ref) = refs[:map_count], refs[map_count:]
    members, rows, share = rows_ref.shape
    tok = rows - ID_ROWS
    block = min(BLOCK, members)
    half = tok // 2
    lane = lax.broadcasted_iota(jnp.int32, (half, LANES), 1)

    def one(step, _):
        first = step * block
        for n in range(block):
            row = rows_ref[first + n, tok : tok + 1, :LANES].astype(jnp.float32)
            id_rows_ref[pl.ds(first + n, 1), :] = row
            ids_ref[n] = jnp.broadcast_to(row, (LANES, tok)).T
        tokens = rows_ref[pl.ds(first, block), :tok, :].reshape(block * tok, share)
        ids = ids_ref[...].reshape(block * tok, LANES)
        tile = 0
        for at in range(0, map_count, 2):
            some = jnp.concatenate([m[...] for m in maps[at : at + 2]], axis=0)
            product = lax.dot_general(
                tokens, some, (((1,), (1,)), ((), ())), preferred_element_type=jnp.float32
            )
            total = jnp.zeros((block * tok, LANES), jnp.float32) if tile == 0 else total_ref[...]
            for n in range(some.shape[0] // LANES):
                named = ids == tile_labels(labels_ref, tile, rank, (1, LANES))
                total += jnp.where(named, product[:, n * LANES : (n + 1) * LANES], 0.0)
                tile += 1
            total_ref[...] = total
        for n in range(block):
            total = total_ref[n * tok : (n + 1) * tok, :]
            total += pltpu.roll(total, LANES // 2, 1)
            packed_ref[first + n] = jnp.where(lane < rank, total[:half], total[half:])
        return 0

    lax.fori_loop(0, members // block, one, 0)


def down_product(labels, rows, maps, rank):
    members, tok, share = rows.shape
    tok -= ID_ROWS
    map_rows = sum(m.shape[0] for m in maps)
    return pl.pallas_call(
        functools.partial(down_kernel, len(maps), rank),
        out_shape=[
            jax.ShapeDtypeStruct((members, tok // 2, LANES), jnp.float32),
            jax.ShapeDtypeStruct((members, tok), jnp.float32),
        ],
        in_specs=[IN_SMEM, IN_VMEM] + [IN_VMEM] * len(maps),
        out_specs=[IN_VMEM, IN_VMEM],
        scratch_shapes=[
            pltpu.VMEM((min(BLOCK, members) * tok, LANES), jnp.float32),
            pltpu.VMEM((min(BLOCK, members), tok, LANES), jnp.float32),
        ],
        compiler_params=params(8 * min(BLOCK, members) * tok * LANES),
        cost_estimate=pl.CostEstimate(
            flops=2 * map_rows * members * tok * share,
            bytes_accessed=2 * share * (map_rows + members * tok),
            transcendentals=0,
        ),
        name="down_product",
    )(labels, rows, *maps)


def copies_kernel(terms_ref, out_ref):
    own = jnp.sum(terms_ref[...], axis=0).astype(jnp.bfloat16)
    for member in range(out_ref.shape[0]):
        out_ref[member] = own


def summed_copies(terms):
    return pl.pallas_call(
        copies_kernel,
        out_shape=jax.ShapeDtypeStruct(terms.shape, jnp.bfloat16),
        in_specs=[IN_VMEM],
        out_specs=IN_VMEM,
        compiler_params=params(),
        name="summed_copies",
    )(terms)


def up_kernel(map_count, rank, offsets, labels_ref, me_ref, ids_ref, shrunk_ref, *refs):
    half, members = shrunk_ref.shape[1], len(offsets)
    maps, outs = refs[:map_count], refs[map_count : map_count + members]
    spread_ref = refs[-1]
    tok = 2 * half
    block = min(BLOCK, members)
    tiles = spread_ref.shape[1] // LANES
    lane = lax.broadcasted_iota(jnp.int32, (half, LANES), 1)
    held = jnp.concatenate([m[...] for m in maps], axis=0)
    for first in range(0, members, block):
        for n in range(block):
            member = me_ref[0] ^ offsets[first + n]
            packed = shrunk_ref[member].astype(jnp.float32)
            turned = pltpu.roll(packed, LANES // 2, 1)
            shrunk = jnp.concatenate(
                [jnp.where(lane < rank, packed, turned), jnp.where(lane < rank, turned, packed)], axis=0
            )
            ids = jnp.broadcast_to(ids_ref[pl.ds(member, 1), :], (LANES, tok)).T
            for tile in range(tiles):
                named = ids == tile_labels(labels_ref, tile, rank, (1, LANES))
                spread_ref[n * tok : (n + 1) * tok, tile * LANES : (tile + 1) * LANES] = jnp.where(
                    named, shrunk, 0.0
                ).astype(jnp.bfloat16)
        product = jnp.dot(spread_ref[...], held, preferred_element_type=jnp.float32)
        product = (adapter_scale * product).astype(jnp.bfloat16)
        for n in range(block):
            outs[first + n][...] = product[n * tok : (n + 1) * tok, :]


def up_product(labels, me, ids, shrunk, maps, rank, offsets):
    members, tok = len(offsets), ids.shape[1]
    map_rows, piece = sum(m.shape[0] for m in maps), maps[0].shape[1]
    return pl.pallas_call(
        functools.partial(up_kernel, len(maps), rank, offsets),
        out_shape=[jax.ShapeDtypeStruct((tok, piece), jnp.bfloat16)] * members,
        in_specs=[IN_SMEM, IN_SMEM, IN_VMEM, IN_VMEM] + [IN_VMEM] * len(maps),
        out_specs=[IN_VMEM] * members,
        scratch_shapes=[pltpu.VMEM((min(BLOCK, members) * tok, map_rows), jnp.bfloat16)],
        compiler_params=params(2 * min(BLOCK, members) * tok * map_rows),
        cost_estimate=pl.CostEstimate(
            flops=2 * map_rows * members * tok * piece,
            bytes_accessed=2 * piece * (map_rows + members * tok),
            transcendentals=0,
        ),
        name="up_product",
    )(labels, me, ids, shrunk, *maps)


def place_kernel(offsets, me_ref, *refs):
    blocks, out_ref, sems = refs[:-2], refs[-2], refs[-1]
    share = blocks[0].shape[1]
    copies = []
    for n, block in enumerate(blocks):
        at = pl.multiple_of((me_ref[0] ^ offsets[n]) * share, LANES)
        copies.append(pltpu.make_async_copy(block, out_ref.at[:, pl.ds(at, share)], sems.at[n]))
    for copy in copies:
        copy.start()
    for copy in copies:
        copy.wait()


def place(me, offsets, blocks):
    tok, share = blocks[0].shape
    return pl.pallas_call(
        functools.partial(place_kernel, offsets),
        out_shape=jax.ShapeDtypeStruct((tok, len(blocks) * share), jnp.bfloat16),
        in_specs=[IN_SMEM] + [ANYWHERE] * len(blocks),
        out_specs=ANYWHERE,
        scratch_shapes=[pltpu.SemaphoreType.DMA((len(blocks),))],
        compiler_params=params(),
        name="place_results",
    )(me, *blocks)


def per_device(token_adapter_index, hidden, adapter_down_maps, adapter_up_maps):
    tok, width = hidden.shape
    groups, outer, inner = (lax.axis_size(a) for a in ("groups", "outer", "inner"))
    group, level, place_in_group = (lax.axis_index(a) for a in ("groups", "outer", "inner"))
    members = groups * inner
    share = width // members
    rank = adapter_up_maps.shape[1]
    me = group * inner + place_in_group

    def slices(array):
        return [
            lax.dynamic_slice_in_dim(array, (me ^ offset) * share, share, axis=1) for offset in range(inner)
        ]

    def exchanged(blocks):
        return blocks[:1] + [to_partner(blocks[n], "inner", inner, n) for n in range(1, inner)]

    def rings(near, far, first_cost=0, second_after=()):
        near, far = [near], [far]
        for step in range(1, outer):
            for blocks in near, far:
                block = blocks[-1]
                if step == 2:
                    block = after(block, *second_after)
                    if first_cost:
                        block = joined([block], first_cost)
                blocks.append(next_on_ring(block, outer))
        return near, far

    steps_back = jnp.arange(outer, dtype=jnp.int32)[:, None]
    labels = ((level - steps_back + outer) % outer) * inner + (
        place_in_group ^ jnp.arange(inner, dtype=jnp.int32)[None, :]
    )
    labels = labels.reshape(-1)

    middle = inner // 2
    down = exchanged(slices(adapter_down_maps[0].T))
    down_near, down_far = rings(joined(down[:middle], AHEAD), joined(down[middle:], AHEAD), first_cost=SLIGHTLY_AHEAD)
    ids = token_adapter_index.reshape(1, tok)
    rows = swap(outgoing_rows(after(hidden, down_near[0]), ids, members))
    up = exchanged([after(block, down_near[1]) for block in slices(adapter_up_maps[0])])

    down_maps = [m for pair in zip(down_near, down_far) for m in pair]
    packed, id_rows = down_product(labels, rows, down_maps, rank)
    up_near, up_far = rings(
        after(jnp.concatenate(up[:middle], axis=0), down_near[-1]),
        jnp.concatenate([after(block, down_far[-1]) for block in up[middle:]], axis=0),
        second_after=[packed],
    )
    up_maps = [m for pair in zip(up_near, up_far) for m in pair]
    shrunk = swap(summed_copies(swap(packed)))
    shrunk = after(shrunk, to_partner(after(id_rows, shrunk), "inner", inner, 1))
    offsets = sorted(range(1, members), key=lambda n: (-(n >= inner) - (n % inner >= 2), -(n >= inner), n)) + [0]
    results = []
    for some in offsets[: members // 2], offsets[members // 2 :]:
        results += up_product(labels, me.reshape(1), id_rows, shrunk, up_maps, rank, some)
    returned = [to_partner(r, PLANE, members, n) for r, n in zip(results[:-1], offsets)]
    return place(me.reshape(1), offsets, returned + results[-1:])


def solution(mesh):
    groups, wide = mesh.shape["groups"], mesh.shape["wide"]
    outer = 1 << ((wide.bit_length() - 1) // 2)
    fine = Mesh(mesh.devices.reshape(groups, outer, wide // outer), ("groups", "outer", "inner"))
    owner = ("outer", "inner")
    rows = P(("groups",) + owner, None)
    return jax.shard_map(
        per_device,
        mesh=fine,
        in_specs=(rows, rows, P(owner, None, None), P(owner, None, None)),
        out_specs=rows,
        check_vma=False,
    )
```

```python
import functools

import jax
import jax.numpy as jnp
from jax import lax
from jax.experimental import pallas as pl
from jax.experimental.pallas import tpu as pltpu
from jax.sharding import Mesh
from jax.sharding import PartitionSpec as P

adapter_scale = 2.0
PLANE = ("groups", "inner")
LANES = 128
ID_ROWS = 8
AHEAD, SLIGHTLY_AHEAD = 10**11, 6 * 10**9
BLOCK = 8
IN_VMEM = pl.BlockSpec(memory_space=pltpu.VMEM)
IN_SMEM = pl.BlockSpec(memory_space=pltpu.SMEM)
ANYWHERE = pl.BlockSpec(memory_space=pl.ANY)


def params(scratch_bytes=0):
    return pltpu.CompilerParams(vmem_limit_bytes=(12 << 20) + 2 * scratch_bytes)


def to_partner(value, axes, size, offset):
    return lax.ppermute(value, axes, [(i, i ^ offset) for i in range(size)])


def next_on_ring(block, outer):
    return lax.ppermute(block, "outer", [(i, (i + 1) % outer) for i in range(outer)])


def after(value, *earlier):
    return lax.optimization_barrier((value,) + earlier)[0]


def swap(value):
    return lax.all_to_all(value, PLANE, split_axis=0, concat_axis=0, tiled=True)


def tile_labels(labels_ref, tile, rank, shape):
    per_tile = LANES // rank
    lane = lax.broadcasted_iota(jnp.int32, shape, 1)
    label = jnp.full(shape, labels_ref[tile * per_tile], jnp.int32)
    for n in range(1, per_tile):
        label = jnp.where(lane >= n * rank, labels_ref[tile * per_tile + n], label)
    return label.astype(jnp.float32)


def join_kernel(*refs):
    blocks, out_ref = refs[:-1], refs[-1]
    rows = blocks[0].shape[0]
    for n, block in enumerate(blocks):
        out_ref[n * rows : (n + 1) * rows, :] = block[...]


def joined(blocks, cost):
    rows, share = blocks[0].shape
    return pl.pallas_call(
        join_kernel,
        out_shape=jax.ShapeDtypeStruct((len(blocks) * rows, share), jnp.bfloat16),
        in_specs=[IN_VMEM] * len(blocks),
        out_specs=IN_VMEM,
        compiler_params=params(),
        cost_estimate=pl.CostEstimate(flops=cost, bytes_accessed=10**6, transcendentals=0),
        name="join_blocks",
    )(*blocks)


def outgoing_kernel(hidden_ref, ids_ref, out_ref, sems):
    members, rows, share = out_ref.shape
    tok = rows - ID_ROWS
    copies = [
        pltpu.make_async_copy(
            hidden_ref.at[:, pl.ds(member * share, share)], out_ref.at[member, pl.ds(0, tok)], sems.at[member]
        )
        for member in range(members)
    ]
    for copy in copies:
        copy.start()
    ids = jnp.broadcast_to(ids_ref[...].astype(jnp.float32).astype(jnp.bfloat16), (ID_ROWS, tok))
    for member in range(members):
        out_ref[member, tok:, :tok] = ids
        if share > tok:
            out_ref[member, tok:, tok:] = jnp.zeros((ID_ROWS, share - tok), jnp.bfloat16)
    for copy in copies:
        copy.wait()


def outgoing_rows(hidden, ids, members):
    tok, width = hidden.shape
    share = width // members
    return pl.pallas_call(
        outgoing_kernel,
        out_shape=jax.ShapeDtypeStruct((members, tok + ID_ROWS, share), jnp.bfloat16),
        in_specs=[ANYWHERE, IN_VMEM],
        out_specs=IN_VMEM,
        scratch_shapes=[pltpu.SemaphoreType.DMA((members,))],
        compiler_params=params(),
        name="outgoing_rows",
    )(hidden, ids)


def down_kernel(map_count, rank, labels_ref, rows_ref, *refs):
    maps, (packed_ref, id_rows_ref, total_ref, ids_ref) = refs[:map_count], refs[map_count:]
    members, rows, share = rows_ref.shape
    tok = rows - ID_ROWS
    block = min(BLOCK, members)
    half = tok // 2
    lane = lax.broadcasted_iota(jnp.int32, (half, LANES), 1)

    def one(step, _):
        first = step * block
        for n in range(block):
            row = rows_ref[first + n, tok : tok + 1, :LANES].astype(jnp.float32)
            id_rows_ref[pl.ds(first + n, 1), :] = row
            ids_ref[n] = jnp.broadcast_to(row, (LANES, tok)).T
        tokens = rows_ref[pl.ds(first, block), :tok, :].reshape(block * tok, share)
        ids = ids_ref[...].reshape(block * tok, LANES)
        tile = 0
        for at in range(0, map_count, 2):
            some = jnp.concatenate([m[...] for m in maps[at : at + 2]], axis=0)
            product = lax.dot_general(
                tokens, some, (((1,), (1,)), ((), ())), preferred_element_type=jnp.float32
            )
            total = jnp.zeros((block * tok, LANES), jnp.float32) if tile == 0 else total_ref[...]
            for n in range(some.shape[0] // LANES):
                named = ids == tile_labels(labels_ref, tile, rank, (1, LANES))
                total += jnp.where(named, product[:, n * LANES : (n + 1) * LANES], 0.0)
                tile += 1
            total_ref[...] = total
        for n in range(block):
            total = total_ref[n * tok : (n + 1) * tok, :]
            total += pltpu.roll(total, LANES // 2, 1)
            packed_ref[first + n] = jnp.where(lane < rank, total[:half], total[half:])
        return 0

    lax.fori_loop(0, members // block, one, 0)


def down_product(labels, rows, maps, rank):
    members, tok, share = rows.shape
    tok -= ID_ROWS
    map_rows = sum(m.shape[0] for m in maps)
    return pl.pallas_call(
        functools.partial(down_kernel, len(maps), rank),
        out_shape=[
            jax.ShapeDtypeStruct((members, tok // 2, LANES), jnp.float32),
            jax.ShapeDtypeStruct((members, tok), jnp.float32),
        ],
        in_specs=[IN_SMEM, IN_VMEM] + [IN_VMEM] * len(maps),
        out_specs=[IN_VMEM, IN_VMEM],
        scratch_shapes=[
            pltpu.VMEM((min(BLOCK, members) * tok, LANES), jnp.float32),
            pltpu.VMEM((min(BLOCK, members), tok, LANES), jnp.float32),
        ],
        compiler_params=params(8 * min(BLOCK, members) * tok * LANES),
        cost_estimate=pl.CostEstimate(
            flops=2 * map_rows * members * tok * share,
            bytes_accessed=2 * share * (map_rows + members * tok),
            transcendentals=0,
        ),
        name="down_product",
    )(labels, rows, *maps)


def copies_kernel(terms_ref, out_ref):
    own = jnp.sum(terms_ref[...], axis=0).astype(jnp.bfloat16)
    for member in range(out_ref.shape[0]):
        out_ref[member] = own


def summed_copies(terms):
    return pl.pallas_call(
        copies_kernel,
        out_shape=jax.ShapeDtypeStruct(terms.shape, jnp.bfloat16),
        in_specs=[IN_VMEM],
        out_specs=IN_VMEM,
        compiler_params=params(),
        name="summed_copies",
    )(terms)


def up_kernel(map_count, rank, offsets, labels_ref, me_ref, ids_ref, shrunk_ref, *refs):
    half, members = shrunk_ref.shape[1], len(offsets)
    maps, outs = refs[:map_count], refs[map_count : map_count + members]
    spread_ref = refs[-1]
    tok = 2 * half
    block = min(BLOCK, members)
    tiles = spread_ref.shape[1] // LANES
    lane = lax.broadcasted_iota(jnp.int32, (half, LANES), 1)
    held = jnp.concatenate([m[...] for m in maps], axis=0)
    for first in range(0, members, block):
        for n in range(block):
            member = me_ref[0] ^ offsets[first + n]
            packed = shrunk_ref[member].astype(jnp.float32)
            turned = pltpu.roll(packed, LANES // 2, 1)
            shrunk = jnp.concatenate(
                [jnp.where(lane < rank, packed, turned), jnp.where(lane < rank, turned, packed)], axis=0
            )
            ids = jnp.broadcast_to(ids_ref[pl.ds(member, 1), :], (LANES, tok)).T
            for tile in range(tiles):
                named = ids == tile_labels(labels_ref, tile, rank, (1, LANES))
                spread_ref[n * tok : (n + 1) * tok, tile * LANES : (tile + 1) * LANES] = jnp.where(
                    named, shrunk, 0.0
                ).astype(jnp.bfloat16)
        product = jnp.dot(spread_ref[...], held, preferred_element_type=jnp.float32)
        product = (adapter_scale * product).astype(jnp.bfloat16)
        for n in range(block):
            outs[first + n][...] = product[n * tok : (n + 1) * tok, :]


def up_product(labels, me, ids, shrunk, maps, rank, offsets):
    members, tok = len(offsets), ids.shape[1]
    map_rows, piece = sum(m.shape[0] for m in maps), maps[0].shape[1]
    return pl.pallas_call(
        functools.partial(up_kernel, len(maps), rank, offsets),
        out_shape=[jax.ShapeDtypeStruct((tok, piece), jnp.bfloat16)] * members,
        in_specs=[IN_SMEM, IN_SMEM, IN_VMEM, IN_VMEM] + [IN_VMEM] * len(maps),
        out_specs=[IN_VMEM] * members,
        scratch_shapes=[pltpu.VMEM((min(BLOCK, members) * tok, map_rows), jnp.bfloat16)],
        compiler_params=params(2 * min(BLOCK, members) * tok * map_rows),
        cost_estimate=pl.CostEstimate(
            flops=2 * map_rows * members * tok * piece,
            bytes_accessed=2 * piece * (map_rows + members * tok),
            transcendentals=0,
        ),
        name="up_product",
    )(labels, me, ids, shrunk, *maps)


def place_kernel(offsets, me_ref, *refs):
    blocks, out_ref, sems = refs[:-2], refs[-2], refs[-1]
    share = blocks[0].shape[1]
    copies = []
    for n, block in enumerate(blocks):
        at = pl.multiple_of((me_ref[0] ^ offsets[n]) * share, LANES)
        copies.append(pltpu.make_async_copy(block, out_ref.at[:, pl.ds(at, share)], sems.at[n]))
    for copy in copies:
        copy.start()
    for copy in copies:
        copy.wait()


def place(me, offsets, blocks):
    tok, share = blocks[0].shape
    return pl.pallas_call(
        functools.partial(place_kernel, offsets),
        out_shape=jax.ShapeDtypeStruct((tok, len(blocks) * share), jnp.bfloat16),
        in_specs=[IN_SMEM] + [ANYWHERE] * len(blocks),
        out_specs=ANYWHERE,
        scratch_shapes=[pltpu.SemaphoreType.DMA((len(blocks),))],
        compiler_params=params(),
        name="place_results",
    )(me, *blocks)


def per_device(token_adapter_index, hidden, adapter_down_maps, adapter_up_maps):
    tok, width = hidden.shape
    groups, outer, inner = (lax.axis_size(a) for a in ("groups", "outer", "inner"))
    group, level, place_in_group = (lax.axis_index(a) for a in ("groups", "outer", "inner"))
    members = groups * inner
    share = width // members
    rank = adapter_up_maps.shape[1]
    me = group * inner + place_in_group

    def slices(array):
        return [
            lax.dynamic_slice_in_dim(array, (me ^ offset) * share, share, axis=1) for offset in range(inner)
        ]

    def exchanged(blocks):
        return blocks[:1] + [to_partner(blocks[n], "inner", inner, n) for n in range(1, inner)]

    def rings(near, far, near_cost, far_cost, far_second_after=()):
        near, far = [near], [far]
        for step in range(1, outer):
            near_block, far_block = near[-1], far[-1]
            if step == 2:
                far_block = after(far_block, *far_second_after)
                if near_cost:
                    near_block = joined([near_block], near_cost)
                if far_cost:
                    far_block = joined([far_block], far_cost)
            near.append(next_on_ring(near_block, outer))
            far.append(next_on_ring(far_block, outer))
        return near, far

    steps_back = jnp.arange(outer, dtype=jnp.int32)[:, None]
    labels = ((level - steps_back + outer) % outer) * inner + (
        place_in_group ^ jnp.arange(inner, dtype=jnp.int32)[None, :]
    )
    labels = labels.reshape(-1)

    middle = inner // 2
    down = exchanged(slices(adapter_down_maps[0].T))
    down_near, down_far = rings(joined(down[:middle], AHEAD), joined(down[middle:], AHEAD), SLIGHTLY_AHEAD, SLIGHTLY_AHEAD)
    ids = token_adapter_index.reshape(1, tok)
    rows = swap(outgoing_rows(after(hidden, down_near[0]), ids, members))
    up = exchanged([after(block, down_near[1]) for block in slices(adapter_up_maps[0])])

    down_maps = [m for pair in zip(down_near, down_far) for m in pair]
    packed, id_rows = down_product(labels, rows, down_maps, rank)
    up_near, up_far = rings(
        after(jnp.concatenate(up[:middle], axis=0), down_near[-1]),
        jnp.concatenate([after(block, down_far[-1]) for block in up[middle:]], axis=0),
        SLIGHTLY_AHEAD,
        0,
        far_second_after=[packed],
    )
    up_maps = [m for pair in zip(up_near, up_far) for m in pair]
    shrunk = swap(summed_copies(swap(packed)))
    offsets = sorted(range(1, members), key=lambda n: (-(n >= inner) - (n % inner >= 2), -(n >= inner), n)) + [0]
    results = []
    for some in offsets[: members // 2], offsets[members // 2 :]:
        results += up_product(labels, me.reshape(1), id_rows, shrunk, up_maps, rank, some)
    returned = [to_partner(r, PLANE, members, n) for r, n in zip(results[:-1], offsets)]
    return place(me.reshape(1), offsets, returned + results[-1:])


def solution(mesh):
    groups, wide = mesh.shape["groups"], mesh.shape["wide"]
    outer = 1 << ((wide.bit_length() - 1) // 2)
    fine = Mesh(mesh.devices.reshape(groups, outer, wide // outer), ("groups", "outer", "inner"))
    owner = ("outer", "inner")
    rows = P(("groups",) + owner, None)
    return jax.shard_map(
        per_device,
        mesh=fine,
        in_specs=(rows, rows, P(owner, None, None), P(owner, None, None)),
        out_specs=rows,
        check_vma=False,
    )
```

```python
import functools
import math

import jax
import jax.numpy as jnp
from jax import lax
from jax.experimental import pallas as pl
from jax.experimental.pallas import tpu as pltpu
from jax.sharding import Mesh
from jax.sharding import PartitionSpec as P

adapter_scale = 2.0
PLANE = ("groups", "inner")
LANES = 128
ID_ROWS = 8
AHEAD, SLIGHTLY_AHEAD = 10**11, 6 * 10**9
BLOCK = 8
IN_VMEM = pl.BlockSpec(memory_space=pltpu.VMEM)
IN_SMEM = pl.BlockSpec(memory_space=pltpu.SMEM)
ANYWHERE = pl.BlockSpec(memory_space=pl.ANY)


def params(scratch_bytes=0):
    return pltpu.CompilerParams(vmem_limit_bytes=(12 << 20) + 2 * scratch_bytes)


def to_partner(value, axes, size, offset):
    return lax.ppermute(value, axes, [(i, i ^ offset) for i in range(size)])


def next_on_ring(block, outer):
    return lax.ppermute(block, "outer", [(i, (i + 1) % outer) for i in range(outer)])


def after(value, *earlier):
    return lax.optimization_barrier((value,) + earlier)[0]


def swap(value):
    return lax.all_to_all(value, PLANE, split_axis=0, concat_axis=0, tiled=True)


def tile_labels(labels_ref, tile, rank, shape):
    per_tile = LANES // rank
    lane = lax.broadcasted_iota(jnp.int32, shape, 1)
    label = jnp.full(shape, labels_ref[tile * per_tile], jnp.int32)
    for n in range(1, per_tile):
        label = jnp.where(lane >= n * rank, labels_ref[tile * per_tile + n], label)
    return label.astype(jnp.float32)


def join_kernel(*refs):
    blocks, out_ref = refs[:-1], refs[-1]
    rows = blocks[0].shape[0]
    for n, block in enumerate(blocks):
        out_ref[n * rows : (n + 1) * rows, :] = block[...]


def joined(blocks, cost):
    rows, share = blocks[0].shape
    return pl.pallas_call(
        join_kernel,
        out_shape=jax.ShapeDtypeStruct((len(blocks) * rows, share), jnp.bfloat16),
        in_specs=[IN_VMEM] * len(blocks),
        out_specs=IN_VMEM,
        compiler_params=params(),
        cost_estimate=pl.CostEstimate(flops=cost, bytes_accessed=10**6, transcendentals=0),
        name="join_blocks",
    )(*blocks)


def pass_kernel(block_ref, out_ref):
    del block_ref, out_ref


def passed(block, cost):
    return pl.pallas_call(
        pass_kernel,
        out_shape=jax.ShapeDtypeStruct(block.shape, block.dtype),
        in_specs=[ANYWHERE],
        out_specs=ANYWHERE,
        input_output_aliases={0: 0},
        compiler_params=params(),
        cost_estimate=pl.CostEstimate(flops=cost, bytes_accessed=10**6, transcendentals=0),
        name="pass_block",
    )(block)


def outgoing_kernel(hidden_ref, ids_ref, out_ref, sems):
    members, rows, share = out_ref.shape
    tok = rows - ID_ROWS
    copies = [
        pltpu.make_async_copy(
            hidden_ref.at[:, pl.ds(member * share, share)], out_ref.at[member, pl.ds(0, tok)], sems.at[member]
        )
        for member in range(members)
    ]
    for copy in copies:
        copy.start()
    ids = jnp.broadcast_to(ids_ref[...].astype(jnp.float32).astype(jnp.bfloat16), (ID_ROWS, tok))
    for member in range(members):
        out_ref[member, tok:, :tok] = ids
        if share > tok:
            out_ref[member, tok:, tok:] = jnp.zeros((ID_ROWS, share - tok), jnp.bfloat16)
    for copy in copies:
        copy.wait()


def outgoing_rows(hidden, ids, members):
    tok, width = hidden.shape
    share = width // members
    return pl.pallas_call(
        outgoing_kernel,
        out_shape=jax.ShapeDtypeStruct((members, tok + ID_ROWS, share), jnp.bfloat16),
        in_specs=[ANYWHERE, IN_VMEM],
        out_specs=IN_VMEM,
        scratch_shapes=[pltpu.SemaphoreType.DMA((members,))],
        compiler_params=params(),
        name="outgoing_rows",
    )(hidden, ids)


def down_kernel(map_count, rank, labels_ref, rows_ref, *refs):
    maps, (packed_ref, id_rows_ref, total_ref, ids_ref) = refs[:map_count], refs[map_count:]
    members, rows, share = rows_ref.shape
    tok = rows - ID_ROWS
    block = min(BLOCK, members)
    half = tok // 2
    lane = lax.broadcasted_iota(jnp.int32, (half, LANES), 1)

    def one(step, _):
        first = step * block
        for n in range(block):
            row = rows_ref[first + n, tok : tok + 1, :LANES].astype(jnp.float32)
            id_rows_ref[pl.ds(first + n, 1), :] = row
            ids_ref[n] = jnp.broadcast_to(row, (LANES, tok)).T
        tokens = rows_ref[pl.ds(first, block), :tok, :].reshape(block * tok, share)
        ids = ids_ref[...].reshape(block * tok, LANES)
        tile = 0
        for at in range(0, map_count, 2):
            some = jnp.concatenate([m[...] for m in maps[at : at + 2]], axis=0)
            product = lax.dot_general(
                tokens, some, (((1,), (1,)), ((), ())), preferred_element_type=jnp.float32
            )
            total = jnp.zeros((block * tok, LANES), jnp.float32) if tile == 0 else total_ref[...]
            for n in range(some.shape[0] // LANES):
                named = ids == tile_labels(labels_ref, tile, rank, (1, LANES))
                total += jnp.where(named, product[:, n * LANES : (n + 1) * LANES], 0.0)
                tile += 1
            total_ref[...] = total
        for n in range(block):
            total = total_ref[n * tok : (n + 1) * tok, :]
            total += pltpu.roll(total, LANES // 2, 1)
            packed_ref[first + n] = jnp.where(lane < rank, total[:half], total[half:])
        return 0

    lax.fori_loop(0, members // block, one, 0)


def down_product(labels, rows, maps, rank):
    members, tok, share = rows.shape
    tok -= ID_ROWS
    map_rows = sum(m.shape[0] for m in maps)
    return pl.pallas_call(
        functools.partial(down_kernel, len(maps), rank),
        out_shape=[
            jax.ShapeDtypeStruct((members, tok // 2, LANES), jnp.float32),
            jax.ShapeDtypeStruct((members, tok), jnp.float32),
        ],
        in_specs=[IN_SMEM, IN_VMEM] + [IN_VMEM] * len(maps),
        out_specs=[IN_VMEM, IN_VMEM],
        scratch_shapes=[
            pltpu.VMEM((min(BLOCK, members) * tok, LANES), jnp.float32),
            pltpu.VMEM((min(BLOCK, members), tok, LANES), jnp.float32),
        ],
        compiler_params=params(8 * min(BLOCK, members) * tok * LANES),
        cost_estimate=pl.CostEstimate(
            flops=2 * map_rows * members * tok * share,
            bytes_accessed=2 * share * (map_rows + members * tok),
            transcendentals=0,
        ),
        name="down_product",
    )(labels, rows, *maps)


def copies_kernel(terms_ref, out_ref):
    own = jnp.sum(terms_ref[...], axis=0).astype(jnp.bfloat16)
    for member in range(out_ref.shape[0]):
        out_ref[member] = own


def summed_copies(terms):
    return pl.pallas_call(
        copies_kernel,
        out_shape=jax.ShapeDtypeStruct(terms.shape, jnp.bfloat16),
        in_specs=[IN_VMEM],
        out_specs=IN_VMEM,
        compiler_params=params(),
        name="summed_copies",
    )(terms)


def rows_at_once(members):
    return members if members <= BLOCK else math.gcd(BLOCK, members)


def up_kernel(map_count, rank, offsets, labels_ref, me_ref, ids_ref, shrunk_ref, *refs):
    half, members = shrunk_ref.shape[1], len(offsets)
    maps, outs = refs[:map_count], refs[map_count : map_count + members]
    spread_ref = refs[-1]
    tok = 2 * half
    block = rows_at_once(members)
    tiles = spread_ref.shape[1] // LANES
    lane = lax.broadcasted_iota(jnp.int32, (half, LANES), 1)
    held = jnp.concatenate([m[...] for m in maps], axis=0)
    for first in range(0, members, block):
        for n in range(block):
            member = me_ref[0] ^ offsets[first + n]
            packed = shrunk_ref[member].astype(jnp.float32)
            turned = pltpu.roll(packed, LANES // 2, 1)
            shrunk = jnp.concatenate(
                [jnp.where(lane < rank, packed, turned), jnp.where(lane < rank, turned, packed)], axis=0
            )
            ids = jnp.broadcast_to(ids_ref[pl.ds(member, 1), :], (LANES, tok)).T
            for tile in range(tiles):
                named = ids == tile_labels(labels_ref, tile, rank, (1, LANES))
                spread_ref[n * tok : (n + 1) * tok, tile * LANES : (tile + 1) * LANES] = jnp.where(
                    named, shrunk, 0.0
                ).astype(jnp.bfloat16)
        product = jnp.dot(spread_ref[...], held, preferred_element_type=jnp.float32)
        product = (adapter_scale * product).astype(jnp.bfloat16)
        for n in range(block):
            outs[first + n][...] = product[n * tok : (n + 1) * tok, :]


def up_product(labels, me, ids, shrunk, maps, rank, offsets):
    members, tok = len(offsets), ids.shape[1]
    map_rows, piece = sum(m.shape[0] for m in maps), maps[0].shape[1]
    return pl.pallas_call(
        functools.partial(up_kernel, len(maps), rank, offsets),
        out_shape=[jax.ShapeDtypeStruct((tok, piece), jnp.bfloat16)] * members,
        in_specs=[IN_SMEM, IN_SMEM, IN_VMEM, IN_VMEM] + [IN_VMEM] * len(maps),
        out_specs=[IN_VMEM] * members,
        scratch_shapes=[pltpu.VMEM((rows_at_once(members) * tok, map_rows), jnp.bfloat16)],
        compiler_params=params(2 * rows_at_once(members) * tok * map_rows),
        cost_estimate=pl.CostEstimate(
            flops=2 * map_rows * members * tok * piece,
            bytes_accessed=2 * piece * (map_rows + members * tok),
            transcendentals=0,
        ),
        name="up_product",
    )(labels, me, ids, shrunk, *maps)


def place_kernel(offsets, me_ref, *refs):
    blocks, out_ref, sems = refs[:-2], refs[-2], refs[-1]
    share = blocks[0].shape[1]
    copies = []
    for n, block in enumerate(blocks):
        at = pl.multiple_of((me_ref[0] ^ offsets[n]) * share, LANES)
        copies.append(pltpu.make_async_copy(block, out_ref.at[:, pl.ds(at, share)], sems.at[n]))
    for copy in copies:
        copy.start()
    for copy in copies:
        copy.wait()


def place(me, offsets, blocks):
    tok, share = blocks[0].shape
    return pl.pallas_call(
        functools.partial(place_kernel, offsets),
        out_shape=jax.ShapeDtypeStruct((tok, len(blocks) * share), jnp.bfloat16),
        in_specs=[IN_SMEM] + [ANYWHERE] * len(blocks),
        out_specs=ANYWHERE,
        scratch_shapes=[pltpu.SemaphoreType.DMA((len(blocks),))],
        compiler_params=params(),
        name="place_results",
    )(me, *blocks)


def per_device(token_adapter_index, hidden, adapter_down_maps, adapter_up_maps):
    tok, width = hidden.shape
    groups, outer, inner = (lax.axis_size(a) for a in ("groups", "outer", "inner"))
    group, level, place_in_group = (lax.axis_index(a) for a in ("groups", "outer", "inner"))
    members = groups * inner
    share = width // members
    rank = adapter_up_maps.shape[1]
    me = group * inner + place_in_group

    def slices(array):
        return [
            lax.dynamic_slice_in_dim(array, (me ^ offset) * share, share, axis=1) for offset in range(inner)
        ]

    def exchanged(blocks):
        return blocks[:1] + [to_partner(blocks[n], "inner", inner, n) for n in range(1, inner)]

    def rings(near, far, near_cost, far_cost, far_second_after=()):
        near, far = [near], [far]
        for step in range(1, outer):
            if step == 2:
                if near_cost:
                    near[-1] = passed(near[-1], near_cost)
                if far_cost:
                    far[-1] = passed(far[-1], far_cost)
                far[-1] = after(far[-1], *far_second_after)
            near.append(next_on_ring(near[-1], outer))
            far.append(next_on_ring(far[-1], outer))
        return near, far

    steps_back = jnp.arange(outer, dtype=jnp.int32)[:, None]
    labels = ((level - steps_back + outer) % outer) * inner + (
        place_in_group ^ jnp.arange(inner, dtype=jnp.int32)[None, :]
    )
    labels = labels.reshape(-1)

    middle = inner // 2
    down = exchanged(slices(adapter_down_maps[0].T))
    down_near, down_far = rings(joined(down[:middle], AHEAD), joined(down[middle:], AHEAD), SLIGHTLY_AHEAD, SLIGHTLY_AHEAD)
    ids = token_adapter_index.reshape(1, tok)
    rows = swap(outgoing_rows(after(hidden, down_near[0]), ids, members))
    up = exchanged([after(block, down_near[1]) for block in slices(adapter_up_maps[0])])

    down_maps = [m for pair in zip(down_near, down_far) for m in pair]
    packed, id_rows = down_product(labels, rows, down_maps, rank)
    up_near, up_far = rings(
        after(jnp.concatenate(up[:middle], axis=0), down_near[-1]),
        joined([after(block, down_far[-1]) for block in up[middle:]], 0),
        SLIGHTLY_AHEAD,
        0,
        far_second_after=[packed],
    )
    up_maps = [m for pair in zip(up_near, up_far) for m in pair]
    shrunk = swap(summed_copies(swap(packed)))
    offsets = sorted(range(1, members), key=lambda n: (-(n >= inner) - (n % inner >= 2), -(n >= inner), n)) + [0]
    results = []
    for some in offsets[: members // 4], offsets[members // 4 :]:
        results += up_product(labels, me.reshape(1), id_rows, shrunk, up_maps, rank, some)
    returned = [to_partner(r, PLANE, members, n) for r, n in zip(results[:-1], offsets)]
    return place(me.reshape(1), offsets, returned + results[-1:])


def solution(mesh):
    groups, wide = mesh.shape["groups"], mesh.shape["wide"]
    outer = 1 << ((wide.bit_length() - 1) // 2)
    fine = Mesh(mesh.devices.reshape(groups, outer, wide // outer), ("groups", "outer", "inner"))
    owner = ("outer", "inner")
    rows = P(("groups",) + owner, None)
    return jax.shard_map(
        per_device,
        mesh=fine,
        in_specs=(rows, rows, P(owner, None, None), P(owner, None, None)),
        out_specs=rows,
        check_vma=False,
    )
```

```python
import functools
import math

import jax
import jax.numpy as jnp
from jax import lax
from jax.experimental import pallas as pl
from jax.experimental.pallas import tpu as pltpu
from jax.sharding import Mesh
from jax.sharding import PartitionSpec as P

adapter_scale = 2.0
PLANE = ("groups", "inner")
LANES = 128
ID_ROWS = 8
AHEAD, SLIGHTLY_AHEAD = 10**11, 6 * 10**9
BLOCK = 8
IN_VMEM = pl.BlockSpec(memory_space=pltpu.VMEM)
IN_SMEM = pl.BlockSpec(memory_space=pltpu.SMEM)
ANYWHERE = pl.BlockSpec(memory_space=pl.ANY)


def params(scratch_bytes=0):
    return pltpu.CompilerParams(vmem_limit_bytes=(12 << 20) + 2 * scratch_bytes)


def to_partner(value, axes, size, offset):
    return lax.ppermute(value, axes, [(i, i ^ offset) for i in range(size)])


def next_on_ring(block, outer):
    return lax.ppermute(block, "outer", [(i, (i + 1) % outer) for i in range(outer)])


def after(value, *earlier):
    return lax.optimization_barrier((value,) + earlier)[0]


def swap(value):
    return lax.all_to_all(value, PLANE, split_axis=0, concat_axis=0, tiled=True)


def tile_labels(labels_ref, tile, rank, shape):
    per_tile = LANES // rank
    lane = lax.broadcasted_iota(jnp.int32, shape, 1)
    label = jnp.full(shape, labels_ref[tile * per_tile], jnp.int32)
    for n in range(1, per_tile):
        label = jnp.where(lane >= n * rank, labels_ref[tile * per_tile + n], label)
    return label.astype(jnp.float32)


def join_kernel(*refs):
    blocks, out_ref = refs[:-1], refs[-1]
    rows = blocks[0].shape[0]
    for n, block in enumerate(blocks):
        out_ref[n * rows : (n + 1) * rows, :] = block[...]


def joined(blocks, cost):
    rows, share = blocks[0].shape
    return pl.pallas_call(
        join_kernel,
        out_shape=jax.ShapeDtypeStruct((len(blocks) * rows, share), jnp.bfloat16),
        in_specs=[IN_VMEM] * len(blocks),
        out_specs=IN_VMEM,
        compiler_params=params(),
        cost_estimate=pl.CostEstimate(flops=cost, bytes_accessed=10**6, transcendentals=0),
        name="join_blocks",
    )(*blocks)


def outgoing_kernel(hidden_ref, ids_ref, out_ref, sems):
    members, rows, share = out_ref.shape
    tok = rows - ID_ROWS
    copies = [
        pltpu.make_async_copy(
            hidden_ref.at[:, pl.ds(member * share, share)], out_ref.at[member, pl.ds(0, tok)], sems.at[member]
        )
        for member in range(members)
    ]
    for copy in copies:
        copy.start()
    ids = jnp.broadcast_to(ids_ref[...].astype(jnp.float32).astype(jnp.bfloat16), (ID_ROWS, tok))
    for member in range(members):
        out_ref[member, tok:, :tok] = ids
        if share > tok:
            out_ref[member, tok:, tok:] = jnp.zeros((ID_ROWS, share - tok), jnp.bfloat16)
    for copy in copies:
        copy.wait()


def outgoing_rows(hidden, ids, members):
    tok, width = hidden.shape
    share = width // members
    return pl.pallas_call(
        outgoing_kernel,
        out_shape=jax.ShapeDtypeStruct((members, tok + ID_ROWS, share), jnp.bfloat16),
        in_specs=[ANYWHERE, IN_VMEM],
        out_specs=IN_VMEM,
        scratch_shapes=[pltpu.SemaphoreType.DMA((members,))],
        compiler_params=params(),
        name="outgoing_rows",
    )(hidden, ids)


def down_kernel(map_count, rank, labels_ref, rows_ref, *refs):
    maps, (packed_ref, id_rows_ref, total_ref, ids_ref) = refs[:map_count], refs[map_count:]
    members, rows, share = rows_ref.shape
    tok = rows - ID_ROWS
    block = min(BLOCK, members)
    half = tok // 2
    lane = lax.broadcasted_iota(jnp.int32, (half, LANES), 1)

    def one(step, _):
        first = step * block
        for n in range(block):
            row = rows_ref[first + n, tok : tok + 1, :LANES].astype(jnp.float32)
            id_rows_ref[pl.ds(first + n, 1), :] = row
            ids_ref[n] = jnp.broadcast_to(row, (LANES, tok)).T
        tokens = rows_ref[pl.ds(first, block), :tok, :].reshape(block * tok, share)
        ids = ids_ref[...].reshape(block * tok, LANES)
        tile = 0
        for at in range(0, map_count, 2):
            some = jnp.concatenate([m[...] for m in maps[at : at + 2]], axis=0)
            product = lax.dot_general(
                tokens, some, (((1,), (1,)), ((), ())), preferred_element_type=jnp.float32
            )
            total = jnp.zeros((block * tok, LANES), jnp.float32) if tile == 0 else total_ref[...]
            for n in range(some.shape[0] // LANES):
                named = ids == tile_labels(labels_ref, tile, rank, (1, LANES))
                total += jnp.where(named, product[:, n * LANES : (n + 1) * LANES], 0.0)
                tile += 1
            total_ref[...] = total
        for n in range(block):
            total = total_ref[n * tok : (n + 1) * tok, :]
            total += pltpu.roll(total, LANES // 2, 1)
            packed_ref[first + n] = jnp.where(lane < rank, total[:half], total[half:])
        return 0

    lax.fori_loop(0, members // block, one, 0)


def down_product(labels, rows, maps, rank):
    members, tok, share = rows.shape
    tok -= ID_ROWS
    map_rows = sum(m.shape[0] for m in maps)
    return pl.pallas_call(
        functools.partial(down_kernel, len(maps), rank),
        out_shape=[
            jax.ShapeDtypeStruct((members, tok // 2, LANES), jnp.float32),
            jax.ShapeDtypeStruct((members, tok), jnp.float32),
        ],
        in_specs=[IN_SMEM, IN_VMEM] + [IN_VMEM] * len(maps),
        out_specs=[IN_VMEM, IN_VMEM],
        scratch_shapes=[
            pltpu.VMEM((min(BLOCK, members) * tok, LANES), jnp.float32),
            pltpu.VMEM((min(BLOCK, members), tok, LANES), jnp.float32),
        ],
        compiler_params=params(8 * min(BLOCK, members) * tok * LANES),
        cost_estimate=pl.CostEstimate(
            flops=2 * map_rows * members * tok * share,
            bytes_accessed=2 * share * (map_rows + members * tok),
            transcendentals=0,
        ),
        name="down_product",
    )(labels, rows, *maps)


def copies_kernel(terms_ref, out_ref):
    own = jnp.sum(terms_ref[...], axis=0).astype(jnp.bfloat16)
    for member in range(out_ref.shape[0]):
        out_ref[member] = own


def summed_copies(terms):
    return pl.pallas_call(
        copies_kernel,
        out_shape=jax.ShapeDtypeStruct(terms.shape, jnp.bfloat16),
        in_specs=[IN_VMEM],
        out_specs=IN_VMEM,
        compiler_params=params(),
        name="summed_copies",
    )(terms)


def rows_at_once(members):
    return members if members <= BLOCK else math.gcd(BLOCK, members)


def up_kernel(map_count, rank, offsets, labels_ref, me_ref, ids_ref, shrunk_ref, *refs):
    half, members = shrunk_ref.shape[1], len(offsets)
    maps, outs = refs[:map_count], refs[map_count : map_count + members]
    spread_ref = refs[-1]
    tok = 2 * half
    block = rows_at_once(members)
    tiles = spread_ref.shape[1] // LANES
    lane = lax.broadcasted_iota(jnp.int32, (half, LANES), 1)
    held = jnp.concatenate([m[...] for m in maps], axis=0)
    for first in range(0, members, block):
        for n in range(block):
            member = me_ref[0] ^ offsets[first + n]
            packed = shrunk_ref[member].astype(jnp.float32)
            turned = pltpu.roll(packed, LANES // 2, 1)
            shrunk = jnp.concatenate(
                [jnp.where(lane < rank, packed, turned), jnp.where(lane < rank, turned, packed)], axis=0
            )
            ids = jnp.broadcast_to(ids_ref[pl.ds(member, 1), :], (LANES, tok)).T
            for tile in range(tiles):
                named = ids == tile_labels(labels_ref, tile, rank, (1, LANES))
                spread_ref[n * tok : (n + 1) * tok, tile * LANES : (tile + 1) * LANES] = jnp.where(
                    named, shrunk, 0.0
                ).astype(jnp.bfloat16)
        product = jnp.dot(spread_ref[...], held, preferred_element_type=jnp.float32)
        product = (adapter_scale * product).astype(jnp.bfloat16)
        for n in range(block):
            outs[first + n][...] = product[n * tok : (n + 1) * tok, :]


def up_product(labels, me, ids, shrunk, maps, rank, offsets):
    members, tok = len(offsets), ids.shape[1]
    map_rows, piece = sum(m.shape[0] for m in maps), maps[0].shape[1]
    return pl.pallas_call(
        functools.partial(up_kernel, len(maps), rank, offsets),
        out_shape=[jax.ShapeDtypeStruct((tok, piece), jnp.bfloat16)] * members,
        in_specs=[IN_SMEM, IN_SMEM, IN_VMEM, IN_VMEM] + [IN_VMEM] * len(maps),
        out_specs=[IN_VMEM] * members,
        scratch_shapes=[pltpu.VMEM((rows_at_once(members) * tok, map_rows), jnp.bfloat16)],
        compiler_params=params(2 * rows_at_once(members) * tok * map_rows),
        cost_estimate=pl.CostEstimate(
            flops=2 * map_rows * members * tok * piece,
            bytes_accessed=2 * piece * (map_rows + members * tok),
            transcendentals=0,
        ),
        name="up_product",
    )(labels, me, ids, shrunk, *maps)


def place_kernel(offsets, me_ref, *refs):
    blocks, out_ref, sems = refs[:-2], refs[-2], refs[-1]
    share = blocks[0].shape[1]
    copies = []
    for n, block in enumerate(blocks):
        at = pl.multiple_of((me_ref[0] ^ offsets[n]) * share, LANES)
        copies.append(pltpu.make_async_copy(block, out_ref.at[:, pl.ds(at, share)], sems.at[n]))
    for copy in copies:
        copy.start()
    for copy in copies:
        copy.wait()


def place(me, offsets, blocks):
    tok, share = blocks[0].shape
    return pl.pallas_call(
        functools.partial(place_kernel, offsets),
        out_shape=jax.ShapeDtypeStruct((tok, len(blocks) * share), jnp.bfloat16),
        in_specs=[IN_SMEM] + [ANYWHERE] * len(blocks),
        out_specs=ANYWHERE,
        scratch_shapes=[pltpu.SemaphoreType.DMA((len(blocks),))],
        compiler_params=params(),
        name="place_results",
    )(me, *blocks)


def per_device(token_adapter_index, hidden, adapter_down_maps, adapter_up_maps):
    tok, width = hidden.shape
    groups, outer, inner = (lax.axis_size(a) for a in ("groups", "outer", "inner"))
    group, level, place_in_group = (lax.axis_index(a) for a in ("groups", "outer", "inner"))
    members = groups * inner
    share = width // members
    rank = adapter_up_maps.shape[1]
    me = group * inner + place_in_group

    def slices(array):
        return [
            lax.dynamic_slice_in_dim(array, (me ^ offset) * share, share, axis=1) for offset in range(inner)
        ]

    def exchanged(blocks):
        return blocks[:1] + [to_partner(blocks[n], "inner", inner, n) for n in range(1, inner)]

    def rings(near, far, near_cost, far_cost, far_second_after=()):
        near, far = [near], [far]
        for step in range(1, outer):
            near_block, far_block = near[-1], far[-1]
            if step == 2:
                far_block = after(far_block, *far_second_after)
                if near_cost:
                    near_block = joined([near_block], near_cost)
                if far_cost:
                    far_block = joined([far_block], far_cost)
            near.append(next_on_ring(near_block, outer))
            far.append(next_on_ring(far_block, outer))
        return near, far

    steps_back = jnp.arange(outer, dtype=jnp.int32)[:, None]
    labels = ((level - steps_back + outer) % outer) * inner + (
        place_in_group ^ jnp.arange(inner, dtype=jnp.int32)[None, :]
    )
    labels = labels.reshape(-1)

    middle = inner // 2
    down = exchanged(slices(adapter_down_maps[0].T))
    down_near, down_far = rings(joined(down[:middle], AHEAD), joined(down[middle:], AHEAD), SLIGHTLY_AHEAD, SLIGHTLY_AHEAD)
    ids = token_adapter_index.reshape(1, tok)
    rows = swap(outgoing_rows(after(hidden, down_near[0]), ids, members))
    up = exchanged([after(block, down_near[1]) for block in slices(adapter_up_maps[0])])

    down_maps = [m for pair in zip(down_near, down_far) for m in pair]
    packed, id_rows = down_product(labels, rows, down_maps, rank)
    up_near, up_far = rings(
        after(jnp.concatenate(up[:middle], axis=0), down_near[-1]),
        joined([after(block, down_far[-1]) for block in up[middle:]], SLIGHTLY_AHEAD),
        SLIGHTLY_AHEAD,
        0,
        far_second_after=[packed],
    )
    up_maps = [m for pair in zip(up_near, up_far) for m in pair]
    shrunk = swap(summed_copies(swap(packed)))
    offsets = sorted(range(1, members), key=lambda n: (-(n >= inner) - (n % inner >= 2), -(n >= inner), n)) + [0]
    results = []
    for some in offsets[: members // 4], offsets[members // 4 :]:
        results += up_product(labels, me.reshape(1), id_rows, shrunk, up_maps, rank, some)
    returned = [to_partner(r, PLANE, members, n) for r, n in zip(results[:-1], offsets)]
    return place(me.reshape(1), offsets, returned + results[-1:])


def solution(mesh):
    groups, wide = mesh.shape["groups"], mesh.shape["wide"]
    outer = 1 << ((wide.bit_length() - 1) // 2)
    fine = Mesh(mesh.devices.reshape(groups, outer, wide // outer), ("groups", "outer", "inner"))
    owner = ("outer", "inner")
    rows = P(("groups",) + owner, None)
    return jax.shard_map(
        per_device,
        mesh=fine,
        in_specs=(rows, rows, P(owner, None, None), P(owner, None, None)),
        out_specs=rows,
        check_vma=False,
    )
```

```python
import functools
import math

import jax
import jax.numpy as jnp
from jax import lax
from jax.experimental import pallas as pl
from jax.experimental.pallas import tpu as pltpu
from jax.sharding import Mesh
from jax.sharding import PartitionSpec as P

adapter_scale = 2.0
PLANE = ("groups", "inner")
LANES = 128
ID_ROWS = 8
AHEAD, SLIGHTLY_AHEAD = 10**11, 6 * 10**9
BLOCK = 8
IN_VMEM = pl.BlockSpec(memory_space=pltpu.VMEM)
IN_SMEM = pl.BlockSpec(memory_space=pltpu.SMEM)
ANYWHERE = pl.BlockSpec(memory_space=pl.ANY)


def params(product_bytes=0):
    return pltpu.CompilerParams(vmem_limit_bytes=(12 << 20) + 2 * product_bytes if product_bytes else 5 << 20)


def to_partner(value, axes, size, offset):
    return lax.ppermute(value, axes, [(i, i ^ offset) for i in range(size)])


def next_on_ring(block, outer):
    return lax.ppermute(block, "outer", [(i, (i + 1) % outer) for i in range(outer)])


def after(value, *earlier):
    return lax.optimization_barrier((value,) + earlier)[0]


def swap(value):
    return lax.all_to_all(value, PLANE, split_axis=0, concat_axis=0, tiled=True)


def tile_labels(labels_ref, tile, rank, shape):
    per_tile = LANES // rank
    lane = lax.broadcasted_iota(jnp.int32, shape, 1)
    label = jnp.full(shape, labels_ref[tile * per_tile], jnp.int32)
    for n in range(1, per_tile):
        label = jnp.where(lane >= n * rank, labels_ref[tile * per_tile + n], label)
    return label.astype(jnp.float32)


def join_kernel(*refs):
    blocks, out_ref = refs[:-1], refs[-1]
    rows = blocks[0].shape[0]
    for n, block in enumerate(blocks):
        out_ref[n * rows : (n + 1) * rows, :] = block[...]


def joined(blocks, cost):
    rows, share = blocks[0].shape
    return pl.pallas_call(
        join_kernel,
        out_shape=jax.ShapeDtypeStruct((len(blocks) * rows, share), jnp.bfloat16),
        in_specs=[IN_VMEM] * len(blocks),
        out_specs=IN_VMEM,
        compiler_params=params(),
        cost_estimate=pl.CostEstimate(flops=cost, bytes_accessed=10**6, transcendentals=0),
        name="join_blocks",
    )(*blocks)


def outgoing_kernel(hidden_ref, ids_ref, out_ref, sems):
    members, rows, share = out_ref.shape
    tok = rows - ID_ROWS
    copies = [
        pltpu.make_async_copy(
            hidden_ref.at[:, pl.ds(member * share, share)], out_ref.at[member, pl.ds(0, tok)], sems.at[member]
        )
        for member in range(members)
    ]
    for copy in copies:
        copy.start()
    ids = jnp.broadcast_to(ids_ref[...].astype(jnp.float32).astype(jnp.bfloat16), (ID_ROWS, tok))
    for member in range(members):
        out_ref[member, tok:, :tok] = ids
        if share > tok:
            out_ref[member, tok:, tok:] = jnp.zeros((ID_ROWS, share - tok), jnp.bfloat16)
    for copy in copies:
        copy.wait()


def outgoing_rows(hidden, ids, members):
    tok, width = hidden.shape
    share = width // members
    return pl.pallas_call(
        outgoing_kernel,
        out_shape=jax.ShapeDtypeStruct((members, tok + ID_ROWS, share), jnp.bfloat16),
        in_specs=[ANYWHERE, IN_VMEM],
        out_specs=IN_VMEM,
        scratch_shapes=[pltpu.SemaphoreType.DMA((members,))],
        compiler_params=params(),
        name="outgoing_rows",
    )(hidden, ids)


def down_kernel(map_count, rank, labels_ref, rows_ref, *refs):
    maps, (packed_ref, id_rows_ref, total_ref, ids_ref) = refs[:map_count], refs[map_count:]
    members, rows, share = rows_ref.shape
    tok = rows - ID_ROWS
    block = min(BLOCK, members)
    half = tok // 2
    lane = lax.broadcasted_iota(jnp.int32, (half, LANES), 1)

    def one(step, _):
        first = step * block
        for n in range(block):
            row = rows_ref[first + n, tok : tok + 1, :LANES].astype(jnp.float32)
            id_rows_ref[pl.ds(first + n, 1), :] = row
            ids_ref[n] = jnp.broadcast_to(row, (LANES, tok)).T
        tokens = rows_ref[pl.ds(first, block), :tok, :].reshape(block * tok, share)
        ids = ids_ref[...].reshape(block * tok, LANES)
        tile = 0
        for at in range(0, map_count, 2):
            some = jnp.concatenate([m[...] for m in maps[at : at + 2]], axis=0)
            product = lax.dot_general(
                tokens, some, (((1,), (1,)), ((), ())), preferred_element_type=jnp.float32
            )
            total = jnp.zeros((block * tok, LANES), jnp.float32) if tile == 0 else total_ref[...]
            for n in range(some.shape[0] // LANES):
                named = ids == tile_labels(labels_ref, tile, rank, (1, LANES))
                total += jnp.where(named, product[:, n * LANES : (n + 1) * LANES], 0.0)
                tile += 1
            total_ref[...] = total
        for n in range(block):
            total = total_ref[n * tok : (n + 1) * tok, :]
            total += pltpu.roll(total, LANES // 2, 1)
            packed_ref[first + n] = jnp.where(lane < rank, total[:half], total[half:])
        return 0

    lax.fori_loop(0, members // block, one, 0)


def down_product(labels, rows, maps, rank):
    members, tok, share = rows.shape
    tok -= ID_ROWS
    map_rows = sum(m.shape[0] for m in maps)
    return pl.pallas_call(
        functools.partial(down_kernel, len(maps), rank),
        out_shape=[
            jax.ShapeDtypeStruct((members, tok // 2, LANES), jnp.float32),
            jax.ShapeDtypeStruct((members, tok), jnp.float32),
        ],
        in_specs=[IN_SMEM, IN_VMEM] + [IN_VMEM] * len(maps),
        out_specs=[IN_VMEM, IN_VMEM],
        scratch_shapes=[
            pltpu.VMEM((min(BLOCK, members) * tok, LANES), jnp.float32),
            pltpu.VMEM((min(BLOCK, members), tok, LANES), jnp.float32),
        ],
        compiler_params=params(8 * min(BLOCK, members) * tok * LANES),
        cost_estimate=pl.CostEstimate(
            flops=2 * map_rows * members * tok * share,
            bytes_accessed=2 * share * (map_rows + members * tok),
            transcendentals=0,
        ),
        name="down_product",
    )(labels, rows, *maps)


def copies_kernel(terms_ref, out_ref):
    own = jnp.sum(terms_ref[...], axis=0).astype(jnp.bfloat16)
    for member in range(out_ref.shape[0]):
        out_ref[member] = own


def summed_copies(terms):
    return pl.pallas_call(
        copies_kernel,
        out_shape=jax.ShapeDtypeStruct(terms.shape, jnp.bfloat16),
        in_specs=[IN_VMEM],
        out_specs=IN_VMEM,
        compiler_params=params(),
        name="summed_copies",
    )(terms)


def rows_at_once(members):
    return members if members <= BLOCK else math.gcd(BLOCK, members)


def up_kernel(map_count, rank, offsets, labels_ref, me_ref, ids_ref, shrunk_ref, *refs):
    half, members = shrunk_ref.shape[1], len(offsets)
    maps, outs = refs[:map_count], refs[map_count : map_count + members]
    spread_ref = refs[-1]
    tok = 2 * half
    block = rows_at_once(members)
    tiles = spread_ref.shape[1] // LANES
    lane = lax.broadcasted_iota(jnp.int32, (half, LANES), 1)
    held = jnp.concatenate([m[...] for m in maps], axis=0)
    for first in range(0, members, block):
        for n in range(block):
            member = me_ref[0] ^ offsets[first + n]
            packed = shrunk_ref[member].astype(jnp.float32)
            turned = pltpu.roll(packed, LANES // 2, 1)
            shrunk = jnp.concatenate(
                [jnp.where(lane < rank, packed, turned), jnp.where(lane < rank, turned, packed)], axis=0
            )
            ids = jnp.broadcast_to(ids_ref[pl.ds(member, 1), :], (LANES, tok)).T
            for tile in range(tiles):
                named = ids == tile_labels(labels_ref, tile, rank, (1, LANES))
                spread_ref[n * tok : (n + 1) * tok, tile * LANES : (tile + 1) * LANES] = jnp.where(
                    named, shrunk, 0.0
                ).astype(jnp.bfloat16)
        product = jnp.dot(spread_ref[...], held, preferred_element_type=jnp.float32)
        product = (adapter_scale * product).astype(jnp.bfloat16)
        for n in range(block):
            outs[first + n][...] = product[n * tok : (n + 1) * tok, :]


def up_product(labels, me, ids, shrunk, maps, rank, offsets):
    members, tok = len(offsets), ids.shape[1]
    map_rows, piece = sum(m.shape[0] for m in maps), maps[0].shape[1]
    return pl.pallas_call(
        functools.partial(up_kernel, len(maps), rank, offsets),
        out_shape=[jax.ShapeDtypeStruct((tok, piece), jnp.bfloat16)] * members,
        in_specs=[IN_SMEM, IN_SMEM, IN_VMEM, IN_VMEM] + [IN_VMEM] * len(maps),
        out_specs=[IN_VMEM] * members,
        scratch_shapes=[pltpu.VMEM((rows_at_once(members) * tok, map_rows), jnp.bfloat16)],
        compiler_params=params(2 * rows_at_once(members) * tok * map_rows),
        cost_estimate=pl.CostEstimate(
            flops=2 * map_rows * members * tok * piece,
            bytes_accessed=2 * piece * (map_rows + members * tok),
            transcendentals=0,
        ),
        name="up_product",
    )(labels, me, ids, shrunk, *maps)


def place_kernel(offsets, me_ref, *refs):
    blocks, out_ref, sems = refs[:-2], refs[-2], refs[-1]
    share = blocks[0].shape[1]
    copies = []
    for n, block in enumerate(blocks):
        at = pl.multiple_of((me_ref[0] ^ offsets[n]) * share, LANES)
        copies.append(pltpu.make_async_copy(block, out_ref.at[:, pl.ds(at, share)], sems.at[n]))
    for copy in copies:
        copy.start()
    for copy in copies:
        copy.wait()


def place(me, offsets, blocks):
    tok, share = blocks[0].shape
    return pl.pallas_call(
        functools.partial(place_kernel, offsets),
        out_shape=jax.ShapeDtypeStruct((tok, len(blocks) * share), jnp.bfloat16),
        in_specs=[IN_SMEM] + [ANYWHERE] * len(blocks),
        out_specs=ANYWHERE,
        scratch_shapes=[pltpu.SemaphoreType.DMA((len(blocks),))],
        compiler_params=params(),
        name="place_results",
    )(me, *blocks)


def per_device(token_adapter_index, hidden, adapter_down_maps, adapter_up_maps):
    tok, width = hidden.shape
    groups, outer, inner = (lax.axis_size(a) for a in ("groups", "outer", "inner"))
    group, level, place_in_group = (lax.axis_index(a) for a in ("groups", "outer", "inner"))
    members = groups * inner
    share = width // members
    rank = adapter_up_maps.shape[1]
    me = group * inner + place_in_group

    def slices(array):
        return [
            lax.dynamic_slice_in_dim(array, (me ^ offset) * share, share, axis=1) for offset in range(inner)
        ]

    def exchanged(blocks):
        return blocks[:1] + [to_partner(blocks[n], "inner", inner, n) for n in range(1, inner)]

    def rings(near, far, near_cost, far_cost, far_second_after=()):
        near, far = [near], [far]
        for step in range(1, outer):
            near_block, far_block = near[-1], far[-1]
            if step == 2:
                far_block = after(far_block, *far_second_after)
                if near_cost:
                    near_block = joined([near_block], near_cost)
                if far_cost:
                    far_block = joined([far_block], far_cost)
            near.append(next_on_ring(near_block, outer))
            far.append(next_on_ring(far_block, outer))
        return near, far

    steps_back = jnp.arange(outer, dtype=jnp.int32)[:, None]
    labels = ((level - steps_back + outer) % outer) * inner + (
        place_in_group ^ jnp.arange(inner, dtype=jnp.int32)[None, :]
    )
    labels = labels.reshape(-1)

    middle = inner // 2
    down = exchanged(slices(adapter_down_maps[0].T))
    down_near, down_far = rings(joined(down[:middle], AHEAD), joined(down[middle:], AHEAD), SLIGHTLY_AHEAD, SLIGHTLY_AHEAD)
    ids = token_adapter_index.reshape(1, tok)
    rows = swap(outgoing_rows(after(hidden, down_near[0]), ids, members))
    up = exchanged([after(block, down_near[1]) for block in slices(adapter_up_maps[0])])

    down_maps = [m for pair in zip(down_near, down_far) for m in pair]
    packed, id_rows = down_product(labels, rows, down_maps, rank)
    up_near, up_far = rings(
        after(jnp.concatenate(up[:middle], axis=0), down_near[-1]),
        jnp.concatenate([after(block, down_far[-1]) for block in up[middle:]], axis=0),
        SLIGHTLY_AHEAD,
        0,
        far_second_after=[packed],
    )
    up_maps = [m for pair in zip(up_near, up_far) for m in pair]
    shrunk = swap(summed_copies(swap(packed)))
    offsets = sorted(range(1, members), key=lambda n: (-(n >= inner) - (n % inner >= 2), -(n >= inner), n)) + [0]
    results = []
    for some in offsets[: members // 4], offsets[members // 4 :]:
        results += up_product(labels, me.reshape(1), id_rows, shrunk, up_maps, rank, some)
    returned = [to_partner(r, PLANE, members, n) for r, n in zip(results[:-1], offsets)]
    return place(me.reshape(1), offsets, returned + results[-1:])


def solution(mesh):
    groups, wide = mesh.shape["groups"], mesh.shape["wide"]
    outer = 1 << ((wide.bit_length() - 1) // 2)
    fine = Mesh(mesh.devices.reshape(groups, outer, wide // outer), ("groups", "outer", "inner"))
    owner = ("outer", "inner")
    rows = P(("groups",) + owner, None)
    return jax.shard_map(
        per_device,
        mesh=fine,
        in_specs=(rows, rows, P(owner, None, None), P(owner, None, None)),
        out_specs=rows,
        check_vma=False,
    )
```

```python
import functools

import jax
import jax.numpy as jnp
from jax import lax
from jax.experimental import pallas as pl
from jax.experimental.pallas import tpu as pltpu
from jax.sharding import Mesh
from jax.sharding import PartitionSpec as P

adapter_scale = 2.0
PLANE = ("groups", "inner")
LANES = 128
ID_ROWS = 8
AHEAD, SLIGHTLY_AHEAD = 10**11, 6 * 10**9
BLOCK = 8
IN_VMEM = pl.BlockSpec(memory_space=pltpu.VMEM)
IN_SMEM = pl.BlockSpec(memory_space=pltpu.SMEM)
ANYWHERE = pl.BlockSpec(memory_space=pl.ANY)


def params(scratch_bytes=0):
    return pltpu.CompilerParams(vmem_limit_bytes=(12 << 20) + 2 * scratch_bytes)


def to_partner(value, axes, size, offset):
    return lax.ppermute(value, axes, [(i, i ^ offset) for i in range(size)])


def next_on_ring(block, outer):
    return lax.ppermute(block, "outer", [(i, (i + 1) % outer) for i in range(outer)])


def after(value, *earlier):
    return lax.optimization_barrier((value,) + earlier)[0]


def swap(value):
    return lax.all_to_all(value, PLANE, split_axis=0, concat_axis=0, tiled=True)


def tile_labels(labels_ref, tile, rank, shape):
    per_tile = LANES // rank
    lane = lax.broadcasted_iota(jnp.int32, shape, 1)
    label = jnp.full(shape, labels_ref[tile * per_tile], jnp.int32)
    for n in range(1, per_tile):
        label = jnp.where(lane >= n * rank, labels_ref[tile * per_tile + n], label)
    return label.astype(jnp.float32)


def join_kernel(*refs):
    blocks, out_ref = refs[:-1], refs[-1]
    rows = blocks[0].shape[0]
    for n, block in enumerate(blocks):
        out_ref[n * rows : (n + 1) * rows, :] = block[...]


def joined(blocks, cost):
    rows, share = blocks[0].shape
    return pl.pallas_call(
        join_kernel,
        out_shape=jax.ShapeDtypeStruct((len(blocks) * rows, share), jnp.bfloat16),
        in_specs=[IN_VMEM] * len(blocks),
        out_specs=IN_VMEM,
        compiler_params=params(),
        cost_estimate=pl.CostEstimate(flops=cost, bytes_accessed=10**6, transcendentals=0),
        name="join_blocks",
    )(*blocks)


def outgoing_kernel(hidden_ref, ids_ref, out_ref, sems):
    members, rows, share = out_ref.shape
    tok = rows - ID_ROWS
    copies = [
        pltpu.make_async_copy(
            hidden_ref.at[:, pl.ds(member * share, share)], out_ref.at[member, pl.ds(0, tok)], sems.at[member]
        )
        for member in range(members)
    ]
    for copy in copies:
        copy.start()
    ids = jnp.broadcast_to(ids_ref[...].astype(jnp.float32).astype(jnp.bfloat16), (ID_ROWS, tok))
    for member in range(members):
        out_ref[member, tok:, :tok] = ids
        if share > tok:
            out_ref[member, tok:, tok:] = jnp.zeros((ID_ROWS, share - tok), jnp.bfloat16)
    for copy in copies:
        copy.wait()


def outgoing_rows(hidden, ids, members):
    tok, width = hidden.shape
    share = width // members
    return pl.pallas_call(
        outgoing_kernel,
        out_shape=jax.ShapeDtypeStruct((members, tok + ID_ROWS, share), jnp.bfloat16),
        in_specs=[ANYWHERE, IN_VMEM],
        out_specs=IN_VMEM,
        scratch_shapes=[pltpu.SemaphoreType.DMA((members,))],
        compiler_params=params(),
        name="outgoing_rows",
    )(hidden, ids)


def down_kernel(map_count, rank, labels_ref, rows_ref, *refs):
    maps, (packed_ref, id_rows_ref, total_ref, ids_ref) = refs[:map_count], refs[map_count:]
    members, rows, share = rows_ref.shape
    tok = rows - ID_ROWS
    block = min(BLOCK, members)
    half = tok // 2
    lane = lax.broadcasted_iota(jnp.int32, (half, LANES), 1)

    def one(step, _):
        first = step * block
        for n in range(block):
            row = rows_ref[first + n, tok : tok + 1, :LANES].astype(jnp.float32)
            id_rows_ref[pl.ds(first + n, 1), :] = row
            ids_ref[n] = jnp.broadcast_to(row, (LANES, tok)).T
        tokens = rows_ref[pl.ds(first, block), :tok, :].reshape(block * tok, share)
        ids = ids_ref[...].reshape(block * tok, LANES)
        tile = 0
        for at in range(0, map_count, 2):
            some = jnp.concatenate([m[...] for m in maps[at : at + 2]], axis=0)
            product = lax.dot_general(
                tokens, some, (((1,), (1,)), ((), ())), preferred_element_type=jnp.float32
            )
            total = jnp.zeros((block * tok, LANES), jnp.float32) if tile == 0 else total_ref[...]
            for n in range(some.shape[0] // LANES):
                named = ids == tile_labels(labels_ref, tile, rank, (1, LANES))
                total += jnp.where(named, product[:, n * LANES : (n + 1) * LANES], 0.0)
                tile += 1
            total_ref[...] = total
        for n in range(block):
            total = total_ref[n * tok : (n + 1) * tok, :]
            total += pltpu.roll(total, LANES // 2, 1)
            packed_ref[first + n] = jnp.where(lane < rank, total[:half], total[half:]).astype(jnp.bfloat16)
        return 0

    lax.fori_loop(0, members // block, one, 0)


def down_product(labels, rows, maps, rank):
    members, tok, share = rows.shape
    tok -= ID_ROWS
    map_rows = sum(m.shape[0] for m in maps)
    return pl.pallas_call(
        functools.partial(down_kernel, len(maps), rank),
        out_shape=[
            jax.ShapeDtypeStruct((members, tok // 2, LANES), jnp.bfloat16),
            jax.ShapeDtypeStruct((members, tok), jnp.float32),
        ],
        in_specs=[IN_SMEM, IN_VMEM] + [IN_VMEM] * len(maps),
        out_specs=[IN_VMEM, IN_VMEM],
        scratch_shapes=[
            pltpu.VMEM((min(BLOCK, members) * tok, LANES), jnp.float32),
            pltpu.VMEM((min(BLOCK, members), tok, LANES), jnp.float32),
        ],
        compiler_params=params(8 * min(BLOCK, members) * tok * LANES),
        cost_estimate=pl.CostEstimate(
            flops=2 * map_rows * members * tok * share,
            bytes_accessed=2 * share * (map_rows + members * tok),
            transcendentals=0,
        ),
        name="down_product",
    )(labels, rows, *maps)


def copies_kernel(terms_ref, out_ref):
    own = jnp.sum(terms_ref[...].astype(jnp.float32), axis=0).astype(jnp.bfloat16)
    for member in range(out_ref.shape[0]):
        out_ref[member] = own


def summed_copies(terms):
    return pl.pallas_call(
        copies_kernel,
        out_shape=jax.ShapeDtypeStruct(terms.shape, jnp.bfloat16),
        in_specs=[IN_VMEM],
        out_specs=IN_VMEM,
        compiler_params=params(),
        name="summed_copies",
    )(terms)


def up_kernel(map_count, rank, offsets, labels_ref, me_ref, ids_ref, shrunk_ref, *refs):
    half, members = shrunk_ref.shape[1], len(offsets)
    maps, outs = refs[:map_count], refs[map_count : map_count + members]
    spread_ref = refs[-1]
    tok = 2 * half
    block = min(BLOCK, members)
    tiles = spread_ref.shape[1] // LANES
    lane = lax.broadcasted_iota(jnp.int32, (half, LANES), 1)
    held = jnp.concatenate([m[...] for m in maps], axis=0)
    for first in range(0, members, block):
        for n in range(block):
            member = me_ref[0] ^ offsets[first + n]
            packed = shrunk_ref[member].astype(jnp.float32)
            turned = pltpu.roll(packed, LANES // 2, 1)
            shrunk = jnp.concatenate(
                [jnp.where(lane < rank, packed, turned), jnp.where(lane < rank, turned, packed)], axis=0
            )
            ids = jnp.broadcast_to(ids_ref[pl.ds(member, 1), :], (LANES, tok)).T
            for tile in range(tiles):
                named = ids == tile_labels(labels_ref, tile, rank, (1, LANES))
                spread_ref[n * tok : (n + 1) * tok, tile * LANES : (tile + 1) * LANES] = jnp.where(
                    named, shrunk, 0.0
                ).astype(jnp.bfloat16)
        product = jnp.dot(spread_ref[...], held, preferred_element_type=jnp.float32)
        product = (adapter_scale * product).astype(jnp.bfloat16)
        for n in range(block):
            outs[first + n][...] = product[n * tok : (n + 1) * tok, :]


def up_product(labels, me, ids, shrunk, maps, rank, offsets):
    members, tok = len(offsets), ids.shape[1]
    map_rows, piece = sum(m.shape[0] for m in maps), maps[0].shape[1]
    return pl.pallas_call(
        functools.partial(up_kernel, len(maps), rank, offsets),
        out_shape=[jax.ShapeDtypeStruct((tok, piece), jnp.bfloat16)] * members,
        in_specs=[IN_SMEM, IN_SMEM, IN_VMEM, IN_VMEM] + [IN_VMEM] * len(maps),
        out_specs=[IN_VMEM] * members,
        scratch_shapes=[pltpu.VMEM((min(BLOCK, members) * tok, map_rows), jnp.bfloat16)],
        compiler_params=params(2 * min(BLOCK, members) * tok * map_rows),
        cost_estimate=pl.CostEstimate(
            flops=2 * map_rows * members * tok * piece,
            bytes_accessed=2 * piece * (map_rows + members * tok),
            transcendentals=0,
        ),
        name="up_product",
    )(labels, me, ids, shrunk, *maps)


def place_kernel(offsets, me_ref, *refs):
    blocks, out_ref, sems = refs[:-2], refs[-2], refs[-1]
    share = blocks[0].shape[1]
    copies = []
    for n, block in enumerate(blocks):
        at = pl.multiple_of((me_ref[0] ^ offsets[n]) * share, LANES)
        copies.append(pltpu.make_async_copy(block, out_ref.at[:, pl.ds(at, share)], sems.at[n]))
    for copy in copies:
        copy.start()
    for copy in copies:
        copy.wait()


def place(me, offsets, blocks):
    tok, share = blocks[0].shape
    return pl.pallas_call(
        functools.partial(place_kernel, offsets),
        out_shape=jax.ShapeDtypeStruct((tok, len(blocks) * share), jnp.bfloat16),
        in_specs=[IN_SMEM] + [ANYWHERE] * len(blocks),
        out_specs=ANYWHERE,
        scratch_shapes=[pltpu.SemaphoreType.DMA((len(blocks),))],
        compiler_params=params(),
        name="place_results",
    )(me, *blocks)


def per_device(token_adapter_index, hidden, adapter_down_maps, adapter_up_maps):
    tok, width = hidden.shape
    groups, outer, inner = (lax.axis_size(a) for a in ("groups", "outer", "inner"))
    group, level, place_in_group = (lax.axis_index(a) for a in ("groups", "outer", "inner"))
    members = groups * inner
    share = width // members
    rank = adapter_up_maps.shape[1]
    me = group * inner + place_in_group

    def slices(array):
        return [
            lax.dynamic_slice_in_dim(array, (me ^ offset) * share, share, axis=1) for offset in range(inner)
        ]

    def exchanged(blocks):
        return blocks[:1] + [to_partner(blocks[n], "inner", inner, n) for n in range(1, inner)]

    def rings(near, far, near_cost, far_cost, far_second_after=()):
        near, far = [near], [far]
        for step in range(1, outer):
            near_block, far_block = near[-1], far[-1]
            if step == 2:
                far_block = after(far_block, *far_second_after)
                if near_cost:
                    near_block = joined([near_block], near_cost)
                if far_cost:
                    far_block = joined([far_block], far_cost)
            near.append(next_on_ring(near_block, outer))
            far.append(next_on_ring(far_block, outer))
        return near, far

    steps_back = jnp.arange(outer, dtype=jnp.int32)[:, None]
    labels = ((level - steps_back + outer) % outer) * inner + (
        place_in_group ^ jnp.arange(inner, dtype=jnp.int32)[None, :]
    )
    labels = labels.reshape(-1)

    middle = inner // 2
    down = exchanged(slices(adapter_down_maps[0].T))
    down_near, down_far = rings(joined(down[:middle], AHEAD), joined(down[middle:], AHEAD), SLIGHTLY_AHEAD, SLIGHTLY_AHEAD)
    ids = token_adapter_index.reshape(1, tok)
    rows = swap(outgoing_rows(after(hidden, down_near[0]), ids, members))
    own_up = [after(block, down_near[1]) for block in slices(adapter_up_maps[0])]
    halves = [jnp.concatenate([own_up[n], own_up[n + middle]], axis=0) for n in range(middle)]
    halves = halves[:1] + [to_partner(halves[n], "inner", inner, n) for n in range(1, middle)]
    up_first_near = jnp.concatenate([h[:rank] for h in halves], axis=0)
    up_first_far = to_partner(jnp.concatenate([h[rank:] for h in halves], axis=0), "inner", inner, middle)

    down_maps = [m for pair in zip(down_near, down_far) for m in pair]
    packed, id_rows = down_product(labels, rows, down_maps, rank)
    up_near, up_far = rings(
        after(up_first_near, down_near[-1]),
        after(up_first_far, down_far[-1]),
        SLIGHTLY_AHEAD,
        0,
        far_second_after=[packed],
    )
    up_maps = [m for pair in zip(up_near, up_far) for m in pair]
    shrunk = swap(summed_copies(swap(packed)))
    offsets = sorted(range(1, members), key=lambda n: (-(n >= inner) - (n % inner >= 2), -(n >= inner), n)) + [0]
    results = []
    for some in offsets[: members // 2], offsets[members // 2 :]:
        results += up_product(labels, me.reshape(1), id_rows, shrunk, up_maps, rank, some)
    returned = [to_partner(r, PLANE, members, n) for r, n in zip(results[:-1], offsets)]
    return place(me.reshape(1), offsets, returned + results[-1:])


def solution(mesh):
    groups, wide = mesh.shape["groups"], mesh.shape["wide"]
    outer = 1 << ((wide.bit_length() - 1) // 2)
    fine = Mesh(mesh.devices.reshape(groups, outer, wide // outer), ("groups", "outer", "inner"))
    owner = ("outer", "inner")
    rows = P(("groups",) + owner, None)
    return jax.shard_map(
        per_device,
        mesh=fine,
        in_specs=(rows, rows, P(owner, None, None), P(owner, None, None)),
        out_specs=rows,
        check_vma=False,
    )
```

```python
import functools

import jax
import jax.numpy as jnp
from jax import lax
from jax.experimental import pallas as pl
from jax.experimental.pallas import tpu as pltpu
from jax.sharding import Mesh
from jax.sharding import PartitionSpec as P

adapter_scale = 2.0
PLANE = ("groups", "inner")
LANES = 128
ID_ROWS = 8
AHEAD, SLIGHTLY_AHEAD = 10**11, 6 * 10**9
BLOCK = 8
IN_VMEM = pl.BlockSpec(memory_space=pltpu.VMEM)
IN_SMEM = pl.BlockSpec(memory_space=pltpu.SMEM)
ANYWHERE = pl.BlockSpec(memory_space=pl.ANY)


def params(scratch_bytes=0):
    return pltpu.CompilerParams(vmem_limit_bytes=(12 << 20) + 2 * scratch_bytes)


def to_partner(value, axes, size, offset):
    return lax.ppermute(value, axes, [(i, i ^ offset) for i in range(size)])


def next_on_ring(block, outer):
    return lax.ppermute(block, "outer", [(i, (i + 1) % outer) for i in range(outer)])


def after(value, *earlier):
    return lax.optimization_barrier((value,) + earlier)[0]


def swap(value):
    return lax.all_to_all(value, PLANE, split_axis=0, concat_axis=0, tiled=True)


def tile_labels(labels_ref, tile, rank, shape):
    per_tile = LANES // rank
    lane = lax.broadcasted_iota(jnp.int32, shape, 1)
    label = jnp.full(shape, labels_ref[tile * per_tile], jnp.int32)
    for n in range(1, per_tile):
        label = jnp.where(lane >= n * rank, labels_ref[tile * per_tile + n], label)
    return label.astype(jnp.float32)


def join_kernel(*refs):
    blocks, out_ref = refs[:-1], refs[-1]
    rows = blocks[0].shape[0]
    for n, block in enumerate(blocks):
        out_ref[n * rows : (n + 1) * rows, :] = block[...]


def joined(blocks, cost):
    rows, share = blocks[0].shape
    return pl.pallas_call(
        join_kernel,
        out_shape=jax.ShapeDtypeStruct((len(blocks) * rows, share), jnp.bfloat16),
        in_specs=[IN_VMEM] * len(blocks),
        out_specs=IN_VMEM,
        compiler_params=params(),
        cost_estimate=pl.CostEstimate(flops=cost, bytes_accessed=10**6, transcendentals=0),
        name="join_blocks",
    )(*blocks)


def outgoing_kernel(hidden_ref, ids_ref, out_ref, sems):
    members, rows, share = out_ref.shape
    tok = rows - ID_ROWS
    copies = [
        pltpu.make_async_copy(
            hidden_ref.at[:, pl.ds(member * share, share)], out_ref.at[member, pl.ds(0, tok)], sems.at[member]
        )
        for member in range(members)
    ]
    for copy in copies:
        copy.start()
    ids = jnp.broadcast_to(ids_ref[...].astype(jnp.float32).astype(jnp.bfloat16), (ID_ROWS, tok))
    for member in range(members):
        out_ref[member, tok:, :tok] = ids
        if share > tok:
            out_ref[member, tok:, tok:] = jnp.zeros((ID_ROWS, share - tok), jnp.bfloat16)
    for copy in copies:
        copy.wait()


def outgoing_rows(hidden, ids, members):
    tok, width = hidden.shape
    share = width // members
    return pl.pallas_call(
        outgoing_kernel,
        out_shape=jax.ShapeDtypeStruct((members, tok + ID_ROWS, share), jnp.bfloat16),
        in_specs=[ANYWHERE, IN_VMEM],
        out_specs=IN_VMEM,
        scratch_shapes=[pltpu.SemaphoreType.DMA((members,))],
        compiler_params=params(),
        name="outgoing_rows",
    )(hidden, ids)


def down_kernel(map_count, rank, labels_ref, rows_ref, *refs):
    maps, (packed_ref, id_rows_ref, total_ref, ids_ref) = refs[:map_count], refs[map_count:]
    members, rows, share = rows_ref.shape
    tok = rows - ID_ROWS
    block = min(BLOCK, members)
    half = tok // 2
    lane = lax.broadcasted_iota(jnp.int32, (half, LANES), 1)

    def one(step, _):
        first = step * block
        for n in range(block):
            row = rows_ref[first + n, tok : tok + 1, :LANES].astype(jnp.float32)
            id_rows_ref[pl.ds(first + n, 1), :] = row
            ids_ref[n] = jnp.broadcast_to(row, (LANES, tok)).T
        tokens = rows_ref[pl.ds(first, block), :tok, :].reshape(block * tok, share)
        ids = ids_ref[...].reshape(block * tok, LANES)
        tile = 0
        for at in range(0, map_count, 2):
            some = jnp.concatenate([m[...] for m in maps[at : at + 2]], axis=0)
            product = lax.dot_general(
                tokens, some, (((1,), (1,)), ((), ())), preferred_element_type=jnp.float32
            )
            total = jnp.zeros((block * tok, LANES), jnp.float32) if tile == 0 else total_ref[...]
            for n in range(some.shape[0] // LANES):
                named = ids == tile_labels(labels_ref, tile, rank, (1, LANES))
                total += jnp.where(named, product[:, n * LANES : (n + 1) * LANES], 0.0)
                tile += 1
            total_ref[...] = total
        for n in range(block):
            total = total_ref[n * tok : (n + 1) * tok, :]
            total += pltpu.roll(total, LANES // 2, 1)
            packed_ref[first + n] = jnp.where(lane < rank, total[:half], total[half:])
        return 0

    lax.fori_loop(0, members // block, one, 0)


def down_product(labels, rows, maps, rank):
    members, tok, share = rows.shape
    tok -= ID_ROWS
    map_rows = sum(m.shape[0] for m in maps)
    return pl.pallas_call(
        functools.partial(down_kernel, len(maps), rank),
        out_shape=[
            jax.ShapeDtypeStruct((members, tok // 2, LANES), jnp.float32),
            jax.ShapeDtypeStruct((members, tok), jnp.float32),
        ],
        in_specs=[IN_SMEM, IN_VMEM] + [IN_VMEM] * len(maps),
        out_specs=[IN_VMEM, IN_VMEM],
        scratch_shapes=[
            pltpu.VMEM((min(BLOCK, members) * tok, LANES), jnp.float32),
            pltpu.VMEM((min(BLOCK, members), tok, LANES), jnp.float32),
        ],
        compiler_params=params(8 * min(BLOCK, members) * tok * LANES),
        cost_estimate=pl.CostEstimate(
            flops=2 * map_rows * members * tok * share,
            bytes_accessed=2 * share * (map_rows + members * tok),
            transcendentals=0,
        ),
        name="down_product",
    )(labels, rows, *maps)


def copies_kernel(terms_ref, out_ref):
    own = jnp.sum(terms_ref[...], axis=0).astype(jnp.bfloat16)
    for member in range(out_ref.shape[0]):
        out_ref[member] = own


def summed_copies(terms):
    return pl.pallas_call(
        copies_kernel,
        out_shape=jax.ShapeDtypeStruct(terms.shape, jnp.bfloat16),
        in_specs=[IN_VMEM],
        out_specs=IN_VMEM,
        compiler_params=params(),
        name="summed_copies",
    )(terms)


def up_kernel(map_count, rank, offsets, labels_ref, me_ref, ids_ref, shrunk_ref, *refs):
    half, members = shrunk_ref.shape[1], len(offsets)
    maps, outs = refs[:map_count], refs[map_count : map_count + members]
    spread_ref = refs[-1]
    tok = 2 * half
    block = min(BLOCK, members)
    tiles = spread_ref.shape[1] // LANES
    lane = lax.broadcasted_iota(jnp.int32, (half, LANES), 1)
    held = jnp.concatenate([m[...] for m in maps], axis=0)
    for first in range(0, members, block):
        for n in range(block):
            member = me_ref[0] ^ offsets[first + n]
            packed = shrunk_ref[member].astype(jnp.float32)
            turned = pltpu.roll(packed, LANES // 2, 1)
            shrunk = jnp.concatenate(
                [jnp.where(lane < rank, packed, turned), jnp.where(lane < rank, turned, packed)], axis=0
            )
            ids = jnp.broadcast_to(ids_ref[pl.ds(member, 1), :], (LANES, tok)).T
            for tile in range(tiles):
                named = ids == tile_labels(labels_ref, tile, rank, (1, LANES))
                spread_ref[n * tok : (n + 1) * tok, tile * LANES : (tile + 1) * LANES] = jnp.where(
                    named, shrunk, 0.0
                ).astype(jnp.bfloat16)
        product = jnp.dot(spread_ref[...], held, preferred_element_type=jnp.float32)
        product = (adapter_scale * product).astype(jnp.bfloat16)
        for n in range(block):
            outs[first + n][...] = product[n * tok : (n + 1) * tok, :]


def up_product(labels, me, ids, shrunk, maps, rank, offsets):
    members, tok = len(offsets), ids.shape[1]
    map_rows, piece = sum(m.shape[0] for m in maps), maps[0].shape[1]
    return pl.pallas_call(
        functools.partial(up_kernel, len(maps), rank, offsets),
        out_shape=[jax.ShapeDtypeStruct((tok, piece), jnp.bfloat16)] * members,
        in_specs=[IN_SMEM, IN_SMEM, IN_VMEM, IN_VMEM] + [IN_VMEM] * len(maps),
        out_specs=[IN_VMEM] * members,
        scratch_shapes=[pltpu.VMEM((min(BLOCK, members) * tok, map_rows), jnp.bfloat16)],
        compiler_params=params(2 * min(BLOCK, members) * tok * map_rows),
        cost_estimate=pl.CostEstimate(
            flops=2 * map_rows * members * tok * piece,
            bytes_accessed=2 * piece * (map_rows + members * tok),
            transcendentals=0,
        ),
        name="up_product",
    )(labels, me, ids, shrunk, *maps)


def place_kernel(offsets, me_ref, *refs):
    blocks, out_ref, sems = refs[:-2], refs[-2], refs[-1]
    share = blocks[0].shape[1]
    copies = []
    for n, block in enumerate(blocks):
        at = pl.multiple_of((me_ref[0] ^ offsets[n]) * share, LANES)
        copies.append(pltpu.make_async_copy(block, out_ref.at[:, pl.ds(at, share)], sems.at[n]))
    for copy in copies:
        copy.start()
    for copy in copies:
        copy.wait()


def place(me, offsets, blocks):
    tok, share = blocks[0].shape
    return pl.pallas_call(
        functools.partial(place_kernel, offsets),
        out_shape=jax.ShapeDtypeStruct((tok, len(blocks) * share), jnp.bfloat16),
        in_specs=[IN_SMEM] + [ANYWHERE] * len(blocks),
        out_specs=ANYWHERE,
        scratch_shapes=[pltpu.SemaphoreType.DMA((len(blocks),))],
        compiler_params=params(),
        name="place_results",
    )(me, *blocks)


def per_device(token_adapter_index, hidden, adapter_down_maps, adapter_up_maps):
    tok, width = hidden.shape
    groups, outer, inner = (lax.axis_size(a) for a in ("groups", "outer", "inner"))
    group, level, place_in_group = (lax.axis_index(a) for a in ("groups", "outer", "inner"))
    members = groups * inner
    share = width // members
    rank = adapter_up_maps.shape[1]
    me = group * inner + place_in_group

    def slices(array):
        return [
            lax.dynamic_slice_in_dim(array, (me ^ offset) * share, share, axis=1) for offset in range(inner)
        ]

    def exchanged(blocks):
        return blocks[:1] + [to_partner(blocks[n], "inner", inner, n) for n in range(1, inner)]

    def rings(near, far, near_cost, far_cost, far_second_after=()):
        near, far = [near], [far]
        for step in range(1, outer):
            near_block, far_block = near[-1], far[-1]
            if step == 2:
                far_block = after(far_block, *far_second_after)
                if near_cost:
                    near_block = joined([near_block], near_cost)
                if far_cost:
                    far_block = joined([far_block], far_cost)
            near.append(next_on_ring(near_block, outer))
            far.append(next_on_ring(far_block, outer))
        return near, far

    steps_back = jnp.arange(outer, dtype=jnp.int32)[:, None]
    labels = ((level - steps_back + outer) % outer) * inner + (
        place_in_group ^ jnp.arange(inner, dtype=jnp.int32)[None, :]
    )
    labels = labels.reshape(-1)

    middle = inner // 2
    down = exchanged(slices(adapter_down_maps[0].T))
    down_near, down_far = rings(joined(down[:middle], AHEAD), joined(down[middle:], AHEAD), SLIGHTLY_AHEAD, SLIGHTLY_AHEAD)
    ids = token_adapter_index.reshape(1, tok)
    rows = swap(outgoing_rows(after(hidden, down_near[0]), ids, members))
    up = exchanged([after(block, down_near[1]) for block in slices(adapter_up_maps[0])])

    down_maps = [m for pair in zip(down_near, down_far) for m in pair]
    packed, id_rows = down_product(labels, rows, down_maps, rank)
    up_near, up_far = rings(
        after(jnp.concatenate(up[:middle], axis=0), down_near[-1]),
        joined([after(block, down_far[-1]) for block in up[middle:]], SLIGHTLY_AHEAD // 4),
        SLIGHTLY_AHEAD,
        0,
        far_second_after=[packed],
    )
    up_maps = [m for pair in zip(up_near, up_far) for m in pair]
    shrunk = swap(summed_copies(swap(packed)))
    offsets = sorted(range(1, members), key=lambda n: (-(n >= inner) - (n % inner >= 2), -(n >= inner), n)) + [0]
    results = []
    for some in offsets[: members // 2], offsets[members // 2 :]:
        results += up_product(labels, me.reshape(1), id_rows, shrunk, up_maps, rank, some)
    returned = [to_partner(r, PLANE, members, n) for r, n in zip(results[:-1], offsets)]
    return place(me.reshape(1), offsets, returned + results[-1:])


def solution(mesh):
    groups, wide = mesh.shape["groups"], mesh.shape["wide"]
    outer = 1 << ((wide.bit_length() - 1) // 2)
    fine = Mesh(mesh.devices.reshape(groups, outer, wide // outer), ("groups", "outer", "inner"))
    owner = ("outer", "inner")
    rows = P(("groups",) + owner, None)
    return jax.shard_map(
        per_device,
        mesh=fine,
        in_specs=(rows, rows, P(owner, None, None), P(owner, None, None)),
        out_specs=rows,
        check_vma=False,
    )
```

```python
import functools

import jax
import jax.numpy as jnp
from jax import lax
from jax.experimental import pallas as pl
from jax.experimental.pallas import tpu as pltpu
from jax.sharding import Mesh
from jax.sharding import PartitionSpec as P

adapter_scale = 2.0
PLANE = ("groups", "inner")
LANES = 128
ID_ROWS = 8
AHEAD, SLIGHTLY_AHEAD = 10**11, 6 * 10**9
BLOCK = 8
IN_VMEM = pl.BlockSpec(memory_space=pltpu.VMEM)
IN_SMEM = pl.BlockSpec(memory_space=pltpu.SMEM)
ANYWHERE = pl.BlockSpec(memory_space=pl.ANY)


def params(scratch_bytes=0):
    return pltpu.CompilerParams(vmem_limit_bytes=(12 << 20) + 2 * scratch_bytes)


def to_partner(value, axes, size, offset):
    return lax.ppermute(value, axes, [(i, i ^ offset) for i in range(size)])


def next_on_ring(block, outer):
    return lax.ppermute(block, "outer", [(i, (i + 1) % outer) for i in range(outer)])


def after(value, *earlier):
    return lax.optimization_barrier((value,) + earlier)[0]


def swap(value):
    return lax.all_to_all(value, PLANE, split_axis=0, concat_axis=0, tiled=True)


def tile_labels(labels_ref, tile, rank, shape):
    per_tile = LANES // rank
    lane = lax.broadcasted_iota(jnp.int32, shape, 1)
    label = jnp.full(shape, labels_ref[tile * per_tile], jnp.int32)
    for n in range(1, per_tile):
        label = jnp.where(lane >= n * rank, labels_ref[tile * per_tile + n], label)
    return label.astype(jnp.float32)


def join_kernel(*refs):
    blocks, out_ref = refs[:-1], refs[-1]
    rows = blocks[0].shape[0]
    for n, block in enumerate(blocks):
        out_ref[n * rows : (n + 1) * rows, :] = block[...]


def joined(blocks, cost):
    rows, share = blocks[0].shape
    return pl.pallas_call(
        join_kernel,
        out_shape=jax.ShapeDtypeStruct((len(blocks) * rows, share), jnp.bfloat16),
        in_specs=[IN_VMEM] * len(blocks),
        out_specs=IN_VMEM,
        compiler_params=params(),
        cost_estimate=pl.CostEstimate(flops=cost, bytes_accessed=10**6, transcendentals=0),
        name="join_blocks",
    )(*blocks)


def outgoing_kernel(hidden_ref, ids_ref, out_ref, sems):
    members, rows, share = out_ref.shape
    tok = rows - ID_ROWS
    copies = [
        pltpu.make_async_copy(
            hidden_ref.at[:, pl.ds(member * share, share)], out_ref.at[member, pl.ds(0, tok)], sems.at[member]
        )
        for member in range(members)
    ]
    for copy in copies:
        copy.start()
    ids = jnp.broadcast_to(ids_ref[...].astype(jnp.float32).astype(jnp.bfloat16), (ID_ROWS, tok))
    for member in range(members):
        out_ref[member, tok:, :tok] = ids
        if share > tok:
            out_ref[member, tok:, tok:] = jnp.zeros((ID_ROWS, share - tok), jnp.bfloat16)
    for copy in copies:
        copy.wait()


def outgoing_rows(hidden, ids, members):
    tok, width = hidden.shape
    share = width // members
    return pl.pallas_call(
        outgoing_kernel,
        out_shape=jax.ShapeDtypeStruct((members, tok + ID_ROWS, share), jnp.bfloat16),
        in_specs=[ANYWHERE, IN_VMEM],
        out_specs=IN_VMEM,
        scratch_shapes=[pltpu.SemaphoreType.DMA((members,))],
        compiler_params=params(),
        name="outgoing_rows",
    )(hidden, ids)


def down_kernel(map_count, rank, labels_ref, rows_ref, *refs):
    maps, (packed_ref, id_rows_ref, total_ref, ids_ref) = refs[:map_count], refs[map_count:]
    members, rows, share = rows_ref.shape
    tok = rows - ID_ROWS
    block = min(BLOCK, members)
    half = tok // 2
    lane = lax.broadcasted_iota(jnp.int32, (half, LANES), 1)

    def one(step, _):
        first = step * block
        for n in range(block):
            row = rows_ref[first + n, tok : tok + 1, :LANES].astype(jnp.float32)
            id_rows_ref[pl.ds(first + n, 1), :] = row
            ids_ref[n] = jnp.broadcast_to(row, (LANES, tok)).T
        tokens = rows_ref[pl.ds(first, block), :tok, :].reshape(block * tok, share)
        ids = ids_ref[...].reshape(block * tok, LANES)
        tile = 0
        for at in range(0, map_count, 2):
            some = jnp.concatenate([m[...] for m in maps[at : at + 2]], axis=0)
            product = lax.dot_general(
                tokens, some, (((1,), (1,)), ((), ())), preferred_element_type=jnp.float32
            )
            total = jnp.zeros((block * tok, LANES), jnp.float32) if tile == 0 else total_ref[...]
            for n in range(some.shape[0] // LANES):
                named = ids == tile_labels(labels_ref, tile, rank, (1, LANES))
                total += jnp.where(named, product[:, n * LANES : (n + 1) * LANES], 0.0)
                tile += 1
            total_ref[...] = total
        for n in range(block):
            total = total_ref[n * tok : (n + 1) * tok, :]
            total += pltpu.roll(total, LANES // 2, 1)
            packed_ref[first + n] = jnp.where(lane < rank, total[:half], total[half:])
        return 0

    lax.fori_loop(0, members // block, one, 0)


def down_product(labels, rows, maps, rank):
    members, tok, share = rows.shape
    tok -= ID_ROWS
    map_rows = sum(m.shape[0] for m in maps)
    return pl.pallas_call(
        functools.partial(down_kernel, len(maps), rank),
        out_shape=[
            jax.ShapeDtypeStruct((members, tok // 2, LANES), jnp.float32),
            jax.ShapeDtypeStruct((members, tok), jnp.float32),
        ],
        in_specs=[IN_SMEM, IN_VMEM] + [IN_VMEM] * len(maps),
        out_specs=[IN_VMEM, IN_VMEM],
        scratch_shapes=[
            pltpu.VMEM((min(BLOCK, members) * tok, LANES), jnp.float32),
            pltpu.VMEM((min(BLOCK, members), tok, LANES), jnp.float32),
        ],
        compiler_params=params(8 * min(BLOCK, members) * tok * LANES),
        cost_estimate=pl.CostEstimate(
            flops=2 * map_rows * members * tok * share,
            bytes_accessed=2 * share * (map_rows + members * tok),
            transcendentals=0,
        ),
        name="down_product",
    )(labels, rows, *maps)


def copies_kernel(terms_ref, out_ref):
    own = jnp.sum(terms_ref[...], axis=0).astype(jnp.bfloat16)
    for member in range(out_ref.shape[0]):
        out_ref[member] = own


def summed_copies(terms):
    return pl.pallas_call(
        copies_kernel,
        out_shape=jax.ShapeDtypeStruct(terms.shape, jnp.bfloat16),
        in_specs=[IN_VMEM],
        out_specs=IN_VMEM,
        compiler_params=params(),
        name="summed_copies",
    )(terms)


def up_kernel(map_count, rank, offsets, labels_ref, me_ref, ids_ref, shrunk_ref, *refs):
    half, members = shrunk_ref.shape[1], len(offsets)
    maps, outs = refs[:map_count], refs[map_count : map_count + members]
    spread_ref = refs[-1]
    tok = 2 * half
    block = min(BLOCK, members)
    tiles = spread_ref.shape[1] // LANES
    lane = lax.broadcasted_iota(jnp.int32, (half, LANES), 1)
    held = jnp.concatenate([m[...] for m in maps], axis=0)
    for first in range(0, members, block):
        for n in range(block):
            member = me_ref[0] ^ offsets[first + n]
            packed = shrunk_ref[member].astype(jnp.float32)
            turned = pltpu.roll(packed, LANES // 2, 1)
            shrunk = jnp.concatenate(
                [jnp.where(lane < rank, packed, turned), jnp.where(lane < rank, turned, packed)], axis=0
            )
            ids = jnp.broadcast_to(ids_ref[pl.ds(member, 1), :], (LANES, tok)).T
            for tile in range(tiles):
                named = ids == tile_labels(labels_ref, tile, rank, (1, LANES))
                spread_ref[n * tok : (n + 1) * tok, tile * LANES : (tile + 1) * LANES] = jnp.where(
                    named, shrunk, 0.0
                ).astype(jnp.bfloat16)
        product = jnp.dot(spread_ref[...], held, preferred_element_type=jnp.float32)
        product = (adapter_scale * product).astype(jnp.bfloat16)
        for n in range(block):
            outs[first + n][...] = product[n * tok : (n + 1) * tok, :]


def up_product(labels, me, ids, shrunk, maps, rank, offsets):
    members, tok = len(offsets), ids.shape[1]
    map_rows, piece = sum(m.shape[0] for m in maps), maps[0].shape[1]
    return pl.pallas_call(
        functools.partial(up_kernel, len(maps), rank, offsets),
        out_shape=[jax.ShapeDtypeStruct((tok, piece), jnp.bfloat16)] * members,
        in_specs=[IN_SMEM, IN_SMEM, IN_VMEM, IN_VMEM] + [IN_VMEM] * len(maps),
        out_specs=[IN_VMEM] * members,
        scratch_shapes=[pltpu.VMEM((min(BLOCK, members) * tok, map_rows), jnp.bfloat16)],
        compiler_params=params(2 * min(BLOCK, members) * tok * map_rows),
        cost_estimate=pl.CostEstimate(
            flops=2 * map_rows * members * tok * piece,
            bytes_accessed=2 * piece * (map_rows + members * tok),
            transcendentals=0,
        ),
        name="up_product",
    )(labels, me, ids, shrunk, *maps)


def place_kernel(offsets, me_ref, *refs):
    blocks, out_ref, sems = refs[:-2], refs[-2], refs[-1]
    share = blocks[0].shape[1]
    copies = []
    for n, block in enumerate(blocks):
        at = pl.multiple_of((me_ref[0] ^ offsets[n]) * share, LANES)
        copies.append(pltpu.make_async_copy(block, out_ref.at[:, pl.ds(at, share)], sems.at[n]))
    for copy in copies:
        copy.start()
    for copy in copies:
        copy.wait()


def place(me, offsets, blocks):
    tok, share = blocks[0].shape
    return pl.pallas_call(
        functools.partial(place_kernel, offsets),
        out_shape=jax.ShapeDtypeStruct((tok, len(blocks) * share), jnp.bfloat16),
        in_specs=[IN_SMEM] + [ANYWHERE] * len(blocks),
        out_specs=ANYWHERE,
        scratch_shapes=[pltpu.SemaphoreType.DMA((len(blocks),))],
        compiler_params=params(),
        name="place_results",
    )(me, *blocks)


def per_device(token_adapter_index, hidden, adapter_down_maps, adapter_up_maps):
    tok, width = hidden.shape
    groups, outer, inner = (lax.axis_size(a) for a in ("groups", "outer", "inner"))
    group, level, place_in_group = (lax.axis_index(a) for a in ("groups", "outer", "inner"))
    members = groups * inner
    share = width // members
    rank = adapter_up_maps.shape[1]
    me = group * inner + place_in_group

    def slices(array):
        return [
            lax.dynamic_slice_in_dim(array, (me ^ offset) * share, share, axis=1) for offset in range(inner)
        ]

    def exchanged(blocks):
        return blocks[:1] + [to_partner(blocks[n], "inner", inner, n) for n in range(1, inner)]

    def rings(near, far, near_cost, far_cost, far_second_after=()):
        near, far = [near], [far]
        for step in range(1, outer):
            near_block, far_block = near[-1], far[-1]
            if step == 2:
                far_block = after(far_block, *far_second_after)
                if near_cost:
                    near_block = joined([near_block], near_cost)
                if far_cost:
                    far_block = joined([far_block], far_cost)
            near.append(next_on_ring(near_block, outer))
            far.append(next_on_ring(far_block, outer))
        return near, far

    steps_back = jnp.arange(outer, dtype=jnp.int32)[:, None]
    labels = ((level - steps_back + outer) % outer) * inner + (
        place_in_group ^ jnp.arange(inner, dtype=jnp.int32)[None, :]
    )
    labels = labels.reshape(-1)

    middle = inner // 2
    down = exchanged(slices(adapter_down_maps[0].T))
    down_near, down_far = rings(joined(down[:middle], AHEAD), joined(down[middle:], AHEAD), SLIGHTLY_AHEAD, SLIGHTLY_AHEAD)
    ids = token_adapter_index.reshape(1, tok)
    rows = swap(outgoing_rows(after(hidden, down_near[0]), ids, members))
    up = exchanged([after(block, down_near[1]) for block in slices(adapter_up_maps[0])])

    down_maps = [m for pair in zip(down_near, down_far) for m in pair]
    packed, id_rows = down_product(labels, rows, down_maps, rank)
    up_near, up_far = rings(
        after(jnp.concatenate(up[:middle], axis=0), down_near[-1]),
        joined([after(block, down_near[-1]) for block in up[middle:]], SLIGHTLY_AHEAD // 4),
        SLIGHTLY_AHEAD,
        0,
        far_second_after=[packed],
    )
    up_maps = [m for pair in zip(up_near, up_far) for m in pair]
    shrunk = swap(summed_copies(swap(packed)))
    offsets = sorted(range(1, members), key=lambda n: (-(n >= inner) - (n % inner >= 2), -(n >= inner), n)) + [0]
    results = []
    for some in offsets[: members // 2], offsets[members // 2 :]:
        results += up_product(labels, me.reshape(1), id_rows, shrunk, up_maps, rank, some)
    returned = [to_partner(r, PLANE, members, n) for r, n in zip(results[:-1], offsets)]
    return place(me.reshape(1), offsets, returned + results[-1:])


def solution(mesh):
    groups, wide = mesh.shape["groups"], mesh.shape["wide"]
    outer = 1 << ((wide.bit_length() - 1) // 2)
    fine = Mesh(mesh.devices.reshape(groups, outer, wide // outer), ("groups", "outer", "inner"))
    owner = ("outer", "inner")
    rows = P(("groups",) + owner, None)
    return jax.shard_map(
        per_device,
        mesh=fine,
        in_specs=(rows, rows, P(owner, None, None), P(owner, None, None)),
        out_specs=rows,
        check_vma=False,
    )
```

```python
import functools

import jax
import jax.numpy as jnp
from jax import lax
from jax.experimental import pallas as pl
from jax.experimental.pallas import tpu as pltpu
from jax.sharding import Mesh
from jax.sharding import PartitionSpec as P

adapter_scale = 2.0
PLANE = ("groups", "inner")
LANES = 128
ID_ROWS = 8
AHEAD, SLIGHTLY_AHEAD = 10**11, 6 * 10**9
BLOCK = 8
IN_VMEM = pl.BlockSpec(memory_space=pltpu.VMEM)
IN_SMEM = pl.BlockSpec(memory_space=pltpu.SMEM)
ANYWHERE = pl.BlockSpec(memory_space=pl.ANY)


def params(scratch_bytes=0):
    return pltpu.CompilerParams(vmem_limit_bytes=(12 << 20) + 2 * scratch_bytes)


def to_partner(value, axes, size, offset):
    return lax.ppermute(value, axes, [(i, i ^ offset) for i in range(size)])


def next_on_ring(block, outer):
    return lax.ppermute(block, "outer", [(i, (i + 1) % outer) for i in range(outer)])


def after(value, *earlier):
    return lax.optimization_barrier((value,) + earlier)[0]


def swap(value):
    return lax.all_to_all(value, PLANE, split_axis=0, concat_axis=0, tiled=True)


def tile_labels(labels_ref, tile, rank, shape):
    per_tile = LANES // rank
    lane = lax.broadcasted_iota(jnp.int32, shape, 1)
    label = jnp.full(shape, labels_ref[tile * per_tile], jnp.int32)
    for n in range(1, per_tile):
        label = jnp.where(lane >= n * rank, labels_ref[tile * per_tile + n], label)
    return label.astype(jnp.float32)


def join_kernel(*refs):
    blocks, out_ref = refs[:-1], refs[-1]
    rows = blocks[0].shape[0]
    for n, block in enumerate(blocks):
        out_ref[n * rows : (n + 1) * rows, :] = block[...]


def joined(blocks, cost):
    rows, share = blocks[0].shape
    return pl.pallas_call(
        join_kernel,
        out_shape=jax.ShapeDtypeStruct((len(blocks) * rows, share), jnp.bfloat16),
        in_specs=[IN_VMEM] * len(blocks),
        out_specs=IN_VMEM,
        compiler_params=params(),
        cost_estimate=pl.CostEstimate(flops=cost, bytes_accessed=10**6, transcendentals=0),
        name="join_blocks",
    )(*blocks)


def outgoing_kernel(hidden_ref, ids_ref, out_ref, sems):
    members, rows, share = out_ref.shape
    tok = rows - ID_ROWS
    copies = [
        pltpu.make_async_copy(
            hidden_ref.at[:, pl.ds(member * share, share)], out_ref.at[member, pl.ds(0, tok)], sems.at[member]
        )
        for member in range(members)
    ]
    for copy in copies:
        copy.start()
    ids = jnp.broadcast_to(ids_ref[...].astype(jnp.float32).astype(jnp.bfloat16), (ID_ROWS, tok))
    for member in range(members):
        out_ref[member, tok:, :tok] = ids
        if share > tok:
            out_ref[member, tok:, tok:] = jnp.zeros((ID_ROWS, share - tok), jnp.bfloat16)
    for copy in copies:
        copy.wait()


def outgoing_rows(hidden, ids, members):
    tok, width = hidden.shape
    share = width // members
    return pl.pallas_call(
        outgoing_kernel,
        out_shape=jax.ShapeDtypeStruct((members, tok + ID_ROWS, share), jnp.bfloat16),
        in_specs=[ANYWHERE, IN_VMEM],
        out_specs=IN_VMEM,
        scratch_shapes=[pltpu.SemaphoreType.DMA((members,))],
        compiler_params=params(),
        name="outgoing_rows",
    )(hidden, ids)


def down_kernel(map_count, rank, labels_ref, rows_ref, *refs):
    maps, (packed_ref, id_rows_ref, total_ref, ids_ref) = refs[:map_count], refs[map_count:]
    members, rows, share = rows_ref.shape
    tok = rows - ID_ROWS
    block = min(BLOCK, members)
    half = tok // 2
    lane = lax.broadcasted_iota(jnp.int32, (half, LANES), 1)

    def one(step, _):
        first = step * block
        for n in range(block):
            row = rows_ref[first + n, tok : tok + 1, :LANES].astype(jnp.float32)
            id_rows_ref[pl.ds(first + n, 1), :] = row
            ids_ref[n] = jnp.broadcast_to(row, (LANES, tok)).T
        tokens = rows_ref[pl.ds(first, block), :tok, :].reshape(block * tok, share)
        ids = ids_ref[...].reshape(block * tok, LANES)
        tile = 0
        for at in range(0, map_count, 2):
            some = jnp.concatenate([m[...] for m in maps[at : at + 2]], axis=0)
            product = lax.dot_general(
                tokens, some, (((1,), (1,)), ((), ())), preferred_element_type=jnp.float32
            )
            total = jnp.zeros((block * tok, LANES), jnp.float32) if tile == 0 else total_ref[...]
            for n in range(some.shape[0] // LANES):
                named = ids == tile_labels(labels_ref, tile, rank, (1, LANES))
                total += jnp.where(named, product[:, n * LANES : (n + 1) * LANES], 0.0)
                tile += 1
            total_ref[...] = total
        for n in range(block):
            total = total_ref[n * tok : (n + 1) * tok, :]
            total += pltpu.roll(total, LANES // 2, 1)
            packed_ref[first + n] = jnp.where(lane < rank, total[:half], total[half:])
        return 0

    lax.fori_loop(0, members // block, one, 0)


def down_product(labels, rows, maps, rank):
    members, tok, share = rows.shape
    tok -= ID_ROWS
    map_rows = sum(m.shape[0] for m in maps)
    return pl.pallas_call(
        functools.partial(down_kernel, len(maps), rank),
        out_shape=[
            jax.ShapeDtypeStruct((members, tok // 2, LANES), jnp.float32),
            jax.ShapeDtypeStruct((members, tok), jnp.float32),
        ],
        in_specs=[IN_SMEM, IN_VMEM] + [IN_VMEM] * len(maps),
        out_specs=[IN_VMEM, IN_VMEM],
        scratch_shapes=[
            pltpu.VMEM((min(BLOCK, members) * tok, LANES), jnp.float32),
            pltpu.VMEM((min(BLOCK, members), tok, LANES), jnp.float32),
        ],
        compiler_params=params(8 * min(BLOCK, members) * tok * LANES),
        cost_estimate=pl.CostEstimate(
            flops=2 * map_rows * members * tok * share,
            bytes_accessed=2 * share * (map_rows + members * tok),
            transcendentals=0,
        ),
        name="down_product",
    )(labels, rows, *maps)


def copies_kernel(terms_ref, out_ref):
    own = jnp.sum(terms_ref[...], axis=0).astype(jnp.bfloat16)
    for member in range(out_ref.shape[0]):
        out_ref[member] = own


def summed_copies(terms):
    return pl.pallas_call(
        copies_kernel,
        out_shape=jax.ShapeDtypeStruct(terms.shape, jnp.bfloat16),
        in_specs=[IN_VMEM],
        out_specs=IN_VMEM,
        compiler_params=params(),
        name="summed_copies",
    )(terms)


def up_kernel(map_count, rank, offsets, labels_ref, me_ref, ids_ref, shrunk_ref, *refs):
    half, members = shrunk_ref.shape[1], len(offsets)
    maps, outs = refs[:map_count], refs[map_count : map_count + members]
    spread_ref = refs[-1]
    tok = 2 * half
    block = min(BLOCK, members)
    tiles = spread_ref.shape[1] // LANES
    lane = lax.broadcasted_iota(jnp.int32, (half, LANES), 1)
    held = jnp.concatenate([m[...] for m in maps], axis=0)
    for first in range(0, members, block):
        for n in range(block):
            member = me_ref[0] ^ offsets[first + n]
            packed = shrunk_ref[member].astype(jnp.float32)
            turned = pltpu.roll(packed, LANES // 2, 1)
            shrunk = jnp.concatenate(
                [jnp.where(lane < rank, packed, turned), jnp.where(lane < rank, turned, packed)], axis=0
            )
            ids = jnp.broadcast_to(ids_ref[pl.ds(member, 1), :], (LANES, tok)).T
            for tile in range(tiles):
                named = ids == tile_labels(labels_ref, tile, rank, (1, LANES))
                spread_ref[n * tok : (n + 1) * tok, tile * LANES : (tile + 1) * LANES] = jnp.where(
                    named, shrunk, 0.0
                ).astype(jnp.bfloat16)
        product = jnp.dot(spread_ref[...], held, preferred_element_type=jnp.float32)
        product = (adapter_scale * product).astype(jnp.bfloat16)
        for n in range(block):
            outs[first + n][...] = product[n * tok : (n + 1) * tok, :]


def up_product(labels, me, ids, shrunk, maps, rank, offsets):
    members, tok = len(offsets), ids.shape[1]
    map_rows, piece = sum(m.shape[0] for m in maps), maps[0].shape[1]
    return pl.pallas_call(
        functools.partial(up_kernel, len(maps), rank, offsets),
        out_shape=[jax.ShapeDtypeStruct((tok, piece), jnp.bfloat16)] * members,
        in_specs=[IN_SMEM, IN_SMEM, IN_VMEM, IN_VMEM] + [IN_VMEM] * len(maps),
        out_specs=[IN_VMEM] * members,
        scratch_shapes=[pltpu.VMEM((min(BLOCK, members) * tok, map_rows), jnp.bfloat16)],
        compiler_params=params(2 * min(BLOCK, members) * tok * map_rows),
        cost_estimate=pl.CostEstimate(
            flops=2 * map_rows * members * tok * piece,
            bytes_accessed=2 * piece * (map_rows + members * tok),
            transcendentals=0,
        ),
        name="up_product",
    )(labels, me, ids, shrunk, *maps)


def place_kernel(offsets, me_ref, *refs):
    blocks, out_ref, sems = refs[:-2], refs[-2], refs[-1]
    share = blocks[0].shape[1]
    copies = []
    for n, block in enumerate(blocks):
        at = pl.multiple_of((me_ref[0] ^ offsets[n]) * share, LANES)
        copies.append(pltpu.make_async_copy(block, out_ref.at[:, pl.ds(at, share)], sems.at[n]))
    for copy in copies:
        copy.start()
    for copy in copies:
        copy.wait()


def place(me, offsets, blocks):
    tok, share = blocks[0].shape
    return pl.pallas_call(
        functools.partial(place_kernel, offsets),
        out_shape=jax.ShapeDtypeStruct((tok, len(blocks) * share), jnp.bfloat16),
        in_specs=[IN_SMEM] + [ANYWHERE] * len(blocks),
        out_specs=ANYWHERE,
        scratch_shapes=[pltpu.SemaphoreType.DMA((len(blocks),))],
        compiler_params=params(),
        name="place_results",
    )(me, *blocks)


def per_device(token_adapter_index, hidden, adapter_down_maps, adapter_up_maps):
    tok, width = hidden.shape
    groups, outer, inner = (lax.axis_size(a) for a in ("groups", "outer", "inner"))
    group, level, place_in_group = (lax.axis_index(a) for a in ("groups", "outer", "inner"))
    members = groups * inner
    share = width // members
    rank = adapter_up_maps.shape[1]
    me = group * inner + place_in_group

    def slices(array):
        return [
            lax.dynamic_slice_in_dim(array, (me ^ offset) * share, share, axis=1) for offset in range(inner)
        ]

    def exchanged(blocks):
        return blocks[:1] + [to_partner(blocks[n], "inner", inner, n) for n in range(1, inner)]

    def rings(near, far, near_cost, far_cost, far_second_after=()):
        near, far = [near], [far]
        for step in range(1, outer):
            near_block, far_block = near[-1], far[-1]
            if step == 2:
                far_block = after(far_block, *far_second_after)
                if near_cost:
                    near_block = joined([near_block], near_cost)
                if far_cost:
                    far_block = joined([far_block], far_cost)
            near.append(next_on_ring(near_block, outer))
            far.append(next_on_ring(far_block, outer))
        return near, far

    steps_back = jnp.arange(outer, dtype=jnp.int32)[:, None]
    labels = ((level - steps_back + outer) % outer) * inner + (
        place_in_group ^ jnp.arange(inner, dtype=jnp.int32)[None, :]
    )
    labels = labels.reshape(-1)

    middle = inner // 2
    down = exchanged(slices(adapter_down_maps[0].T))
    down_near, down_far = rings(joined(down[:middle], AHEAD), joined(down[middle:], AHEAD), SLIGHTLY_AHEAD, SLIGHTLY_AHEAD)
    ids = token_adapter_index.reshape(1, tok)
    rows = swap(outgoing_rows(after(hidden, down_near[0]), ids, members))
    up = exchanged([after(block, down_near[1]) for block in slices(adapter_up_maps[0])])

    down_maps = [m for pair in zip(down_near, down_far) for m in pair]
    packed, id_rows = down_product(labels, rows, down_maps, rank)
    up_near, up_far = rings(
        after(jnp.concatenate(up[:middle], axis=0), down_near[-1]),
        joined([after(block, down_far[-1]) for block in up[middle:]], SLIGHTLY_AHEAD // 4),
        SLIGHTLY_AHEAD,
        0,
        far_second_after=[packed],
    )
    up_maps = [m for pair in zip(up_near, up_far) for m in pair]
    shrunk = swap(summed_copies(swap(packed)))
    offsets = sorted(range(1, members), key=lambda n: (-(n >= inner) - (n % inner >= 2), -(n >= inner), n)) + [0]
    results = []
    quarter = members // 4
    for some in offsets[:quarter], offsets[quarter : 2 * quarter], offsets[2 * quarter :]:
        results += up_product(labels, me.reshape(1), id_rows, shrunk, up_maps, rank, some)
    returned = [to_partner(r, PLANE, members, n) for r, n in zip(results[:-1], offsets)]
    return place(me.reshape(1), offsets, returned + results[-1:])


def solution(mesh):
    groups, wide = mesh.shape["groups"], mesh.shape["wide"]
    outer = 1 << ((wide.bit_length() - 1) // 2)
    fine = Mesh(mesh.devices.reshape(groups, outer, wide // outer), ("groups", "outer", "inner"))
    owner = ("outer", "inner")
    rows = P(("groups",) + owner, None)
    return jax.shard_map(
        per_device,
        mesh=fine,
        in_specs=(rows, rows, P(owner, None, None), P(owner, None, None)),
        out_specs=rows,
        check_vma=False,
    )
```

```python
import functools

import jax
import jax.numpy as jnp
from jax import lax
from jax.experimental import pallas as pl
from jax.experimental.pallas import tpu as pltpu
from jax.sharding import Mesh
from jax.sharding import PartitionSpec as P

adapter_scale = 2.0
PLANE = ("groups", "inner")
LANES = 128
ID_ROWS = 8
AHEAD, SLIGHTLY_AHEAD = 10**11, 6 * 10**9
BLOCK = 8
IN_VMEM = pl.BlockSpec(memory_space=pltpu.VMEM)
IN_SMEM = pl.BlockSpec(memory_space=pltpu.SMEM)
ANYWHERE = pl.BlockSpec(memory_space=pl.ANY)


def params(scratch_bytes=0):
    return pltpu.CompilerParams(vmem_limit_bytes=(12 << 20) + 2 * scratch_bytes)


def to_partner(value, axes, size, offset):
    return lax.ppermute(value, axes, [(i, i ^ offset) for i in range(size)])


def next_on_ring(block, outer):
    return lax.ppermute(block, "outer", [(i, (i + 1) % outer) for i in range(outer)])


def after(value, *earlier):
    return lax.optimization_barrier((value,) + earlier)[0]


def swap(value):
    return lax.all_to_all(value, PLANE, split_axis=0, concat_axis=0, tiled=True)


def tile_labels(labels_ref, tile, rank, shape):
    per_tile = LANES // rank
    lane = lax.broadcasted_iota(jnp.int32, shape, 1)
    label = jnp.full(shape, labels_ref[tile * per_tile], jnp.int32)
    for n in range(1, per_tile):
        label = jnp.where(lane >= n * rank, labels_ref[tile * per_tile + n], label)
    return label.astype(jnp.float32)


def join_kernel(*refs):
    blocks, out_ref = refs[:-1], refs[-1]
    rows = blocks[0].shape[0]
    for n, block in enumerate(blocks):
        out_ref[n * rows : (n + 1) * rows, :] = block[...]


def joined(blocks, cost):
    rows, share = blocks[0].shape
    return pl.pallas_call(
        join_kernel,
        out_shape=jax.ShapeDtypeStruct((len(blocks) * rows, share), jnp.bfloat16),
        in_specs=[IN_VMEM] * len(blocks),
        out_specs=IN_VMEM,
        compiler_params=params(),
        cost_estimate=pl.CostEstimate(flops=cost, bytes_accessed=10**6, transcendentals=0),
        name="join_blocks",
    )(*blocks)


def outgoing_kernel(hidden_ref, ids_ref, out_ref, sems):
    members, rows, share = out_ref.shape
    tok = rows - ID_ROWS
    copies = [
        pltpu.make_async_copy(
            hidden_ref.at[:, pl.ds(member * share, share)], out_ref.at[member, pl.ds(0, tok)], sems.at[member]
        )
        for member in range(members)
    ]
    for copy in copies:
        copy.start()
    ids = jnp.broadcast_to(ids_ref[...].astype(jnp.float32).astype(jnp.bfloat16), (ID_ROWS, tok))
    for member in range(members):
        out_ref[member, tok:, :tok] = ids
        if share > tok:
            out_ref[member, tok:, tok:] = jnp.zeros((ID_ROWS, share - tok), jnp.bfloat16)
    for copy in copies:
        copy.wait()


def outgoing_rows(hidden, ids, members):
    tok, width = hidden.shape
    share = width // members
    return pl.pallas_call(
        outgoing_kernel,
        out_shape=jax.ShapeDtypeStruct((members, tok + ID_ROWS, share), jnp.bfloat16),
        in_specs=[ANYWHERE, IN_VMEM],
        out_specs=IN_VMEM,
        scratch_shapes=[pltpu.SemaphoreType.DMA((members,))],
        compiler_params=params(),
        name="outgoing_rows",
    )(hidden, ids)


def down_kernel(map_count, rank, labels_ref, rows_ref, *refs):
    maps, (packed_ref, id_rows_ref, total_ref, ids_ref) = refs[:map_count], refs[map_count:]
    members, rows, share = rows_ref.shape
    tok = rows - ID_ROWS
    block = min(BLOCK, members)
    half = tok // 2
    lane = lax.broadcasted_iota(jnp.int32, (half, LANES), 1)

    def one(step, _):
        first = step * block
        for n in range(block):
            row = rows_ref[first + n, tok : tok + 1, :LANES].astype(jnp.float32)
            id_rows_ref[pl.ds(first + n, 1), :] = row
            ids_ref[n] = jnp.broadcast_to(row, (LANES, tok)).T
        tokens = rows_ref[pl.ds(first, block), :tok, :].reshape(block * tok, share)
        ids = ids_ref[...].reshape(block * tok, LANES)
        tile = 0
        for at in range(0, map_count, 2):
            some = jnp.concatenate([m[...] for m in maps[at : at + 2]], axis=0)
            product = lax.dot_general(
                tokens, some, (((1,), (1,)), ((), ())), preferred_element_type=jnp.float32
            )
            total = jnp.zeros((block * tok, LANES), jnp.float32) if tile == 0 else total_ref[...]
            for n in range(some.shape[0] // LANES):
                named = ids == tile_labels(labels_ref, tile, rank, (1, LANES))
                total += jnp.where(named, product[:, n * LANES : (n + 1) * LANES], 0.0)
                tile += 1
            total_ref[...] = total
        for n in range(block):
            total = total_ref[n * tok : (n + 1) * tok, :]
            total += pltpu.roll(total, LANES // 2, 1)
            packed_ref[first + n] = jnp.where(lane < rank, total[:half], total[half:])
        return 0

    lax.fori_loop(0, members // block, one, 0)


def down_product(labels, rows, maps, rank):
    members, tok, share = rows.shape
    tok -= ID_ROWS
    map_rows = sum(m.shape[0] for m in maps)
    return pl.pallas_call(
        functools.partial(down_kernel, len(maps), rank),
        out_shape=[
            jax.ShapeDtypeStruct((members, tok // 2, LANES), jnp.float32),
            jax.ShapeDtypeStruct((members, tok), jnp.float32),
        ],
        in_specs=[IN_SMEM, IN_VMEM] + [IN_VMEM] * len(maps),
        out_specs=[IN_VMEM, IN_VMEM],
        scratch_shapes=[
            pltpu.VMEM((min(BLOCK, members) * tok, LANES), jnp.float32),
            pltpu.VMEM((min(BLOCK, members), tok, LANES), jnp.float32),
        ],
        compiler_params=params(8 * min(BLOCK, members) * tok * LANES),
        cost_estimate=pl.CostEstimate(
            flops=2 * map_rows * members * tok * share,
            bytes_accessed=2 * share * (map_rows + members * tok),
            transcendentals=0,
        ),
        name="down_product",
    )(labels, rows, *maps)


def copies_kernel(terms_ref, out_ref):
    own = jnp.sum(terms_ref[...], axis=0).astype(jnp.bfloat16)
    for member in range(out_ref.shape[0]):
        out_ref[member] = own


def summed_copies(terms):
    return pl.pallas_call(
        copies_kernel,
        out_shape=jax.ShapeDtypeStruct(terms.shape, jnp.bfloat16),
        in_specs=[IN_VMEM],
        out_specs=IN_VMEM,
        compiler_params=params(),
        name="summed_copies",
    )(terms)


def up_kernel(map_count, rank, offsets, labels_ref, me_ref, ids_ref, shrunk_ref, *refs):
    half, members = shrunk_ref.shape[1], len(offsets)
    maps, outs = refs[:map_count], refs[map_count : map_count + members]
    spread_ref = refs[-1]
    tok = 2 * half
    block = min(BLOCK, members)
    tiles = spread_ref.shape[1] // LANES
    lane = lax.broadcasted_iota(jnp.int32, (half, LANES), 1)
    held = jnp.concatenate([m[...] for m in maps], axis=0)
    for first in range(0, members, block):
        for n in range(block):
            member = me_ref[0] ^ offsets[first + n]
            packed = shrunk_ref[member].astype(jnp.float32)
            turned = pltpu.roll(packed, LANES // 2, 1)
            shrunk = jnp.concatenate(
                [jnp.where(lane < rank, packed, turned), jnp.where(lane < rank, turned, packed)], axis=0
            )
            ids = jnp.broadcast_to(ids_ref[pl.ds(member, 1), :], (LANES, tok)).T
            for tile in range(tiles):
                named = ids == tile_labels(labels_ref, tile, rank, (1, LANES))
                spread_ref[n * tok : (n + 1) * tok, tile * LANES : (tile + 1) * LANES] = jnp.where(
                    named, shrunk, 0.0
                ).astype(jnp.bfloat16)
        product = jnp.dot(spread_ref[...], held, preferred_element_type=jnp.float32)
        product = (adapter_scale * product).astype(jnp.bfloat16)
        for n in range(block):
            outs[first + n][...] = product[n * tok : (n + 1) * tok, :]


def up_product(labels, me, ids, shrunk, maps, rank, offsets):
    members, tok = len(offsets), ids.shape[1]
    map_rows, piece = sum(m.shape[0] for m in maps), maps[0].shape[1]
    return pl.pallas_call(
        functools.partial(up_kernel, len(maps), rank, offsets),
        out_shape=[jax.ShapeDtypeStruct((tok, piece), jnp.bfloat16)] * members,
        in_specs=[IN_SMEM, IN_SMEM, IN_VMEM, IN_VMEM] + [IN_VMEM] * len(maps),
        out_specs=[IN_VMEM] * members,
        scratch_shapes=[pltpu.VMEM((min(BLOCK, members) * tok, map_rows), jnp.bfloat16)],
        compiler_params=params(2 * min(BLOCK, members) * tok * map_rows),
        cost_estimate=pl.CostEstimate(
            flops=2 * map_rows * members * tok * piece,
            bytes_accessed=2 * piece * (map_rows + members * tok),
            transcendentals=0,
        ),
        name="up_product",
    )(labels, me, ids, shrunk, *maps)


def place_kernel(offsets, me_ref, *refs):
    blocks, out_ref, sems = refs[: len(offsets)], refs[-2], refs[-1]
    share = blocks[0].shape[1]
    copies = []
    for n, block in enumerate(blocks):
        at = pl.multiple_of((me_ref[0] ^ offsets[n]) * share, LANES)
        copies.append(pltpu.make_async_copy(block, out_ref.at[:, pl.ds(at, share)], sems.at[n]))
    for copy in copies:
        copy.start()
    for copy in copies:
        copy.wait()


def place(me, offsets, blocks, width, placed=()):
    tok = blocks[0].shape[0]
    count = len(blocks)
    return pl.pallas_call(
        functools.partial(place_kernel, offsets),
        out_shape=jax.ShapeDtypeStruct((tok, width), jnp.bfloat16),
        in_specs=[IN_SMEM] + [ANYWHERE] * (count + len(placed)),
        out_specs=ANYWHERE,
        scratch_shapes=[pltpu.SemaphoreType.DMA((count,))],
        input_output_aliases={1 + count: 0} if placed else {},
        compiler_params=params(),
        name="place_results",
    )(me, *blocks, *placed)


def per_device(token_adapter_index, hidden, adapter_down_maps, adapter_up_maps):
    tok, width = hidden.shape
    groups, outer, inner = (lax.axis_size(a) for a in ("groups", "outer", "inner"))
    group, level, place_in_group = (lax.axis_index(a) for a in ("groups", "outer", "inner"))
    members = groups * inner
    share = width // members
    rank = adapter_up_maps.shape[1]
    me = group * inner + place_in_group

    def slices(array):
        return [
            lax.dynamic_slice_in_dim(array, (me ^ offset) * share, share, axis=1) for offset in range(inner)
        ]

    def exchanged(blocks):
        return blocks[:1] + [to_partner(blocks[n], "inner", inner, n) for n in range(1, inner)]

    def rings(near, far, near_cost, far_cost, far_second_after=()):
        near, far = [near], [far]
        for step in range(1, outer):
            near_block, far_block = near[-1], far[-1]
            if step == 2:
                far_block = after(far_block, *far_second_after)
                if near_cost:
                    near_block = joined([near_block], near_cost)
                if far_cost:
                    far_block = joined([far_block], far_cost)
            near.append(next_on_ring(near_block, outer))
            far.append(next_on_ring(far_block, outer))
        return near, far

    steps_back = jnp.arange(outer, dtype=jnp.int32)[:, None]
    labels = ((level - steps_back + outer) % outer) * inner + (
        place_in_group ^ jnp.arange(inner, dtype=jnp.int32)[None, :]
    )
    labels = labels.reshape(-1)

    middle = inner // 2
    down = exchanged(slices(adapter_down_maps[0].T))
    down_near, down_far = rings(joined(down[:middle], AHEAD), joined(down[middle:], AHEAD), SLIGHTLY_AHEAD, SLIGHTLY_AHEAD)
    ids = token_adapter_index.reshape(1, tok)
    rows = swap(outgoing_rows(after(hidden, down_near[0]), ids, members))
    up = exchanged([after(block, down_near[1]) for block in slices(adapter_up_maps[0])])

    down_maps = [m for pair in zip(down_near, down_far) for m in pair]
    packed, id_rows = down_product(labels, rows, down_maps, rank)
    up_near, up_far = rings(
        after(jnp.concatenate(up[:middle], axis=0), down_near[-1]),
        joined([after(block, down_far[-1]) for block in up[middle:]], SLIGHTLY_AHEAD // 4),
        SLIGHTLY_AHEAD,
        0,
        far_second_after=[packed],
    )
    up_maps = [m for pair in zip(up_near, up_far) for m in pair]
    shrunk = swap(summed_copies(swap(packed)))
    offsets = sorted(range(1, members), key=lambda n: (-(n >= inner) - (n % inner >= 2), -(n >= inner), n)) + [0]
    results = []
    for some in offsets[: members // 2], offsets[members // 2 :]:
        results += up_product(labels, me.reshape(1), id_rows, shrunk, up_maps, rank, some)
    returned = [to_partner(r, PLANE, members, n) for r, n in zip(results[:-1], offsets)]
    early = (members - 1) // 2
    placed = place(me.reshape(1), offsets[:early] + [0], returned[:early] + results[-1:], width)
    return place(me.reshape(1), offsets[early:-1], returned[early:], width, [placed])


def solution(mesh):
    groups, wide = mesh.shape["groups"], mesh.shape["wide"]
    outer = 1 << ((wide.bit_length() - 1) // 2)
    fine = Mesh(mesh.devices.reshape(groups, outer, wide // outer), ("groups", "outer", "inner"))
    owner = ("outer", "inner")
    rows = P(("groups",) + owner, None)
    return jax.shard_map(
        per_device,
        mesh=fine,
        in_specs=(rows, rows, P(owner, None, None), P(owner, None, None)),
        out_specs=rows,
        check_vma=False,
    )
```

```python
import functools

import jax
import jax.numpy as jnp
from jax import lax
from jax.experimental import pallas as pl
from jax.experimental.pallas import tpu as pltpu
from jax.sharding import Mesh
from jax.sharding import PartitionSpec as P

adapter_scale = 2.0
PLANE = ("groups", "inner")
LANES = 128
ID_ROWS = 8
AHEAD, SLIGHTLY_AHEAD = 10**11, 6 * 10**9
BLOCK = 8
IN_VMEM = pl.BlockSpec(memory_space=pltpu.VMEM)
IN_SMEM = pl.BlockSpec(memory_space=pltpu.SMEM)
ANYWHERE = pl.BlockSpec(memory_space=pl.ANY)


def params(scratch_bytes=0):
    return pltpu.CompilerParams(vmem_limit_bytes=(12 << 20) + 2 * scratch_bytes)


def to_partner(value, axes, size, offset):
    return lax.ppermute(value, axes, [(i, i ^ offset) for i in range(size)])


def next_on_ring(block, outer):
    return lax.ppermute(block, "outer", [(i, (i + 1) % outer) for i in range(outer)])


def after(value, *earlier):
    return lax.optimization_barrier((value,) + earlier)[0]


def swap(value):
    return lax.all_to_all(value, PLANE, split_axis=0, concat_axis=0, tiled=True)


def tile_labels(labels_ref, tile, rank, shape):
    per_tile = LANES // rank
    lane = lax.broadcasted_iota(jnp.int32, shape, 1)
    label = jnp.full(shape, labels_ref[tile * per_tile], jnp.int32)
    for n in range(1, per_tile):
        label = jnp.where(lane >= n * rank, labels_ref[tile * per_tile + n], label)
    return label.astype(jnp.float32)


def join_kernel(*refs):
    blocks, out_ref = refs[:-1], refs[-1]
    rows = blocks[0].shape[0]
    for n, block in enumerate(blocks):
        out_ref[n * rows : (n + 1) * rows, :] = block[...]


def joined(blocks, cost):
    rows, share = blocks[0].shape
    return pl.pallas_call(
        join_kernel,
        out_shape=jax.ShapeDtypeStruct((len(blocks) * rows, share), jnp.bfloat16),
        in_specs=[IN_VMEM] * len(blocks),
        out_specs=IN_VMEM,
        compiler_params=params(),
        cost_estimate=pl.CostEstimate(flops=cost, bytes_accessed=10**6, transcendentals=0),
        name="join_blocks",
    )(*blocks)


def outgoing_kernel(hidden_ref, ids_ref, out_ref, sems):
    members, rows, share = out_ref.shape
    tok = rows - ID_ROWS
    copies = [
        pltpu.make_async_copy(
            hidden_ref.at[:, pl.ds(member * share, share)], out_ref.at[member, pl.ds(0, tok)], sems.at[member]
        )
        for member in range(members)
    ]
    for copy in copies:
        copy.start()
    ids = jnp.broadcast_to(ids_ref[...].astype(jnp.float32).astype(jnp.bfloat16), (ID_ROWS, tok))
    for member in range(members):
        out_ref[member, tok:, :tok] = ids
        if share > tok:
            out_ref[member, tok:, tok:] = jnp.zeros((ID_ROWS, share - tok), jnp.bfloat16)
    for copy in copies:
        copy.wait()


def outgoing_rows(hidden, ids, members):
    tok, width = hidden.shape
    share = width // members
    return pl.pallas_call(
        outgoing_kernel,
        out_shape=jax.ShapeDtypeStruct((members, tok + ID_ROWS, share), jnp.bfloat16),
        in_specs=[ANYWHERE, IN_VMEM],
        out_specs=IN_VMEM,
        scratch_shapes=[pltpu.SemaphoreType.DMA((members,))],
        compiler_params=params(),
        name="outgoing_rows",
    )(hidden, ids)


def down_kernel(map_count, rank, labels_ref, rows_ref, *refs):
    maps, (packed_ref, id_rows_ref, total_ref, ids_ref) = refs[:map_count], refs[map_count:]
    members, rows, share = rows_ref.shape
    tok = rows - ID_ROWS
    block = min(BLOCK, members)
    half = tok // 2
    lane = lax.broadcasted_iota(jnp.int32, (half, LANES), 1)

    def one(step, _):
        first = step * block
        for n in range(block):
            row = rows_ref[first + n, tok : tok + 1, :LANES].astype(jnp.float32)
            id_rows_ref[pl.ds(first + n, 1), :] = row
            ids_ref[n] = jnp.broadcast_to(row, (LANES, tok)).T
        tokens = rows_ref[pl.ds(first, block), :tok, :].reshape(block * tok, share)
        ids = ids_ref[...].reshape(block * tok, LANES)
        tile = 0
        for at in range(0, map_count, 2):
            some = jnp.concatenate([m[...] for m in maps[at : at + 2]], axis=0)
            product = lax.dot_general(
                tokens, some, (((1,), (1,)), ((), ())), preferred_element_type=jnp.float32
            )
            total = jnp.zeros((block * tok, LANES), jnp.float32) if tile == 0 else total_ref[...]
            for n in range(some.shape[0] // LANES):
                named = ids == tile_labels(labels_ref, tile, rank, (1, LANES))
                total += jnp.where(named, product[:, n * LANES : (n + 1) * LANES], 0.0)
                tile += 1
            total_ref[...] = total
        for n in range(block):
            total = total_ref[n * tok : (n + 1) * tok, :]
            total += pltpu.roll(total, LANES // 2, 1)
            packed_ref[first + n] = jnp.where(lane < rank, total[:half], total[half:])
        return 0

    lax.fori_loop(0, members // block, one, 0)


def down_product(labels, rows, maps, rank):
    members, tok, share = rows.shape
    tok -= ID_ROWS
    map_rows = sum(m.shape[0] for m in maps)
    return pl.pallas_call(
        functools.partial(down_kernel, len(maps), rank),
        out_shape=[
            jax.ShapeDtypeStruct((members, tok // 2, LANES), jnp.float32),
            jax.ShapeDtypeStruct((members, tok), jnp.float32),
        ],
        in_specs=[IN_SMEM, IN_VMEM] + [IN_VMEM] * len(maps),
        out_specs=[IN_VMEM, IN_VMEM],
        scratch_shapes=[
            pltpu.VMEM((min(BLOCK, members) * tok, LANES), jnp.float32),
            pltpu.VMEM((min(BLOCK, members), tok, LANES), jnp.float32),
        ],
        compiler_params=params(8 * min(BLOCK, members) * tok * LANES),
        cost_estimate=pl.CostEstimate(
            flops=2 * map_rows * members * tok * share,
            bytes_accessed=2 * share * (map_rows + members * tok),
            transcendentals=0,
        ),
        name="down_product",
    )(labels, rows, *maps)


def copies_kernel(terms_ref, out_ref):
    own = jnp.sum(terms_ref[...], axis=0).astype(jnp.bfloat16)
    for member in range(out_ref.shape[0]):
        out_ref[member] = own


def summed_copies(terms):
    return pl.pallas_call(
        copies_kernel,
        out_shape=jax.ShapeDtypeStruct(terms.shape, jnp.bfloat16),
        in_specs=[IN_VMEM],
        out_specs=IN_VMEM,
        compiler_params=params(),
        name="summed_copies",
    )(terms)


def up_kernel(map_count, rank, offsets, labels_ref, me_ref, ids_ref, shrunk_ref, *refs):
    half, members = shrunk_ref.shape[1], len(offsets)
    maps, outs = refs[:map_count], refs[map_count : map_count + members]
    spread_ref = refs[-1]
    tok = 2 * half
    block = min(BLOCK, members)
    tiles = spread_ref.shape[1] // LANES
    lane = lax.broadcasted_iota(jnp.int32, (half, LANES), 1)
    held = jnp.concatenate([m[...] for m in maps], axis=0)
    for first in range(0, members, block):
        for n in range(block):
            member = me_ref[0] ^ offsets[first + n]
            packed = shrunk_ref[member].astype(jnp.float32)
            turned = pltpu.roll(packed, LANES // 2, 1)
            shrunk = jnp.concatenate(
                [jnp.where(lane < rank, packed, turned), jnp.where(lane < rank, turned, packed)], axis=0
            )
            ids = jnp.broadcast_to(ids_ref[pl.ds(member, 1), :], (LANES, tok)).T
            for tile in range(tiles):
                named = ids == tile_labels(labels_ref, tile, rank, (1, LANES))
                spread_ref[n * tok : (n + 1) * tok, tile * LANES : (tile + 1) * LANES] = jnp.where(
                    named, shrunk, 0.0
                ).astype(jnp.bfloat16)
        product = jnp.dot(spread_ref[...], held, preferred_element_type=jnp.float32)
        product = (adapter_scale * product).astype(jnp.bfloat16)
        for n in range(block):
            outs[first + n][...] = product[n * tok : (n + 1) * tok, :]


def up_product(labels, me, ids, shrunk, maps, rank, offsets):
    members, tok = len(offsets), ids.shape[1]
    map_rows, piece = sum(m.shape[0] for m in maps), maps[0].shape[1]
    return pl.pallas_call(
        functools.partial(up_kernel, len(maps), rank, offsets),
        out_shape=[jax.ShapeDtypeStruct((tok, piece), jnp.bfloat16)] * members,
        in_specs=[IN_SMEM, IN_SMEM, IN_VMEM, IN_VMEM] + [IN_VMEM] * len(maps),
        out_specs=[IN_VMEM] * members,
        scratch_shapes=[pltpu.VMEM((min(BLOCK, members) * tok, map_rows), jnp.bfloat16)],
        compiler_params=params(2 * min(BLOCK, members) * tok * map_rows),
        cost_estimate=pl.CostEstimate(
            flops=2 * map_rows * members * tok * piece,
            bytes_accessed=2 * piece * (map_rows + members * tok),
            transcendentals=0,
        ),
        name="up_product",
    )(labels, me, ids, shrunk, *maps)


def place_kernel(offsets, me_ref, *refs):
    blocks, out_ref, sems = refs[: len(offsets)], refs[-2], refs[-1]
    share = blocks[0].shape[1]
    copies = []
    for n, block in enumerate(blocks):
        at = pl.multiple_of((me_ref[0] ^ offsets[n]) * share, LANES)
        copies.append(pltpu.make_async_copy(block, out_ref.at[:, pl.ds(at, share)], sems.at[n]))
    for copy in copies:
        copy.start()
    for copy in copies:
        copy.wait()


def place(me, offsets, blocks, width, placed=()):
    tok = blocks[0].shape[0]
    count = len(blocks)
    return pl.pallas_call(
        functools.partial(place_kernel, offsets),
        out_shape=jax.ShapeDtypeStruct((tok, width), jnp.bfloat16),
        in_specs=[IN_SMEM] + [ANYWHERE] * (count + len(placed)),
        out_specs=ANYWHERE,
        scratch_shapes=[pltpu.SemaphoreType.DMA((count,))],
        input_output_aliases={1 + count: 0} if placed else {},
        compiler_params=params(),
        name="place_results",
    )(me, *blocks, *placed)


def per_device(token_adapter_index, hidden, adapter_down_maps, adapter_up_maps):
    tok, width = hidden.shape
    groups, outer, inner = (lax.axis_size(a) for a in ("groups", "outer", "inner"))
    group, level, place_in_group = (lax.axis_index(a) for a in ("groups", "outer", "inner"))
    members = groups * inner
    share = width // members
    rank = adapter_up_maps.shape[1]
    me = group * inner + place_in_group

    def slices(array):
        return [
            lax.dynamic_slice_in_dim(array, (me ^ offset) * share, share, axis=1) for offset in range(inner)
        ]

    def exchanged(blocks):
        return blocks[:1] + [to_partner(blocks[n], "inner", inner, n) for n in range(1, inner)]

    def rings(near, far, near_cost, far_cost, far_second_after=()):
        near, far = [near], [far]
        for step in range(1, outer):
            near_block, far_block = near[-1], far[-1]
            if step == 2:
                far_block = after(far_block, *far_second_after)
                if near_cost:
                    near_block = joined([near_block], near_cost)
                if far_cost:
                    far_block = joined([far_block], far_cost)
            near.append(next_on_ring(near_block, outer))
            far.append(next_on_ring(far_block, outer))
        return near, far

    steps_back = jnp.arange(outer, dtype=jnp.int32)[:, None]
    labels = ((level - steps_back + outer) % outer) * inner + (
        place_in_group ^ jnp.arange(inner, dtype=jnp.int32)[None, :]
    )
    labels = labels.reshape(-1)

    middle = inner // 2
    down = exchanged(slices(adapter_down_maps[0].T))
    down_near, down_far = rings(joined(down[:middle], AHEAD), joined(down[middle:], AHEAD), SLIGHTLY_AHEAD, SLIGHTLY_AHEAD)
    ids = token_adapter_index.reshape(1, tok)
    rows = swap(outgoing_rows(after(hidden, down_near[0]), ids, members))
    up = exchanged([after(block, down_near[1]) for block in slices(adapter_up_maps[0])])

    down_maps = [m for pair in zip(down_near, down_far) for m in pair]
    packed, id_rows = down_product(labels, rows, down_maps, rank)
    up_near, up_far = rings(
        after(jnp.concatenate(up[:middle], axis=0), down_near[-1]),
        joined([after(block, down_far[-1]) for block in up[middle:]], SLIGHTLY_AHEAD // 4),
        SLIGHTLY_AHEAD,
        0,
        far_second_after=[packed],
    )
    up_maps = [m for pair in zip(up_near, up_far) for m in pair]
    shrunk = swap(summed_copies(swap(packed)))
    offsets = sorted(range(1, members), key=lambda n: (-(n >= inner) - (n % inner >= 2), -(n >= inner), n)) + [0]
    results = []
    for some in offsets[: members // 2], offsets[members // 2 :]:
        results += up_product(labels, me.reshape(1), id_rows, shrunk, up_maps, rank, some)
    returned = [to_partner(r, PLANE, members, n) for r, n in zip(results[:-1], offsets)]
    early = (members - 1) // 3
    placed = place(me.reshape(1), offsets[:early] + [0], returned[:early] + results[-1:], width)
    return place(me.reshape(1), offsets[early:-1], returned[early:], width, [placed])


def solution(mesh):
    groups, wide = mesh.shape["groups"], mesh.shape["wide"]
    outer = 1 << ((wide.bit_length() - 1) // 2)
    fine = Mesh(mesh.devices.reshape(groups, outer, wide // outer), ("groups", "outer", "inner"))
    owner = ("outer", "inner")
    rows = P(("groups",) + owner, None)
    return jax.shard_map(
        per_device,
        mesh=fine,
        in_specs=(rows, rows, P(owner, None, None), P(owner, None, None)),
        out_specs=rows,
        check_vma=False,
    )
```
